32 devices in a mesh: fsdp: 8 (over z, y), seq: 4 (over x, core).
Axes of the slice: x: 2, y: 2, z: 4, core: 2. Of those that a mesh axis runs over, the one named last changes fastest.
Arguments:
- inputs: bfloat16 [3, 8, 1024, 768], P(None, 'fsdp', 'seq'), may hold values from -6 to 6
- segments: int32 [3, 8, 1024], P(None, 'fsdp'), may hold values from 0 to 5, never falling along the last dimension, each value on 1 to 512 neighbouring positions
- cotangent: bfloat16 [3, 8, 1024, 768], P(None, 'fsdp', 'seq'), may hold values from -6 to 6
- w_qkv: bfloat16 [768, 2304], P('fsdp'), may hold values from -0.21875 to 0.21875
- w_out: bfloat16 [768, 768], P('fsdp'), may hold values from -1.75 to 1.75
- w_up: bfloat16 [768, 3072], P('fsdp'), may hold values from -0.21875 to 0.21875
- w_down: bfloat16 [3072, 768], P('fsdp'), may hold values from -0.15625 to 0.15625
- vectors: bfloat16 [768, 8], P('fsdp'), may hold values from -1 to 1.5
- bias_up: bfloat16 [3072], P('fsdp'), may hold values from -1.5 to 1.5
Outputs:
- result: bfloat16 [3, 8, 1024, 768], P(None, 'fsdp', 'seq')
- grad_input: float32 [3, 8, 1024, 768], P(None, 'fsdp', 'seq')
- grad_qkv: float32 [768, 2304], P('fsdp')
- grad_outproj: float32 [768, 768], P('fsdp')
- grad_up: float32 [768, 3072], P('fsdp')
- grad_down: float32 [3072, 768], P('fsdp')
- grad_vectors: float32 [768, 8], P('fsdp')
- grad_bias_up: float32 [3072], P('fsdp')
The draws below stay inside these ranges and needn't reach their ends.
Inputs may be any that keep to these rules, and one draw needn't show every extreme that they name: `segments`: along each sequence the segment numbers never fall; every one of the 6 numbers holds 1 to 512 tokens of a sequence, and the longest holds exactly 512.
All inputs are finite; a program needn't handle non-finite values.
Results may differ from the reference program's by a relative error of at most 0.014.
Values may be sent and summed in bfloat16 or wider, within the bound.
No kernel may reach another device: no remote copies, remote signals or barrier semaphores. Data moves between devices by JAX's collectives and lax.ppermute only.
A program may use at most 320 MiB of HBM per device.

```python
import math
import jax
import jax.numpy as jnp
import numpy as np
from jax import lax

D = 768
FF = 3072
HEADS = 12
HEAD_DIM = 64
LEN = 1024
MICRO = 3
SEGS = 6
ROWS = 8


def draw_vectors(key, part):
    base = jnp.clip(jax.random.normal(key, (D, 8), jnp.float32), -3.0, 3.0)
    columns = jnp.arange(8)
    gain_column = (columns == 0) | (columns == 5)
    values = jnp.where(gain_column[None, :], 1.0 + 0.15 * base, 0.3 * base)
    return values.astype(jnp.bfloat16)


def with_spikes(entries, stream_key, source, target, shards_of, factor):
    def block_of(axis_at):
        return (jnp.arange(entries.shape[axis_at]) // (entries.shape[axis_at] // shards_of)).reshape((-1,) + (1,) * (entries.ndim - 1 - axis_at))

    near = jax.random.permutation(stream_key, shards_of)[block_of(target)]
    other_side = (block_of(target) + shards_of // 2) % shards_of
    return jnp.where((block_of(source) == near) | (block_of(source) == other_side), factor * entries, entries)


def shard_levels(key, dims, pieces, least, top_value):
    def one(position, parts):
        steps = jax.random.uniform(jax.random.fold_in(jax.random.fold_in(key, 6), position), (parts,), jnp.float32, least / len(pieces), top_value / len(pieces))
        return jnp.repeat(jnp.exp(steps), dims[position] // parts).reshape((-1,) + (1,) * (len(dims) - position - 1))

    factor_of = one(*pieces[0])
    for cut in pieces[1:]:
        factor_of = factor_of * one(*cut)
    return factor_of


def length_profile(amount, total, bound, lean):
    portions = [(1 << 20) // math.isqrt(standing ** lean) + 1 for standing in range(2, amount + 1)]
    spare, holding = total - bound - (amount - 1), [1] * (amount - 1)
    while spare > 0:
        free = [i for i in range(amount - 1) if holding[i] < bound]
        pool, budget = sum([portions[i] for i in free]), spare
        for i in free:
            more = min(bound - holding[i], max(1, budget * portions[i] // pool), spare)
            holding[i] = holding[i] + more
            spare = spare - more
    return np.array([bound] + holding)


def uneven(rng, count, total, reach, skew):
    if count == 2:
        one = jax.random.randint(rng, (), max(1, total - reach), min(reach, total - 1) + 1)
        return jnp.stack([one, total - one])
    lengths = jnp.asarray(length_profile(count, total, reach, skew), jnp.int32)
    pairs = (count - 1) // 2
    source_of, taker = lengths[1:1 + 2 * pairs:2], lengths[2:2 + 2 * pairs:2]
    slack = jnp.minimum(source_of - 1, reach - taker)
    shifted = jax.random.randint(jax.random.fold_in(rng, 1), (pairs,), 0, 1 << 20) % (slack + 1)
    lengths = lengths.at[1:1 + 2 * pairs:2].set(source_of - shifted).at[2:2 + 2 * pairs:2].set(taker + shifted)
    return lengths[jax.random.permutation(jax.random.fold_in(rng, 2), count)]


def scatter_about(rng, dims, scale, limit, split=(), kind=jnp.bfloat16):
    factor_of = shard_levels(rng, dims, split, -0.22, 0.18) if split else 1.0
    drawn = jax.random.normal(rng, dims, jnp.float32) * scale * factor_of
    return jnp.minimum(jnp.maximum(drawn, -limit), limit).astype(kind)


def heavy_noise(rng, dims, scale, reach, cuts, heavy, kind=jnp.bfloat16):
    array = scale * jax.random.normal(rng, dims, jnp.float32)
    if cuts:
        array = array * shard_levels(rng, dims, cuts, -0.22, 0.18)
    return jnp.clip(with_spikes(array, jax.random.fold_in(rng, 3), *heavy), -reach, reach).astype(kind)


def setup_inputs(seed: int = 0) -> dict:
    keys = jax.random.split(jax.random.key(seed), 10)
    inputs = scatter_about(keys[0], (MICRO, ROWS, LEN, D), 1.0, 6.0, ((1, 8), (2, 4)))
    segments = jax.vmap(lambda own: jnp.searchsorted(jnp.cumsum(uneven(own, SEGS, LEN, LEN // 2, 2)), jnp.arange(LEN), side="right"))(jax.random.split(keys[1], MICRO * ROWS)).reshape((MICRO, ROWS, LEN)).astype(jnp.int32)
    cotangent = heavy_noise(keys[2], (MICRO, ROWS, LEN, D), 1.0, 6.0, ((1, 8), (2, 4)), (1, 3, 8, 2.0))
    w_qkv = scatter_about(keys[3], (D, 3 * D), D ** -0.5, 0.21875, ((0, 8),))
    w_out = scatter_about(keys[4], (D, D), (D // 64) ** -0.5, 1.75, ((0, 8),))
    w_up = scatter_about(keys[5], (D, FF), D ** -0.5, 0.21875, ((0, 8),))
    w_down = scatter_about(keys[6], (FF, D), (FF // 2) ** -0.5, 0.15625, ((0, 8),))
    vectors = draw_vectors(jax.random.fold_in(keys[9], 71), 0)
    bias_up = scatter_about(keys[8], (FF,), 0.3, 1.5, ((0, 8),))
    return dict(inputs=inputs, segments=segments, cotangent=cotangent, w_qkv=w_qkv, w_out=w_out, w_up=w_up, w_down=w_down, vectors=vectors, bias_up=bias_up)


@jax.custom_vjp
def low(v):
    return lax.optimization_barrier(v.astype(jnp.bfloat16)).astype(jnp.float32)

@jax.custom_vjp
def low_back(v):
    return v

def low_keep(v):
    return (low(v), None)

def low_pass(kept, grad):
    return (grad,)

def back_keep(v):
    return (v, None)

def back_low(kept, grad):
    return (low(grad),)
low.defvjp(low_keep, low_pass)
low_back.defvjp(back_keep, back_low)
epsilon = 1e-05
masked_value = -1e+30

def matmul_high(left, right):
    return jnp.dot(left, right, precision=lax.Precision.HIGHEST, preferred_element_type=left.dtype)

def layer_norm(values, gain, shift):
    average = lax.optimization_barrier(jnp.mean(values, axis=-1, keepdims=True))
    centred = values - average
    spread = lax.optimization_barrier(jnp.mean(centred * centred, axis=-1, keepdims=True))
    return centred * lax.rsqrt(spread + epsilon) * gain + shift

def to_heads(tensor, groups):
    return tensor.reshape(groups, LEN, HEADS, HEAD_DIM).transpose(0, 2, 1, 3)

def block_forward(inputs, segment_ids, w_qkv, w_out, w_up, w_down, vectors, bias_up):
    groups = inputs.shape[0]
    width = D
    flat_in = inputs.reshape(groups * LEN, width)
    normed_a = low(layer_norm(flat_in, vectors[:, 0], vectors[:, 1]))
    project = matmul_high(normed_a, w_qkv)
    queries = low(low_back((project[:, :width] + vectors[:, 2]) * 0.125))
    keys_part = low(low_back(project[:, width:2 * width]))
    values_part = low(low_back(project[:, 2 * width:] + vectors[:, 3]))
    queries = to_heads(queries, groups)
    keys_part = to_heads(keys_part, groups)
    values_part = to_heads(values_part, groups)
    scores = low_back(jnp.einsum('bhqe,bhke->bhqk', queries, keys_part, precision=lax.Precision.HIGHEST))
    inside = segment_ids[:, None, :, None] == segment_ids[:, None, None, :]
    filler = jnp.full_like(scores, masked_value)
    masked = jnp.where(inside, scores, filler)
    row_max = lax.optimization_barrier(jnp.max(masked, axis=-1, keepdims=True))
    raised = jnp.where(inside, jnp.exp(masked - row_max), jnp.zeros_like(scores))
    probability = low(raised / lax.optimization_barrier(jnp.sum(raised, axis=-1, keepdims=True)))
    context = jnp.einsum('bhqk,bhke->bhqe', probability, values_part, precision=lax.Precision.HIGHEST)
    context = low(low_back(context.transpose(0, 2, 1, 3).reshape(groups * LEN, width)))
    attended = low_back(matmul_high(context, w_out) + vectors[:, 4])
    middle = flat_in + attended
    normed_b = low(layer_norm(middle, vectors[:, 5], vectors[:, 6]))
    hidden = low_back(matmul_high(normed_b, w_up) + bias_up)
    active = low(jax.nn.gelu(hidden, approximate=True))
    branch = low_back(matmul_high(active, w_down) + vectors[:, 7])
    return (middle + branch).reshape(groups, LEN, width)

def reference(inputs, segments, cotangent, w_qkv, w_out, w_up, w_down, vectors, bias_up):
    sequences = MICRO * ROWS
    together = 4 if sequences % 4 == 0 else 1
    steps_total = sequences // together
    flat_inputs = inputs.astype(jnp.float32).reshape(steps_total, together, LEN, D)
    flat_segments = segments.astype(jnp.int32).reshape(steps_total, together, LEN)
    flat_cotangent = cotangent.astype(jnp.float32).reshape(steps_total, together, LEN, D)
    weights = tuple((t.astype(jnp.float32) for t in (w_qkv, w_out, w_up, w_down, vectors, bias_up)))

    def scan_step(totals, slices):
        input_part, segment_part, cotangent_part = slices

        def forward_fn(values, *params):
            return block_forward(values, segment_part, *params)
        output_part, pullback = jax.vjp(forward_fn, input_part, *weights)
        gradients = pullback(cotangent_part)
        totals = tuple((a + b.astype(a.dtype) for a, b in zip(totals, gradients[1:])))
        return (totals, (output_part.astype(jnp.bfloat16), gradients[0].astype(input_part.dtype)))
    starting = tuple((jnp.zeros_like(t) for t in weights))
    totals, (outputs, input_grads) = lax.scan(scan_step, starting, (flat_inputs, flat_segments, flat_cotangent))
    return (outputs.reshape(MICRO, ROWS, LEN, D), input_grads.reshape(MICRO, ROWS, LEN, D), totals[0], totals[1], totals[2], totals[3], totals[4], totals[5])
```

```python
import functools
import math

import jax
import jax.numpy as jnp
from jax import lax
from jax.experimental import pallas as pl
from jax.experimental.pallas import tpu as pltpu
from jax.sharding import PartitionSpec as P

HEADS = 12
HEAD_DIM = 64
EPS = 1e-05
MASKED = -1e30
GELU_A = math.sqrt(2.0 / math.pi)
GELU_B = 0.044715
BF = jnp.bfloat16
F32 = jnp.float32
VMEM_LIMIT = 60 * 1024 * 1024


def shape(dims, dtype=BF):
    return jax.ShapeDtypeStruct(dims, dtype)


def vmem():
    return pl.BlockSpec(memory_space=pltpu.VMEM)


def smem():
    return pl.BlockSpec(memory_space=pltpu.SMEM)


def anywhere():
    return pl.BlockSpec(memory_space=pl.ANY)


def local_kernel(body, outs, name, flops=0, bytes_moved=0, exps=0, **kw):
    return pl.pallas_call(
        body,
        out_shape=outs,
        name=name,
        compiler_params=pltpu.CompilerParams(vmem_limit_bytes=VMEM_LIMIT),
        cost_estimate=pl.CostEstimate(
            flops=flops, bytes_accessed=bytes_moved, transcendentals=exps
        ),
        **kw,
    )


def mm(a, b):
    return lax.dot_general(a, b, (((1,), (0,)), ((), ())), preferred_element_type=F32)


def mm_nt(a, b):
    return lax.dot_general(a, b, (((1,), (1,)), ((), ())), preferred_element_type=F32)


def mm_tn(a, b):
    return lax.dot_general(a, b, (((0,), (0,)), ((), ())), preferred_element_type=F32)


def unit_rows(v):
    centred = v - jnp.mean(v, axis=-1, keepdims=True)
    inverse = lax.rsqrt(jnp.mean(centred * centred, axis=-1, keepdims=True) + EPS)
    return centred * inverse, inverse


def norm_back(grad, unit, inverse, gain):
    t = grad * gain
    first = jnp.mean(t, axis=-1, keepdims=True)
    second = jnp.mean(t * unit, axis=-1, keepdims=True)
    return inverse * (t - first - unit * second)


def pick(at, options):
    out = options[0]
    for s in range(1, len(options)):
        out = jnp.where(at == s, options[s], out)
    return out


def column_of(row, rows):
    return jnp.broadcast_to(row, (128, rows)).T[:, 0:1]


def prep_body(at_ref, wq_ref, up_ref, down_ref, extra_ref, qkv_ref, mlp_ref):
    rows = wq_ref.shape[0]
    width = up_ref.shape[1] // 4
    hw = wq_ref.shape[1] // 12
    part = down_ref.shape[0] // 4
    for s in range(4):

        @pl.when(at_ref[0] == s)
        def _(s=s):
            for n in range(3):
                base = n * 4 * hw + s * hw
                qkv_ref[:, n * hw : (n + 1) * hw] = wq_ref[:, base : base + hw]
            for i in range(width // part):
                col = i * 4 * part + s * part
                mlp_ref[0:rows, i * part : (i + 1) * part] = up_ref[:, col : col + part]
            mlp_ref[rows : rows + part, :] = down_ref[s * part : (s + 1) * part, :]

    qkv_ref[:, 3 * hw :] = extra_ref[...]


def place_body(count, at_ref, *refs):
    pieces, out, sems = refs[:count], refs[count], refs[count + 1]
    copies = [
        pltpu.make_async_copy(piece, out.at[at_ref[n]], sems.at[n])
        for n, piece in enumerate(pieces)
    ]
    for c in copies:
        c.start()
    for c in copies:
        c.wait()


def place(where, pieces, slots):
    return local_kernel(
        functools.partial(place_body, len(pieces)),
        shape((slots,) + pieces[0].shape),
        "place",
        bytes_moved=4 * slots * pieces[0].size,
        in_specs=[smem()] + [anywhere()] * len(pieces),
        out_specs=anywhere(),
        scratch_shapes=[pltpu.SemaphoreType.DMA((len(pieces),))],
    )(where, *pieces)


def segment_column(seg_ref, at, ranks):
    cols = []
    for k in range(4):
        row = seg_ref[pl.ds(ranks[k], 1), :].astype(F32)
        cols.append(column_of(row, row.shape[1]))
    return jnp.concatenate(cols, axis=0)


def forward_body(
    at_ref, x0, x1, x2, x3, w_ref, seg_ref,
    n1_ref, q_ref, k_ref, kt_ref, v_ref, c0, c1, c2, c3, lse_ref, vt_ref, vtr_ref,
):
    at = at_ref[0]
    ranks = [at ^ k for k in range(4)]
    tokens, width = x0.shape
    hw = q_ref.shape[1]
    heads = hw // HEAD_DIM
    tail = (3 * hw) // 128 * 128
    off = 3 * hw - tail
    vt_ref[...] = w_ref[:, tail : tail + 128].astype(F32).T[off : off + 16]
    g1, s1 = vt_ref[0:1, :], vt_ref[1:2, :]
    bq = pick(at, [vt_ref[2:3, s * hw : (s + 1) * hw] for s in range(4)])
    bv = pick(at, [vt_ref[3:4, s * hw : (s + 1) * hw] for s in range(4)])
    for k, x_ref in enumerate((x0, x1, x2, x3)):
        rows = slice(k * tokens, (k + 1) * tokens)
        unit, _ = unit_rows(x_ref[...].astype(F32))
        normed = (unit * g1 + s1).astype(BF)
        n1_ref[rows, :] = normed
        project = mm(normed, w_ref[:, : 3 * hw])
        q_ref[rows, :] = ((project[:, :hw] + bq) * 0.125).astype(BF)
        keys = project[:, hw : 2 * hw]
        k_ref[rows, :] = keys.astype(BF)
        kt_ref[:, rows] = keys.T.astype(BF)
        values = project[:, 2 * hw : 3 * hw] + bv
        v_ref[rows, :] = values.astype(BF)
        vtr_ref[:, rows] = values.T.astype(BF)
    seg_col = segment_column(seg_ref, at, ranks)
    lane_head = lax.broadcasted_iota(jnp.int32, (1, hw), 1) // HEAD_DIM
    lse_ref[...] = jnp.zeros(lse_ref.shape, F32)
    for b, c_ref in enumerate((c0, c1, c2, c3)):
        cols = slice(b * tokens, (b + 1) * tokens)
        seg_row = seg_ref[pl.ds(ranks[b], 1), :].astype(F32)
        bias = jnp.where(seg_col == seg_row, 0.0, MASKED)
        for h in range(heads):
            qh = jnp.where(lane_head == h, q_ref[cols, :], 0).astype(BF)
            s = mm_nt(k_ref[...], qh) + bias
            top = jnp.max(s, axis=0, keepdims=True)
            e = jnp.exp(s - top)
            total = jnp.sum(e, axis=0, keepdims=True)
            part = slice(h * HEAD_DIM, (h + 1) * HEAD_DIM)
            context = mm(vtr_ref[part, :], e.astype(BF)) * (1.0 / total)
            c_ref[part, :] = context.astype(BF)
            lse_ref[h : h + 1, cols] = top + jnp.log(total)


def forward(at, xs, w, seg):
    tokens, width = xs[0].shape
    hw = width // 4
    length = 4 * tokens
    outs = (
        shape((length, width)),
        shape((length, hw)),
        shape((length, hw)),
        shape((hw, length)),
        shape((length, hw)),
        *(shape((hw, tokens)),) * 4,
        shape((8, length), F32),
        shape((16, width), F32),
    )
    flops = 2 * length * width * 3 * hw + 16 * length * length * hw
    return local_kernel(
        forward_body, outs, "attention_forward", flops, 4 * length * width * 2, 3 * length * length,
        in_specs=[smem()] + [vmem()] * 6,
        out_specs=(vmem(),) * len(outs),
        scratch_shapes=[pltpu.VMEM((hw, length), BF)],
    )(at, *xs, w, seg)


def middle_body(at_ref, c0, c1, c2, c3, x_ref, w_ref, vt_ref, y_ref, n2_ref):
    at = at_ref[0]
    hw = c0.shape[0]
    y = x_ref[...].astype(F32) + vt_ref[4:5, :]
    for k, c_ref in enumerate((c0, c1, c2, c3)):
        base = pl.multiple_of((at ^ k) * hw, 64)
        y = y + mm_tn(c_ref[...], w_ref[pl.ds(base, hw), :])
    y_ref[...] = y
    unit, _ = unit_rows(y)
    n2_ref[...] = (unit * vt_ref[5:6, :] + vt_ref[6:7, :]).astype(BF)


def middle(at, cs, x, w_out, vt):
    outs = (shape(x.shape, F32), shape(x.shape))
    return local_kernel(
        middle_body, outs, "middle", 2 * x.size * x.shape[1], 6 * x.size * 2, 0,
        in_specs=[smem()] + [vmem()] * 7,
        out_specs=(vmem(), vmem()),
    )(at, *cs, x, w_out, vt)


def mlp_body(fast, first, micros, at_ref, *refs):
    refs = list(refs)
    take = lambda n: [refs.pop(0) for _ in range(n)]
    n2_refs = take(micros)
    dz_ref, vt_ref = take(2)
    weights = take(4)
    z_in, dn_in = (None, None) if first else take(2)
    z_ref, dn_ref = take(2)
    grads = take(4)
    (bias_ref,) = take(1)
    wu_s, wd_s, n2_s, n2t_s, sem_u, sem_d = take(6)
    step = pl.program_id(0)
    chunk, half = step // 2, step % 2
    width = n2_s.shape[1]
    tokens = n2_s.shape[0] // micros
    hf = wd_s.shape[1]
    y = at_ref[1]

    @pl.when(step == 0)
    def _():
        for t in range(4):
            ch, hh = t // 2, t % 2
            if fast:
                rows = weights[0].shape[1] // 2
                nz = weights[0].shape[0]
                for side in range(2):
                    src = weights[2 * ch + side]
                    yy = y if side == 0 else 1 - y
                    for z in range(nz):
                        dest = pl.multiple_of((2 * z + yy) * rows, 16)
                        pltpu.make_async_copy(
                            src.at[z, pl.ds(0, rows), pl.ds(hh * hf, hf)],
                            wu_s.at[t, pl.ds(dest, rows), :],
                            sem_u.at[t],
                        ).start()
                    for z in range(hh * nz // 2, (hh + 1) * nz // 2):
                        dest = pl.multiple_of((2 * z + yy) * rows - hh * hf, 16)
                        pltpu.make_async_copy(
                            src.at[z, pl.ds(rows, rows), :],
                            wd_s.at[t, pl.ds(dest, rows), :],
                            sem_d.at[t],
                        ).start()
            else:
                pltpu.make_async_copy(
                    weights[2 * ch].at[:, pl.ds(hh * hf, hf)], wu_s.at[t], sem_u.at[t]
                ).start()
                pltpu.make_async_copy(
                    weights[2 * ch + 1].at[pl.ds(hh * hf, hf), :], wd_s.at[t], sem_d.at[t]
                ).start()
        for m in range(micros):
            n2_s[m * tokens : (m + 1) * tokens, :] = n2_refs[m][...]
        n2t_s[...] = n2_s[...].T
        bias_ref[...] = jnp.zeros(bias_ref.shape, F32)
        if first:
            z_ref[...] = jnp.zeros(z_ref.shape, F32)
            dn_ref[...] = jnp.zeros(dn_ref.shape, F32)
        else:
            z_ref[...] = z_in[...]
            dn_ref[...] = dn_in[...]

    pltpu.make_async_copy(wu_s.at[step], wu_s.at[step], sem_u.at[step]).wait()
    pltpu.make_async_copy(wd_s.at[step], wd_s.at[step], sem_d.at[step]).wait()
    wu, wd = wu_s[step], wd_s[step]
    lead = at_ref[2] + chunk
    lanes = pl.ds(pl.multiple_of(half * hf, 128), hf)
    bias = vt_ref[pl.ds(8 + (at_ref[0] ^ lead), 1), lanes]
    u = mm(n2_s[...], wu) + bias
    square = u * u
    t = jnp.tanh(GELU_A * u * (1.0 + GELU_B * square))
    f = (0.5 * u * (1.0 + t)).astype(BF)
    slope = 0.5 * (1.0 + t) + (0.5 * GELU_A) * u * (1.0 - t * t) * (1.0 + 3.0 * GELU_B * square)
    dz = dz_ref[...]
    z_ref[...] += mm(f, wd)
    du = (mm_nt(dz, wd) * slope).astype(BF)
    dn_ref[...] += mm_nt(du, wu)
    bias_ref[pl.ds(chunk, 1), lanes] = jnp.sum(du.astype(F32), axis=0, keepdims=True)
    grad_up = mm(n2t_s[...], du).astype(BF)
    grad_down = mm_tn(f, dz).astype(BF)
    for ch in range(2):
        for hh in range(2):

            @pl.when(step == 2 * ch + hh)
            def _(ch=ch, hh=hh):
                span = slice(hh * hf, (hh + 1) * hf)
                if not fast:
                    grads[2 * ch][:, span] = grad_up
                    grads[2 * ch + 1][span, :] = grad_down
                    return
                rows = grads[0].shape[1] // 2
                count = 2 * grads[0].shape[0]
                for yy in range(2):

                    @pl.when(y == yy)
                    def _(yy=yy):
                        for i in range(count):
                            out = grads[2 * ch + (i % 2 != yy)]
                            out[i // 2, 0:rows, span] = grad_up[i * rows : (i + 1) * rows]
                        for n in range(count // 2):
                            i = hh * count // 2 + n
                            out = grads[2 * ch + (i % 2 != yy)]
                            out[i // 2, rows : 2 * rows, :] = grad_down[n * rows : (n + 1) * rows]


def mlp(fast, info, n2s, dz, vt, weights, carried):
    first = carried is None
    tokens, width = dz.shape
    hf = width // 2
    acc = shape((tokens, width), F32)
    outs = (acc, acc, *(shape(w.shape) for w in weights), shape((8, width), F32))
    ins = (info, *n2s, dz, vt, *weights, *(() if first else carried))
    whole = lambda dims: pl.BlockSpec(dims, lambda i: (0,) * len(dims))
    specs = [smem()] + [whole(a.shape) for a in (*n2s, dz, vt)] + [anywhere()] * 4
    specs += [] if first else [whole(a.shape) for a in carried]
    return local_kernel(
        functools.partial(mlp_body, fast, first, len(n2s)), outs, "feed_forward",
        4 * 12 * tokens * width * hf, 30 * tokens * width, 4 * tokens * hf,
        grid=(4,),
        in_specs=specs,
        out_specs=tuple(whole(o.shape) for o in outs),
        scratch_shapes=[
            pltpu.VMEM((4, width, hf), BF),
            pltpu.VMEM((4, hf, width), BF),
            pltpu.VMEM((tokens, width), BF),
            pltpu.VMEM((width, tokens), BF),
            pltpu.SemaphoreType.DMA((4,)),
            pltpu.SemaphoreType.DMA((4,)),
        ],
    )(*ins)


def turn_body(
    at_ref, y_ref, z_ref, dn_ref, dz_ref, w_ref, vt_ref,
    result_ref, dy_ref, da_ref, d0, d1, d2, d3, sums_ref,
):
    at = at_ref[0]
    hw = d0.shape[0]
    y = y_ref[...]
    result_ref[...] = (y + z_ref[...] + vt_ref[7:8, :]).astype(BF)
    unit, inverse = unit_rows(y)
    dz = dz_ref[...].astype(F32)
    dn = dn_ref[...]
    dy = dz + norm_back(dn, unit, inverse, vt_ref[5:6, :])
    dy_ref[...] = dy
    da = dy.astype(BF)
    da_ref[...] = da
    for k, d_ref in enumerate((d0, d1, d2, d3)):
        base = pl.multiple_of((at ^ k) * hw, 64)
        d_ref[...] = mm_nt(w_ref[pl.ds(base, hw), :], da).astype(BF)
    total = lambda a: jnp.sum(a, axis=0, keepdims=True)
    sums_ref[...] = jnp.concatenate(
        [total(da.astype(F32)), total(dn * unit), total(dn), total(dz), jnp.zeros((4, y.shape[1]), F32)], axis=0
    )


def turn(at, micro, y, z, dn, dz, w_out, vt):
    tokens, width = y.shape
    hw = width // 4
    block = pl.BlockSpec((tokens, width), lambda i: (micro, 0))
    whole = lambda dims: pl.BlockSpec(dims, lambda i: (0,) * len(dims))
    outs = (
        shape((tokens, width)),
        shape((tokens, width), F32),
        shape((tokens, width)),
        *(shape((hw, tokens)),) * 4,
        shape((8, width), F32),
    )
    return local_kernel(
        turn_body, outs, "turn", 2 * tokens * width * width, 20 * tokens * width, 0,
        grid=(1,),
        in_specs=[smem(), whole(y.shape), block, block, block, whole(w_out.shape), whole(vt.shape)],
        out_specs=tuple(whole(o.shape) for o in outs),
    )(at, y, z, dn, dz, w_out, vt)


def outproj_body(fast, micros, info_ref, *refs):
    refs = list(refs)
    cs = [[refs.pop(0) for _ in range(4)] for _ in range(micros)]
    das = [refs.pop(0) for _ in range(micros)]
    outs, scratch = refs[:-1], refs[-1]
    hw = cs[0][0].shape[0]
    at, y = info_ref[0], info_ref[1]
    da = jnp.concatenate([d[...] for d in das], axis=0)
    for k in range(4):
        left = jnp.concatenate([cs[m][k][...] for m in range(micros)], axis=1)
        base = pl.multiple_of((at ^ k) * hw, 64)
        scratch[pl.ds(base, hw), :] = mm(left, da)
    if not fast:
        outs[0][...] = scratch[...]
        return
    keep, keep_other, send = outs
    nz, part = keep.shape[0], keep.shape[1]
    core = at % 2
    for z in range(nz):
        for n in range(2):
            i = 2 * z + (y if n == 0 else 1 - y)
            base = i * 2 * part
            mine = pl.multiple_of(base + core * part, 16)
            others = pl.multiple_of(base + (1 - core) * part, 16)
            (keep, keep_other)[n][z] = scratch[pl.ds(mine, part), :].astype(BF)
            send[n, z] = scratch[pl.ds(others, part), :].astype(BF)


def outproj_grad(fast, info, cs, das, nz, part):
    hw, tokens = cs[0][0].shape
    width = das[0].shape[1]
    micros = len(das)
    if fast:
        one = shape((nz, part, width))
        outs = (one, one, shape((2, nz, part, width)))
    else:
        outs = (shape((width, width), F32),)
    return local_kernel(
        functools.partial(outproj_body, fast, micros), outs, "outproj_grad",
        2 * micros * tokens * width * width, 6 * width * width, 0,
        in_specs=[smem()] + [vmem()] * (5 * micros),
        out_specs=(vmem(),) * len(outs),
        scratch_shapes=[pltpu.VMEM((width, width), F32)],
    )(info, *(c for group in cs for c in group), *das)


def backward_body(first, at_ref, *refs):
    refs = list(refs)
    take = lambda n: [refs.pop(0) for _ in range(n)]
    ds, cs, xs = take(4), take(4), take(4)
    q_ref, k_ref, kt_ref, v_ref, lse_ref, seg_ref, w_ref, n1_ref, vt_ref = take(9)
    acc_in, sums_in = (None, None) if first else take(2)
    acc_ref, sums_ref, dn0_ref, dn2_ref, dn13_ref = take(5)
    dk_s, dv_s, dp_s = take(3)
    at = at_ref[0]
    ranks = [at ^ k for k in range(4)]
    hw, tokens = ds[0].shape
    heads = hw // HEAD_DIM
    seg_col = segment_column(seg_ref, at, ranks)
    lane_head = lax.broadcasted_iota(jnp.int32, (1, hw), 1) // HEAD_DIM
    for b in range(4):
        rows = slice(b * tokens, (b + 1) * tokens)
        seg_row = seg_ref[pl.ds(ranks[b], 1), :].astype(F32)
        bias = jnp.where(seg_col == seg_row, 0.0, MASKED)
        dct = ds[b][...]
        dc = dct.T
        product = dct.astype(F32) * cs[b][...].astype(F32)
        grads, probs, queries, contexts, dqs = [], [], [], [], []
        for h in range(heads):
            part = slice(h * HEAD_DIM, (h + 1) * HEAD_DIM)
            qh = jnp.where(lane_head == h, q_ref[rows, :], 0).astype(BF)
            dch = jnp.where(lane_head == h, dc, 0).astype(BF)
            p = jnp.exp(mm_nt(k_ref[...], qh) + bias - lse_ref[h : h + 1, rows])
            delta = jnp.sum(product[part], axis=0, keepdims=True)
            g = (p * (mm_nt(v_ref[...], dch) - delta)).astype(BF)
            grads.append(g)
            probs.append(p.astype(BF))
            queries.append(qh)
            contexts.append(dch)
            dqs.append(mm(kt_ref[part, :], g))
        dk = mm(jnp.concatenate(grads, axis=1), jnp.concatenate(queries, axis=0))
        dv = mm(jnp.concatenate(probs, axis=1), jnp.concatenate(contexts, axis=0))
        if b == 0:
            dk_s[...] = dk
            dv_s[...] = dv
        else:
            dk_s[...] += dk
            dv_s[...] += dv
        dq = jnp.concatenate(dqs, axis=0).T.astype(BF)
        dp_s[rows, 0:hw] = (dq.astype(F32) * 0.125).astype(BF)
    dp_s[:, hw : 2 * hw] = dk_s[...].astype(BF)
    dp_s[:, 2 * hw : 3 * hw] = dv_s[...].astype(BF)
    total = lambda a: jnp.sum(a, axis=0, keepdims=True)
    acc = mm_tn(n1_ref[...], dp_s[...])
    acc_ref[...] = acc if first else acc_in[...] + acc
    dg1 = ds1 = None
    outs = ((dn0_ref, 0), (dn13_ref, 0), (dn2_ref, 0), (dn13_ref, tokens))
    for k in range(4):
        rows = slice(k * tokens, (k + 1) * tokens)
        dn1 = mm_nt(dp_s[rows, :], w_ref[:, : 3 * hw])
        unit, _ = unit_rows(xs[k][...].astype(F32))
        a, b = total(dn1 * unit), total(dn1)
        dg1, ds1 = (a, b) if k == 0 else (dg1 + a, ds1 + b)
        ref, base = outs[k]
        ref[base : base + tokens, :] = dn1.astype(BF)
    dbq, dbv = (total(dp_s[:, n * hw : (n + 1) * hw].astype(F32)) for n in (0, 2))
    spread = lambda r: jnp.concatenate([jnp.where(at == s, r, 0.0) for s in range(4)], axis=1)
    sums = jnp.concatenate([dg1, ds1, spread(dbq), spread(dbv), jnp.zeros((4, dg1.shape[1]), F32)], axis=0)
    sums_ref[...] = sums if first else sums_in[...] + sums


def backward(at, ds, cs, xs, kept, seg, w, vt, carried):
    n1, q, k, kt, v, lse = kept
    hw, tokens = ds[0].shape
    length, width = n1.shape
    first = carried is None
    outs = (
        shape((width, 3 * hw), F32),
        shape((8, width), F32),
        shape((tokens, width)),
        shape((tokens, width)),
        shape((2 * tokens, width)),
    )
    ins = (*ds, *cs, *xs, q, k, kt, v, lse, seg, w, n1, vt, *(() if first else carried))
    flops = 4 * length * width * 3 * hw + 40 * length * length * hw
    return local_kernel(
        functools.partial(backward_body, first), outs, "attention_backward",
        flops, 8 * length * width * 2, 3 * length * length,
        in_specs=[smem()] + [vmem()] * len(ins),
        out_specs=(vmem(),) * len(outs),
        scratch_shapes=[
            pltpu.VMEM((length, hw), F32),
            pltpu.VMEM((length, hw), F32),
            pltpu.VMEM((length, 3 * hw), BF),
        ],
    )(at, *ins)


def finish_body(a_ref, b_ref, dy_ref, x_ref, vt_ref, gx_ref):
    unit, inverse = unit_rows(x_ref[...].astype(F32))
    dn1 = a_ref[...].astype(F32) + b_ref[...].astype(F32)
    gx_ref[...] = dy_ref[...] + norm_back(dn1, unit, inverse, vt_ref[0:1, :])


def finish(a, b, dy, x, vt):
    return local_kernel(
        finish_body, shape(x.shape, F32), "finish", 20 * x.size, 12 * x.size, 0,
        in_specs=[vmem()] * 5,
        out_specs=vmem(),
    )(a, b, dy, x, vt)


def pack_body(fast, info_ref, acc_ref, rows_ref, *outs):
    width = acc_ref.shape[0]
    hw3 = acc_ref.shape[1]
    columns = jnp.concatenate([rows_ref[...], jnp.zeros((112, width), F32)], axis=0).T[:, 0:64]
    full = jnp.concatenate([acc_ref[...], columns], axis=1)
    if not fast:
        outs[0][...] = full
        return
    own, other = outs
    nz, part = own.shape[0], own.shape[1]
    for y in range(2):

        @pl.when(info_ref[1] == y)
        def _(y=y):
            for i in range(2 * nz):
                out = own if i % 2 == y else other
                out[i // 2] = full[i * part : (i + 1) * part].astype(BF)


def pack(fast, info, acc, rows, nz, part):
    width = acc.shape[0]
    cols = acc.shape[1] + 64
    if fast:
        outs = (shape((nz, part, cols)),) * 2
    else:
        outs = (shape((width, cols), F32),)
    return local_kernel(
        functools.partial(pack_body, fast), outs, "pack", 0, 6 * width * cols, 0,
        in_specs=[smem(), vmem(), vmem()],
        out_specs=(vmem(),) * len(outs),
    )(info, acc, rows)


def assemble_body(
    at_ref, m0, m1, m2, m3, q0, q1, q2, q3, o0, o1,
    gq_ref, go_ref, gu_ref, gd_ref, ex_ref, ms, qs,
):
    at = at_ref[0]
    for k, r in enumerate((m0, m1, m2, m3)):
        ms[at ^ k] = r[...]
    for k, r in enumerate((q0, q1, q2, q3)):
        qs[at ^ k] = r[...].astype(F32)
    rows, part = gu_ref.shape[0], gd_ref.shape[0] // 4
    hw = gq_ref.shape[1] // 12
    for s in range(4):
        up = ms[s, 0:rows, :].astype(F32)
        for i in range(up.shape[1] // part):
            col = i * 4 * part + s * part
            gu_ref[:, col : col + part] = up[:, i * part : (i + 1) * part]
        gd_ref[s * part : (s + 1) * part, :] = ms[s, rows : rows + part, :].astype(F32)
        for n in range(3):
            base = n * 4 * hw + s * hw
            gq_ref[:, base : base + hw] = qs[s, :, n * hw : (n + 1) * hw]
    ex_ref[...] = (qs[0] + qs[1] + qs[2] + qs[3])[:, 3 * hw :]
    first = at % 2 == 0
    a, b = o0[...].astype(F32), o1[...].astype(F32)
    half = a.shape[0]
    go_ref[0:half, :] = jnp.where(first, a, b)
    go_ref[half : 2 * half, :] = jnp.where(first, b, a)


def assemble(at, ms, qs, os, ff):
    width = ms[0].shape[1]
    rows, cols = qs[0].shape
    part = ms[0].shape[0] - rows
    hw = (cols - 64) // 3
    outs = (
        shape((rows, 12 * hw), F32),
        shape((rows, width), F32),
        shape((rows, 4 * width), F32),
        shape((4 * part, width), F32),
        shape((rows, 64), F32),
    )
    return local_kernel(
        assemble_body, outs, "assemble", 0, 16 * rows * width * 4, 0,
        in_specs=[smem()] + [vmem()] * 10,
        out_specs=(vmem(),) * len(outs),
        scratch_shapes=[
            pltpu.VMEM((4,) + ms[0].shape, BF),
            pltpu.VMEM((4,) + qs[0].shape, F32),
        ],
    )(at, *ms, *qs, *os)


def send(x, axis, to):
    n = lax.axis_size(axis)
    return lax.ppermute(x, axis, [(s, to(s)) for s in range(n)])


def seq_swap(x, k):
    return send(x, "seq", lambda s: s ^ k)


def add(*terms):
    out = terms[0].astype(F32)
    for t in terms[1:]:
        out = out + t.astype(F32)
    return out.astype(BF)


def shards(inputs, segments, cotangent, w_qkv, w_out, w_up, w_down, vectors, bias_up):
    micros, _, tokens, width = inputs.shape
    nf = lax.axis_size("fsdp")
    assert lax.axis_size("seq") == 4 and inputs.shape[1] == 1
    rows = w_qkv.shape[0]
    part = w_down.shape[0] // 4
    hw = width // 4
    nz = nf // 2
    fast = nf == 8 and rows % 32 == 0 and part == rows
    at = lax.axis_index("seq")
    me = lax.axis_index("fsdp")
    z, y = me // 2, me % 2
    at1 = at[None].astype(jnp.int32)
    info = jnp.stack([at, y]).astype(jnp.int32)
    infos = [jnp.stack([at, y, jnp.int32(n)]).astype(jnp.int32) for n in (0, 2)]
    y_swap = lambda x: send(x, "fsdp", lambda s: s ^ 1)
    z_pull = lambda x, d: send(x, "fsdp", lambda s: (s - 2 * d) % nf)

    if fast:
        extra = jnp.concatenate([vectors, bias_up.reshape(4, part).T, jnp.zeros((rows, 52), BF)], axis=1)
        qkv_piece, mlp_piece = local_kernel(
            prep_body, (shape((rows, 3 * hw + 64)), shape((rows + part, width))), "prep",
            0, 6 * rows * 4 * width, 0,
            in_specs=[smem()] + [vmem()] * 4,
            out_specs=(vmem(), vmem()),
        )(at1, w_qkv, w_up, w_down, extra)
        out_piece = lax.dynamic_slice_in_dim(w_out, (at % 2) * (rows // 2), rows // 2, 0)
        zs = [(z + d) % nz for d in range(nz)]
        where_all = jnp.stack([2 * a + y for a in zs] + [2 * a + 1 - y for a in zs]).astype(jnp.int32)
        where_z = jnp.stack(zs).astype(jnp.int32)

        def over_zy(piece):
            pulled = [piece] + [z_pull(piece, d) for d in range(1, nz)]
            return pulled + [y_swap(p) for p in pulled]

        w_heads = place(where_all, over_zy(qkv_piece), nf).reshape(width, 3 * hw + 64)
        half = place(where_all, over_zy(out_piece), nf)
        other = seq_swap(half, 1)
        even = at % 2 == 0
        w_out_full = jnp.stack(
            [jnp.where(even, half, other), jnp.where(even, other, half)], axis=1
        ).reshape(width, width)
        own = place(where_z, [mlp_piece] + [z_pull(mlp_piece, d) for d in range(1, nz)], nz)
        oth = y_swap(own)
        own_x = seq_swap(own, 2)
        oth_x = y_swap(own_x)
        chunks = [
            (own, oth),
            (seq_swap(own, 1), seq_swap(oth, 1)),
            (own_x, oth_x),
            (seq_swap(own_x, 1), seq_swap(oth_x, 1)),
        ]
    else:
        gather = lambda a: lax.all_gather(a, "fsdp", axis=0, tiled=True)
        by_head = gather(w_qkv).reshape(width, 3, 4, hw)
        mine = lax.dynamic_index_in_dim(by_head, at, 2, keepdims=False).reshape(width, 3 * hw)
        biases = gather(bias_up).reshape(nf, 4, part).transpose(0, 2, 1).reshape(width, 4)
        w_heads = jnp.concatenate([mine, gather(vectors), biases, jnp.zeros((width, 52), BF)], axis=1)
        w_out_full = gather(w_out)
        ups = gather(w_up).reshape(width, nf, 4, part).transpose(2, 0, 1, 3).reshape(4, width, width)
        downs = gather(w_down).reshape(nf, 4, part, width).transpose(1, 0, 2, 3).reshape(4, width, width)
        one = lambda a, k: lax.dynamic_index_in_dim(a, at ^ k, 0, keepdims=False)
        chunks = [(one(ups, k), one(downs, k)) for k in range(4)]

    segs = segments[:, 0].reshape(micros, 4, tokens)
    own_x_rows = [inputs[m, 0] for m in range(micros)]
    saved, contexts, ys, n2s, spread = [], [], [], [], []
    vt = None
    for m in range(micros):
        x = own_x_rows[m]
        across = seq_swap(x, 2)
        xs = [x, seq_swap(x, 1), across, seq_swap(across, 1)]
        n1, q, k, kt, v, c0, c1, c2, c3, lse, vt = forward(at1, xs, w_heads, segs[m])
        cs = [c0, c1, c2, c3]
        spread.append((xs, cs))
        saved.append((n1, q, k, kt, v, lse))
        contexts.append([c0] + [seq_swap(cs[k], k) for k in (1, 2, 3)])
    for m in range(micros):
        y_m, n2 = middle(at1, contexts[m], own_x_rows[m], w_out_full, vt)
        ys.append(y_m)
        n2s.append(n2)

    dz = cotangent.reshape(micros * tokens, width)
    za, dna, *grads_a, bias_a = mlp(fast, infos[0], n2s, dz, vt, [*chunks[0], *chunks[1]], None)
    zb, dnb, *grads_b, bias_b = mlp(fast, infos[1], n2s, dz, vt, [*chunks[2], *chunks[3]], (za, dna))

    results, dys, das, dcs, row_sums = [], [], [], [], []
    for m in range(micros):
        result, dy, da, d0, d1, d2, d3, sums = turn(at1, m, ys[m], zb, dnb, dz, w_out_full, vt)
        results.append(result)
        dys.append(dy)
        das.append(da)
        row_sums.append(sums)
        dcs.append([d0, seq_swap(d1, 1), seq_swap(d2, 2), seq_swap(d3, 3)])
    out_grads = outproj_grad(fast, info, contexts, das, nz, rows // 2)
    carried = None
    grad_rows = []
    for m in range(micros):
        xs, cs = spread[m]
        acc, sums, dn0, dn2, dn13 = backward(
            at1, dcs[m], cs, xs, saved[m], segs[m], w_heads, vt, carried
        )
        carried = (acc, sums)
        got = seq_swap(dn13, 1)
        mine = add(dn0, got[:tokens])
        theirs = seq_swap(add(dn2, got[tokens:]), 2)
        grad_rows.append(finish(mine, theirs, dys[m], own_x_rows[m], vt))
    acc, sums = carried
    sums_turn = functools.reduce(jnp.add, row_sums)
    bias_rel = jnp.concatenate([bias_a[:2], bias_b[:2]], axis=0)
    bias_abs = jnp.stack(
        [lax.dynamic_index_in_dim(bias_rel, at ^ s, 0, keepdims=False) for s in range(4)]
    )
    rows16 = jnp.concatenate([sums[:4], sums_turn[:4], bias_abs, jnp.zeros((4, width), F32)], axis=0)
    packed = pack(fast, info, acc, rows16, nz, rows)

    if fast:

        def over_z(a):
            return add(
                lax.dynamic_index_in_dim(a, z, 0, keepdims=False),
                *(
                    z_pull(lax.dynamic_index_in_dim(a, (z - d) % nz, 0, keepdims=False), d)
                    for d in range(1, nz)
                ),
            )

        def seq_pieces(a):
            b = seq_swap(a, 2)
            return [a, seq_swap(a, 1), b, seq_swap(b, 1)]

        def chip_sum(k):
            mine, theirs = (grads_a[:2], grads_a[2:]) if k == 0 else (grads_b[:2], grads_b[2:])
            own, oth = (add(a, seq_swap(b, 1)) for a, b in zip(mine, theirs))
            return add(own, y_swap(oth))

        far = chip_sum(2)
        near = chip_sum(0)
        mlp_share = seq_pieces(over_z(add(near, seq_swap(far, 2))))
        keep, keep_other, to_core = out_grads
        from_core = seq_swap(to_core, 1)
        half = add(add(keep, from_core[0]), y_swap(add(keep_other, from_core[1])))
        half = over_z(add(half, seq_swap(half, 2)))
        out_share = [half, seq_swap(half, 1)]
        mine, oth = packed
        qkv_share = seq_pieces(over_z(add(mine, y_swap(oth))))
        g_qkv, g_out, g_up, g_down, g_extra = assemble(at1, mlp_share, qkv_share, out_share, w_up.shape[1])
        g_vec, g_bias = g_extra[:, :8], g_extra[:, 8:12].T.reshape(4 * part)
    else:
        total = lambda a: lax.psum(
            lax.psum_scatter(a.astype(F32), "fsdp", scatter_dimension=0, tiled=True), "seq"
        )
        head_place = lambda a: lax.dynamic_update_slice_in_dim(
            jnp.zeros((width, 3, 4, hw), F32), a.reshape(width, 3, 1, hw), at, 2
        ).reshape(width, 12 * hw)
        full = packed[0]
        g_qkv = total(head_place(full[:, : 3 * hw]))
        g_out = total(out_grads[0])
        extra = total(full[:, 3 * hw :])
        g_vec, g_bias = extra[:, :8], extra[:, 8:12].T.reshape(4 * part)
        pairs = [grads_a[:2], grads_a[2:], grads_b[:2], grads_b[2:]]
        order = lambda n: jnp.stack(
            [
                lax.dynamic_index_in_dim(jnp.stack([p[n] for p in pairs]), at ^ s, 0, keepdims=False)
                for s in range(4)
            ]
        )
        ups = order(0).reshape(4, width, nf, part).transpose(1, 2, 0, 3).reshape(width, 4 * width)
        downs = order(1).reshape(4, nf, part, width).transpose(1, 0, 2, 3).reshape(4 * width, width)
        g_up, g_down = total(ups), total(downs)
    return (
        jnp.stack(results)[:, None],
        jnp.stack(grad_rows)[:, None],
        g_qkv,
        g_out,
        g_up,
        g_down,
        g_vec,
        g_bias,
    )


def solution(mesh):
    rows = P(None, "fsdp", "seq", None)
    first = P("fsdp", None)
    in_specs = (rows, P(None, "fsdp", None), rows, first, first, first, first, first, P("fsdp"))
    out_specs = (rows, rows, first, first, first, first, first, P("fsdp"))
    return jax.shard_map(shards, mesh=mesh, in_specs=in_specs, out_specs=out_specs, check_vma=False)
```

```python
import functools
import math

import jax
import jax.numpy as jnp
from jax import lax
from jax.experimental import pallas as pl
from jax.experimental.pallas import tpu as pltpu
from jax.sharding import PartitionSpec as P

HEADS = 12
HEAD_DIM = 64
EPS = 1e-05
MASKED = -1e30
GELU_A = math.sqrt(2.0 / math.pi)
GELU_B = 0.044715
BF = jnp.bfloat16
F32 = jnp.float32
VMEM_LIMIT = 60 * 1024 * 1024


def shape(dims, dtype=BF):
    return jax.ShapeDtypeStruct(dims, dtype)


def vmem():
    return pl.BlockSpec(memory_space=pltpu.VMEM)


def smem():
    return pl.BlockSpec(memory_space=pltpu.SMEM)


def anywhere():
    return pl.BlockSpec(memory_space=pl.ANY)


def local_kernel(body, outs, name, flops=0, bytes_moved=0, exps=0, **kw):
    return pl.pallas_call(
        body,
        out_shape=outs,
        name=name,
        compiler_params=pltpu.CompilerParams(vmem_limit_bytes=VMEM_LIMIT),
        cost_estimate=pl.CostEstimate(
            flops=flops, bytes_accessed=bytes_moved, transcendentals=exps
        ),
        **kw,
    )


def mm(a, b):
    return lax.dot_general(a, b, (((1,), (0,)), ((), ())), preferred_element_type=F32)


def mm_nt(a, b):
    return lax.dot_general(a, b, (((1,), (1,)), ((), ())), preferred_element_type=F32)


def mm_tn(a, b):
    return lax.dot_general(a, b, (((0,), (0,)), ((), ())), preferred_element_type=F32)


def unit_rows(v):
    centred = v - jnp.mean(v, axis=-1, keepdims=True)
    inverse = lax.rsqrt(jnp.mean(centred * centred, axis=-1, keepdims=True) + EPS)
    return centred * inverse, inverse


def norm_back(grad, unit, inverse, gain):
    t = grad * gain
    first = jnp.mean(t, axis=-1, keepdims=True)
    second = jnp.mean(t * unit, axis=-1, keepdims=True)
    return inverse * (t - first - unit * second)


def pick(at, options):
    out = options[0]
    for s in range(1, len(options)):
        out = jnp.where(at == s, options[s], out)
    return out


def column_of(row, rows):
    return jnp.broadcast_to(row, (128, rows)).T[:, 0:1]


def prep_body(info_ref, wq_ref, wo_ref, up_ref, down_ref, vec_ref, bias_ref, qkv_ref, mlp_ref):
    rows = wq_ref.shape[0]
    width = up_ref.shape[1] // 4
    hw = wq_ref.shape[1] // 12
    part = down_ref.shape[0] // 4
    for s in range(4):

        @pl.when(info_ref[0] == s)
        def _(s=s):
            for n in range(3):
                base = n * 4 * hw + s * hw
                qkv_ref[:, n * hw : (n + 1) * hw] = wq_ref[:, base : base + hw]
            for i in range(width // part):
                col = i * 4 * part + s * part
                mlp_ref[0:rows, i * part : (i + 1) * part] = up_ref[:, col : col + part]
            mlp_ref[rows : rows + part, :] = down_ref[s * part : (s + 1) * part, :]
            third = rows // 3
            mlp_ref[rows + part :, :] = wo_ref[s % 3 * third : (s % 3 + 1) * third, :]

    lines = jnp.concatenate([vec_ref[...].astype(F32), bias_ref[...].astype(F32)], axis=0)
    lines = jnp.concatenate([lines, jnp.zeros((128 - lines.shape[0], rows), F32)], axis=0)
    qkv_ref[:, 3 * hw : 3 * hw + 64] = lines.T[:, 0:64].astype(BF)


def windows(segments, block):
    length = segments.shape[-1]
    first, last = segments[:, ::block, None], segments[:, block - 1 :: block, None]
    low = jnp.sum(segments[:, None, :] < first, axis=-1)
    high = jnp.sum(segments[:, None, :] <= last, axis=-1)
    low = low // 128 * 128
    count = (high - low + block - 1) // block
    start = jnp.minimum(low, length - count * block)
    return jnp.stack([start, count], axis=-1).astype(jnp.int32).reshape(-1)


def for_window(ranges_ref, at, block, body):
    start = pl.multiple_of(ranges_ref[2 * at], 128)
    for size in range(1, 5):

        @pl.when(ranges_ref[2 * at + 1] == size)
        def _(size=size):
            body(pl.ds(start, size * block))


def heads_apart(rows, heads):
    lane_head = lax.broadcasted_iota(jnp.int32, (1, rows.shape[1]), 1) // HEAD_DIM
    return jnp.concatenate([jnp.where(lane_head == h, rows, 0).astype(BF) for h in range(heads)], axis=0)


def own_blocks(wide, heads):
    width = wide.shape[1] // heads
    return [
        wide[h * HEAD_DIM : (h + 1) * HEAD_DIM, h * width : (h + 1) * width] for h in range(heads)
    ]


def picked(array, at):
    if array.ndim == 2:
        return pl.BlockSpec(array.shape, lambda i: (0, 0))
    return pl.BlockSpec((None,) + array.shape[1:], lambda i: (at,) + (0,) * (array.ndim - 1))


def whole(dims):
    return pl.BlockSpec(dims, lambda i: (0,) * len(dims))


def forward_body(info_ref, ranges_ref, x0, x1, x2, x3, seg_ref, w_ref, *refs):
    q_ref, k_ref, v_ref, c_ref, lse_ref, vt_ref, n1_ref, vtr_ref, seg_s = refs
    at = info_ref[0]
    micro = pl.program_id(0)
    tokens, width = x0.shape
    hw = q_ref.shape[1]
    heads = hw // HEAD_DIM
    tail = (3 * hw) // 128 * 128
    off = 3 * hw - tail
    vt_ref[...] = w_ref[:, tail : tail + 128].astype(F32).T[off : off + 16]
    g1, s1 = vt_ref[0:1, :], vt_ref[1:2, :]
    bq = pick(at, [vt_ref[2:3, s * hw : (s + 1) * hw] for s in range(4)])
    bv = pick(at, [vt_ref[3:4, s * hw : (s + 1) * hw] for s in range(4)])
    seg_s[...] = jnp.broadcast_to(seg_ref[...].astype(F32), (128, seg_ref.shape[1])).T
    for k, x_ref in enumerate((x0, x1, x2, x3)):
        unit, _ = unit_rows(x_ref[...].astype(F32))
        n1_ref[pl.ds(pl.multiple_of((at ^ k) * tokens, 128), tokens), :] = (unit * g1 + s1).astype(BF)
    project = mm(n1_ref[...], w_ref[:, : 3 * hw])
    q_ref[...] = ((project[:, :hw] + bq) * 0.125).astype(BF)
    keys = project[:, hw : 2 * hw]
    k_ref[...] = keys.astype(BF)
    values = project[:, 2 * hw : 3 * hw] + bv
    v_ref[...] = values.astype(BF)
    vtr_ref[...] = values.T.astype(BF)
    lse_ref[...] = jnp.zeros(lse_ref.shape, F32)

    def block(b, carry):
        rows = pl.ds(pl.multiple_of(b * tokens, 128), tokens)
        queries = heads_apart(q_ref[rows, :], heads)
        seg_row = seg_ref[0:1, rows].astype(F32)

        def body(span):
            bias = jnp.where(seg_s[span, 0:1] == seg_row, 0.0, MASKED)
            scores = mm_nt(k_ref[span, :], queries) + jnp.concatenate([bias] * heads, axis=1)
            top = jnp.max(scores, axis=0, keepdims=True)
            raised = jnp.exp(scores - top)
            total = jnp.sum(raised, axis=0, keepdims=True)
            context = mm(vtr_ref[:, span], raised.astype(BF)) * (1.0 / total)
            c_ref[b] = jnp.concatenate(own_blocks(context, heads), axis=0).astype(BF)
            log_sum = top + jnp.log(total)
            for h in range(heads):
                lse_ref[h : h + 1, rows] = log_sum[:, h * tokens : (h + 1) * tokens]

        for_window(ranges_ref, 4 * micro + b, tokens, body)
        return carry

    lax.fori_loop(0, 4, block, 0)


def quarters(array, at=None):
    dims = (array.shape[0], None) + array.shape[2:]
    return pl.BlockSpec(dims, (lambda i: (0, i, 0, 0)) if at is None else (lambda i: (0, at, 0, 0)))


def forward(info, ranges, xs, seg, w):
    micros, tokens, width = xs[0].shape
    hw = width // 4
    length = 4 * tokens
    outs = (
        shape((micros, length, hw)),
        shape((micros, length, hw)),
        shape((micros, length, hw)),
        shape((4, micros, hw, tokens)),
        shape((micros, 8, length), F32),
        shape((16, width), F32),
    )
    flops = micros * (2 * length * width * 3 * hw + 16 * length * length * hw)
    return local_kernel(
        forward_body, outs, "attention_forward",
        flops, micros * 4 * length * width * 2, micros * 3 * length * length,
        grid=(micros,),
        in_specs=[smem(), smem()] + [stepped(a) for a in (*xs, seg)] + [whole(w.shape)],
        out_specs=tuple(quarters(o) if n == 3 else stepped(o) for n, o in enumerate(outs)),
        scratch_shapes=[
            pltpu.VMEM((length, width), BF),
            pltpu.VMEM((hw, length), BF),
            pltpu.VMEM((length, 128), F32),
        ],
    )(info, ranges, *xs, seg, w)


def stepped(array, start=0):
    if array.ndim == 2:
        return whole(array.shape)
    return pl.BlockSpec((None,) + array.shape[1:], lambda i: (start + i,) + (0,) * (array.ndim - 1))


def middle_body(halves, info_ref, c_ref, x_ref, vt_ref, *refs):
    if halves:
        src, y_ref, n2_ref, w_ref, sem = refs

        @pl.when(pl.program_id(0) == 0)
        def _():
            pieces = w_ref.shape[0] * 4 // src.shape[0]
            part = pieces // 3
            base = src.shape[1] - part
            copies = [
                pltpu.make_async_copy(
                    src.at[4 * i + s, pl.ds(base, part), :],
                    w_ref.at[pl.ds(i * pieces + s * part, part), :],
                    sem.at[3 * i + s],
                )
                for i in range(src.shape[0] // 4)
                for s in range(3)
            ]
            for c in copies:
                c.start()
            for c in copies:
                c.wait()
    else:
        w_ref, y_ref, n2_ref = refs
    context = c_ref[...].reshape(w_ref.shape[0], c_ref.shape[2])
    y = x_ref[...].astype(F32) + vt_ref[4:5, :] + mm_tn(context, w_ref[...])
    y_ref[...] = y
    unit, _ = unit_rows(y)
    n2_ref[...] = (unit * vt_ref[5:6, :] + vt_ref[6:7, :]).astype(BF)


def middle(info, c, inputs, vt, w):
    micros, tokens, width = inputs.shape
    halves = w.ndim == 3
    outs = (shape((micros * tokens, width), F32), shape((micros * tokens, width)))
    outs += (shape((width, width)),) if halves else ()
    rows = pl.BlockSpec((tokens, width), lambda i: (i, 0))
    return local_kernel(
        functools.partial(middle_body, halves), outs, "middle",
        2 * micros * tokens * width * width, 12 * micros * tokens * width, 0,
        grid=(micros,),
        in_specs=[smem(), quarters(c), stepped(inputs), whole(vt.shape), anywhere() if halves else whole(w.shape)],
        out_specs=(rows, rows) + ((whole((width, width)),) if halves else ()),
        scratch_shapes=[pltpu.SemaphoreType.DMA((w.shape[0],))] if halves else [],
    )(info, c, inputs, vt, w)


def mlp_body(fast, first, lead, info_ref, *refs):
    refs = list(refs)
    take = lambda n: [refs.pop(0) for _ in range(n)]
    n2_ref, dz_ref, vt_ref = take(3)
    weights = take(1 if fast else 4)
    z_in, dn_in = (None, None) if first else take(2)
    z_ref, dn_ref = take(2)
    grads = take(2)
    (bias_ref,) = take(1)
    wu_s, wd_s, n2t_s, g_s, sem_w, sem_g = take(6)
    if not first:
        za_s, dna_s, sem_a = take(3)
        carried = [
            pltpu.make_async_copy(z_in, za_s, sem_a.at[0]),
            pltpu.make_async_copy(dn_in, dna_s, sem_a.at[1]),
        ]
    step = pl.program_id(0)
    width = n2_ref.shape[1]
    y = info_ref[1]
    results = [pltpu.make_async_copy(g_s.at[n], grads[n], sem_g.at[n]) for n in range(2)]

    @pl.when(step == 0)
    def _():
        for ch in range(2):
            if fast:
                src = weights[0]
                count = src.shape[0] // 4
                rank = info_ref[0] ^ (lead + ch)
                rows = width // count
                for i in range(count):
                    for n, dest in enumerate((wu_s, wd_s)):
                        pltpu.make_async_copy(
                            src.at[4 * i + rank, pl.ds(n * rows, rows), :],
                            dest.at[ch, pl.ds(i * rows, rows), :],
                            sem_w.at[2 * ch + n],
                        ).start()
            else:
                for n, dest in enumerate((wu_s, wd_s)):
                    pltpu.make_async_copy(weights[2 * ch + n], dest.at[ch], sem_w.at[2 * ch + n]).start()
        if not first:
            for c in carried:
                c.start()
        n2t_s[...] = n2_ref[...].T
        bias_ref[...] = jnp.zeros(bias_ref.shape, F32)

    for n, dest in enumerate((wu_s, wd_s)):
        pltpu.make_async_copy(dest.at[step], dest.at[step], sem_w.at[2 * step + n]).wait()
    wu, wd = wu_s[step], wd_s[step]
    bias = vt_ref[pl.ds(8 + (info_ref[0] ^ (lead + step)), 1), :]
    u = mm(n2_ref[...], wu) + bias
    square = u * u
    t = jnp.tanh(GELU_A * u * (1.0 + GELU_B * square))
    f = (0.5 * u * (1.0 + t)).astype(BF)
    slope = 0.5 * (1.0 + t) + (0.5 * GELU_A) * u * (1.0 - t * t) * (1.0 + 3.0 * GELU_B * square)
    dz = dz_ref[...]
    du = (mm_nt(dz, wd) * slope).astype(BF)
    bias_ref[pl.ds(step, 1), :] = jnp.sum(du.astype(F32), axis=0, keepdims=True)
    grad_up = mm(n2t_s[...], du).astype(BF)
    grad_down = mm_tn(f, dz).astype(BF)
    if fast:
        count = 2 * g_s.shape[3]
        rows = width // count
        for yy in range(2):

            @pl.when(y == yy)
            def _(yy=yy):
                for i in range(count):
                    g_s[step, 0, int(i % 2 != yy), i // 2] = grad_up[i * rows : (i + 1) * rows]
                    g_s[step, 1, int(i % 2 != yy), i // 2] = grad_down[i * rows : (i + 1) * rows]
    else:
        g_s[step, 0] = grad_up
        g_s[step, 1] = grad_down
    for ch in range(2):

        @pl.when(step == ch)
        def _(ch=ch):
            results[ch].start()

    z, dn = mm(f, wd), mm_nt(du, wu)

    @pl.when(step == 0)
    def _():
        z_ref[...] = z
        dn_ref[...] = dn

    @pl.when(step == 1)
    def _():
        if first:
            z_ref[...] += z
            dn_ref[...] += dn
        else:
            for c in carried:
                c.wait()
            z_ref[...] += z + za_s[...]
            dn_ref[...] += dn + dna_s[...]
        for r in results:
            r.wait()


def mlp(fast, info, lead, n2, dz, vt, weights, carried):
    first = carried is None
    tokens, width = dz.shape
    acc = shape((tokens, width), F32)
    nf = weights[0].shape[0] // 4
    one = (2, 2, nf // 2, width // nf, width) if fast else (2, width, width)
    outs = (acc, acc, shape(one), shape(one), shape((8, width), F32))
    ins = (info, n2, dz, vt, *weights, *(() if first else carried))
    specs = [smem()] + [whole(a.shape) for a in (n2, dz, vt)] + [anywhere()] * len(weights)
    specs += [] if first else [anywhere()] * 2
    more = [] if first else [
        pltpu.VMEM((tokens, width), F32),
        pltpu.VMEM((tokens, width), F32),
        pltpu.SemaphoreType.DMA((2,)),
    ]
    return local_kernel(
        functools.partial(mlp_body, fast, first, lead), outs, "feed_forward",
        24 * tokens * width * width, 30 * tokens * width, 2 * tokens * width,
        grid=(2,),
        in_specs=specs,
        out_specs=(whole(acc.shape),) * 2 + (anywhere(),) * 2 + (whole((8, width)),),
        scratch_shapes=[
            pltpu.VMEM((2, width, width), BF),
            pltpu.VMEM((2, width, width), BF),
            pltpu.VMEM((width, tokens), BF),
            pltpu.VMEM((2,) + one, BF),
            pltpu.SemaphoreType.DMA((4,)),
            pltpu.SemaphoreType.DMA((2,)),
            *more,
        ],
    )(*ins)


def turn_body(chained, info_ref, y_ref, z_ref, dn_ref, dz_ref, w_ref, vt_ref, *refs):
    result_ref, dy_ref, da_ref, d_ref, sums_ref = refs[1:] if chained else refs
    y = y_ref[...]
    result_ref[...] = (y + z_ref[...] + vt_ref[7:8, :]).astype(BF)
    unit, inverse = unit_rows(y)
    dz = dz_ref[...].astype(F32)
    dn = dn_ref[...]
    dy = dz + norm_back(dn, unit, inverse, vt_ref[5:6, :])
    dy_ref[...] = dy
    da = dy.astype(BF)
    da_ref[...] = da
    d_ref[...] = mm_nt(w_ref[...], da).astype(BF).reshape(d_ref.shape)
    total = lambda a: jnp.sum(a, axis=0, keepdims=True)
    rest = jnp.zeros((4, y.shape[1]), F32)
    sums = jnp.concatenate([total(da.astype(F32)), total(dn * unit), total(dn), total(dz), rest], axis=0)

    @pl.when(pl.program_id(0) == 0)
    def _():
        sums_ref[...] = sums

    @pl.when(pl.program_id(0) > 0)
    def _():
        sums_ref[...] += sums


def turn(info, start, count, micros, y, z, dn, dz, w_out, vt, results):
    width = dz.shape[1]
    tokens = dz.shape[0] // micros
    hw = width // 4
    block = pl.BlockSpec((tokens, width), lambda i: (start + i, 0))
    rows = pl.BlockSpec((tokens, width), lambda i: (i, 0))
    outs = (
        shape((micros, tokens, width)),
        shape((count * tokens, width), F32),
        shape((count * tokens, width)),
        shape((4, count, hw, tokens)),
        shape((8, width), F32),
    )
    chained = results is not None
    return local_kernel(
        functools.partial(turn_body, chained), outs, "turn",
        2 * count * tokens * width * width, 20 * count * tokens * width, 0,
        grid=(count,),
        in_specs=[smem(), block, block, block, block, whole(w_out.shape), whole(vt.shape)]
        + ([anywhere()] if chained else []),
        out_specs=(stepped(outs[0], start), rows, rows, quarters(outs[3]), whole((8, width))),
        input_output_aliases={7: 0} if chained else {},
    )(info, y, z, dn, dz, w_out, vt, *((results,) if chained else ()))


def outproj_body(fast, info_ref, c_ref, *refs):
    outs, scratch = refs[:-1][-3 if fast else -1 :], refs[-1]
    das = refs[: -4 if fast else -2]
    at, y = info_ref[0], info_ref[1]
    da = jnp.concatenate([d[...] for d in das], axis=0)
    rows, micros = scratch.shape[0], c_ref.shape[1]
    left = jnp.concatenate([c_ref[:, m].reshape(rows, c_ref.shape[3]) for m in range(micros)], axis=1)
    scratch[...] = mm(left, da)
    if not fast:
        outs[0][...] = scratch[...]
        return
    keep, keep_other, send = outs
    nz, part, half = keep.shape
    first = lax.rem(at, 2) == 0
    for z in range(nz):
        for n in range(2):
            i = 2 * z + (y if n == 0 else 1 - y)
            block = scratch[pl.ds(pl.multiple_of(i * part, 16), part), :].astype(BF)
            left, right = block[:, :half], block[:, half:]
            (keep, keep_other)[n][z] = jnp.where(first, left, right)
            send[n, z] = jnp.where(first, right, left)


def outproj_grad(fast, info, c, das, nz, part):
    width = das[0].shape[1]
    total = sum(d.shape[0] for d in das)
    if fast:
        one = shape((nz, part, width // 2))
        outs = (one, one, shape((2, nz, part, width // 2)))
    else:
        outs = (shape((width, width), F32),)
    return local_kernel(
        functools.partial(outproj_body, fast), outs, "outproj_grad",
        2 * total * width * width, 6 * width * width, 0,
        in_specs=[smem()] + [vmem()] * (1 + len(das)),
        out_specs=(vmem(),) * len(outs),
        scratch_shapes=[pltpu.VMEM((width, width), F32)],
    )(info, c, *das)


def backward_body(first, last, micro, info_ref, ranges_ref, *refs):
    refs = list(refs)
    take = lambda n: [refs.pop(0) for _ in range(n)]
    d_ref, c_ref = take(2)
    xs = take(4)
    q_ref, k_ref, v_ref, lse_ref, seg_ref, w_ref, vt_ref = take(7)
    acc_in, sums_in = (None, None) if first else take(2)
    turned, biases = (take(2), take(2)) if last else ((), ())
    acc_ref, sums_ref, dn0_ref, dn2_ref, dn13_ref = take(5)
    dk_s, dv_s, dp_s, seg_s, dc_s, delta_s, kt_s, n1_s, unit_s = take(9)
    at = info_ref[0]
    _, hw, tokens = d_ref.shape
    heads = hw // HEAD_DIM
    seg_s[...] = jnp.broadcast_to(seg_ref[...].astype(F32), (128, seg_ref.shape[1])).T
    dk_s[...] = jnp.zeros(dk_s.shape, F32)
    dv_s[...] = jnp.zeros(dv_s.shape, F32)
    kt_s[...] = k_ref[...].astype(F32).T.astype(BF)
    for b in range(4):
        dct = d_ref[b].astype(F32)
        dc_s[b] = dct.T.astype(BF)
        product = dct * c_ref[b].astype(F32)
        for h in range(heads):
            delta_s[b, h : h + 1, :] = jnp.sum(product[h * HEAD_DIM : (h + 1) * HEAD_DIM], axis=0, keepdims=True)
    for k in range(4):
        rows = pl.ds(pl.multiple_of((at ^ k) * tokens, 128), tokens)
        unit, _ = unit_rows(xs[k][...].astype(F32))
        unit_s[rows, :] = unit
        n1_s[rows, :] = (unit * vt_ref[0:1, :] + vt_ref[1:2, :]).astype(BF)

    def block(b, carry):
        rows = pl.ds(pl.multiple_of(b * tokens, 128), tokens)
        queries = heads_apart(q_ref[rows, :], heads)
        contexts = heads_apart(dc_s[b], heads)
        seg_row = seg_ref[0:1, rows].astype(F32)
        log_sum = jnp.concatenate([lse_ref[h : h + 1, rows] for h in range(heads)], axis=1)
        delta = jnp.concatenate([delta_s[b, h : h + 1, :] for h in range(heads)], axis=1)

        def body(span):
            bias = jnp.where(seg_s[span, 0:1] == seg_row, 0.0, MASKED)
            scores = mm_nt(k_ref[span, :], queries) + jnp.concatenate([bias] * heads, axis=1)
            p = jnp.exp(scores - log_sum)
            g = (p * (mm_nt(v_ref[span, :], contexts) - delta)).astype(BF)
            dk_s[span, :] += mm(g, queries)
            dv_s[span, :] += mm(p.astype(BF), contexts)
            dq = jnp.concatenate(own_blocks(mm(kt_s[:, span], g), heads), axis=0).T.astype(BF)
            dp_s[rows, 0:hw] = (dq.astype(F32) * 0.125).astype(BF)

        for_window(ranges_ref, 4 * micro + b, tokens, body)
        return carry

    lax.fori_loop(0, 4, block, 0)
    dp_s[:, hw : 2 * hw] = dk_s[...].astype(BF)
    dp_s[:, 2 * hw : 3 * hw] = dv_s[...].astype(BF)
    total = lambda a: jnp.sum(a, axis=0, keepdims=True)
    acc = mm_tn(n1_s[...], dp_s[...])
    acc = acc if first else acc_in[...] + acc
    dg1 = ds1 = None
    outs = ((dn0_ref, 0), (dn13_ref, 0), (dn2_ref, 0), (dn13_ref, tokens))
    for k in range(4):
        rows = pl.ds(pl.multiple_of((at ^ k) * tokens, 128), tokens)
        dn1 = mm_nt(dp_s[rows, :], w_ref[:, : 3 * hw])
        a, b = total(dn1 * unit_s[rows, :]), total(dn1)
        dg1, ds1 = (a, b) if k == 0 else (dg1 + a, ds1 + b)
        ref, base = outs[k]
        ref[base : base + tokens, :] = dn1.astype(BF)
    dbq, dbv = (total(dp_s[:, n * hw : (n + 1) * hw].astype(F32)) for n in (0, 2))
    spread = lambda r: jnp.concatenate([jnp.where(at == s, r, 0.0) for s in range(4)], axis=1)
    sums = jnp.concatenate([dg1, ds1, spread(dbq), spread(dbv), jnp.zeros((4, dg1.shape[1]), F32)], axis=0)
    sums = sums if first else sums_in[...] + sums
    sums_ref[...] = sums
    if not last:
        acc_ref[...] = acc
        return
    width = acc.shape[0]
    rest = turned[0][...] + turned[1][...]
    chunk_rows = [biases[k // 2][k % 2 : k % 2 + 1, :] for k in range(4)]
    lines = [sums[0:4], rest[0:4]] + [pick(at ^ s, chunk_rows) for s in range(4)]
    lines = jnp.concatenate(lines + [jnp.zeros((116, width), F32)], axis=0)
    full = jnp.concatenate([acc, lines.T[:, 0:64]], axis=1)
    acc_ref[...] = full.astype(acc_ref.dtype).reshape(acc_ref.shape)


def backward(info, ranges, micro, d, d_at, c, xs, kept, seg, w, vt, carried, ends):
    q, k, v, lse = kept
    hw, tokens = d.shape[2:]
    length, width = k.shape[1], w.shape[0]
    first, last = carried is None, bool(ends)
    outs = (
        ends[-1] if last else shape((width, 3 * hw), F32),
        shape((8, width), F32),
        shape((tokens, width)),
        shape((tokens, width)),
        shape((2 * tokens, width)),
    )
    rest = (w, vt, *(() if first else carried), *ends[:-1])
    stacked = (*xs, q, k, v, lse, seg)
    specs = [smem(), smem(), quarters(d, d_at), quarters(c, micro)] + [picked(a, micro) for a in stacked]
    specs += [whole(a.shape) for a in rest]
    flops = 4 * length * width * 3 * hw + 40 * length * length * hw
    return local_kernel(
        functools.partial(backward_body, first, last, micro), outs, "attention_backward",
        flops, 8 * length * width * 2, 3 * length * length,
        grid=(1,),
        in_specs=specs,
        out_specs=tuple(whole(o.shape) for o in outs),
        scratch_shapes=[
            pltpu.VMEM((length, hw), F32),
            pltpu.VMEM((length, hw), F32),
            pltpu.VMEM((length, 3 * hw), BF),
            pltpu.VMEM((length, 128), F32),
            pltpu.VMEM((4, tokens, hw), BF),
            pltpu.VMEM((4, 8, tokens), F32),
            pltpu.VMEM((hw, length), BF),
            pltpu.VMEM((length, width), BF),
            pltpu.VMEM((length, width), F32),
        ],
    )(info, ranges, d, c, *stacked, *rest)


def finish_body(chained, a_ref, b_ref, r_ref, dy_ref, x_ref, vt_ref, *refs):
    gx_ref = refs[-1]
    unit, inverse = unit_rows(x_ref[...].astype(F32))
    dn1 = a_ref[...].astype(F32) + b_ref[...].astype(F32) + r_ref[...].astype(F32)
    gx_ref[...] = dy_ref[...] + norm_back(dn1, unit, inverse, vt_ref[0:1, :])


def finish(micro, a, b, r, dy, dy_at, inputs, vt, grads):
    tokens, width = a.shape
    chained = grads is not None
    out = shape(inputs.shape, F32)
    top = pl.BlockSpec((tokens, width), lambda i: (0, 0))
    return local_kernel(
        functools.partial(finish_body, chained), out, "finish", 20 * a.size, 14 * a.size, 0,
        grid=(1,),
        in_specs=[top, top, top, pl.BlockSpec((tokens, width), lambda i: (dy_at, 0)), picked(inputs, micro), whole(vt.shape)] + ([anywhere()] if chained else []),
        out_specs=picked(out, micro),
        input_output_aliases={6: 0} if chained else {},
    )(a, b, r, dy, inputs, vt, *((grads,) if chained else ()))


def assemble_mlp_body(info_ref, m0, m1, m2, m3, gu_ref, gd_ref, ms):
    at = info_ref[0]
    for k, r in enumerate((m0, m1, m2, m3)):
        ms[at ^ k] = r[...]
    rows, part = gu_ref.shape[0], gd_ref.shape[0] // 4
    for s in range(4):
        up = ms[s, 0:rows, :].astype(F32)
        for i in range(up.shape[1] // part):
            col = i * 4 * part + s * part
            gu_ref[:, col : col + part] = up[:, i * part : (i + 1) * part]
        gd_ref[s * part : (s + 1) * part, :] = ms[s, rows : rows + part, :].astype(F32)


def assemble_mlp(info, ms, rows):
    width = ms[0].shape[1]
    part = ms[0].shape[0] - rows
    outs = (shape((rows, 4 * width), F32), shape((4 * part, width), F32))
    return local_kernel(
        assemble_mlp_body, outs, "assemble_mlp", 0, 12 * rows * width * 4, 0,
        in_specs=[smem()] + [vmem()] * 4,
        out_specs=(vmem(),) * 2,
        scratch_shapes=[pltpu.VMEM((4,) + ms[0].shape, BF)],
    )(info, *ms)


def share_body(q_ref, o_ref, out_ref):
    total = lambda r: functools.reduce(jnp.add, [r[n].astype(F32) for n in range(r.shape[0])])
    out_ref[...] = jnp.concatenate([total(q_ref), total(o_ref)], axis=1).astype(BF)


def share(q, o):
    return local_kernel(
        share_body, shape((q.shape[1], q.shape[2] + o.shape[2])), "share", 0, 2 * (q.size + o.size), 0,
        in_specs=[vmem()] * 2,
        out_specs=vmem(),
    )(q, o)


def assemble_heads_body(q_ref, gq_ref, go_ref, gv_ref, gb_ref):
    hw = gq_ref.shape[1] // 12
    half = go_ref.shape[1] // 2
    for s in range(4):
        for n in range(3):
            base = n * 4 * hw + s * hw
            gq_ref[:, base : base + hw] = q_ref[s, :, n * hw : (n + 1) * hw].astype(F32)
    for h in range(2):
        a, b = (q_ref[h + 2 * n, :, 3 * hw + 64 :].astype(F32) for n in range(2))
        go_ref[:, h * half : (h + 1) * half] = a + b
    tail = (3 * hw) // 128 * 128
    off = 3 * hw - tail
    extra = functools.reduce(jnp.add, [q_ref[s, :, tail : tail + 128].astype(F32) for s in range(4)]).T
    gv_ref[...] = extra[off : off + 8]
    gb_ref[...] = extra[off + 8 : off + 12]


def assemble_heads(q, hw):
    rows = q.shape[1]
    outs = (
        shape((rows, 12 * hw), F32),
        shape((rows, 4 * hw), F32),
        shape((8, rows), F32),
        shape((4, rows), F32),
    )
    return local_kernel(
        assemble_heads_body, outs, "assemble_heads", 0, 12 * rows * hw * 16, 0,
        in_specs=[vmem()],
        out_specs=(vmem(),) * 4,
    )(q)


def send(x, axis, to):
    n = lax.axis_size(axis)
    return lax.ppermute(x, axis, [(s, to(s)) for s in range(n)])


def seq_swap(x, k):
    return send(x, "seq", lambda s: s ^ k)


def add(*terms):
    out = terms[0].astype(F32)
    for t in terms[1:]:
        out = out + t.astype(F32)
    return out.astype(BF)


def after(values, *others):
    out = lax.optimization_barrier((values, others))
    return out[0]


def shards(inputs, segments, cotangent, w_qkv, w_out, w_up, w_down, vectors, bias_up):
    micros, _, tokens, width = inputs.shape
    nf = lax.axis_size("fsdp")
    assert lax.axis_size("seq") == 4 and inputs.shape[1] == 1
    rows = w_qkv.shape[0]
    part = w_down.shape[0] // 4
    hw = width // 4
    nz = nf // 2
    fast = nf == 8 and rows % 32 == 0 and part == rows
    at = lax.axis_index("seq")
    me = lax.axis_index("fsdp")
    z, y = me // 2, me % 2
    info = jnp.stack([at, y, z]).astype(jnp.int32)
    y_swap = lambda x: send(x, "fsdp", lambda s: s ^ 1)
    z_pull = lambda x, d: send(x, "fsdp", lambda s: (s - 2 * d) % nf)
    pulled = lambda x: [x] + [z_pull(x, d) for d in range(1, nz)]

    ranges = windows(segments[:, 0], tokens)

    own = inputs[:, 0]
    across = seq_swap(own, 2)
    beside = seq_swap(own, 1)

    if fast:
        qkv_piece, mlp_piece = local_kernel(
            prep_body,
            (shape((rows, 3 * hw + 64)), shape((rows + part + rows // 3, width))),
            "prep", 0, 6 * rows * 4 * width, 0,
            in_specs=[smem()] + [vmem()] * 6,
            out_specs=(vmem(),) * 2,
        )(info, w_qkv, w_out, w_up, w_down, vectors.T, bias_up.reshape(4, part))
        w_heads = lax.all_gather(qkv_piece, "fsdp", axis=0, tiled=True)
        gathered = lax.all_gather(mlp_piece, ("fsdp", "seq"), axis=0, tiled=False)
    else:
        gather = lambda a: lax.all_gather(a, "fsdp", axis=0, tiled=True)
        by_head = gather(w_qkv).reshape(width, 3, 4, hw)
        mine = lax.dynamic_index_in_dim(by_head, at, 2, keepdims=False).reshape(width, 3 * hw)
        biases = gather(bias_up).reshape(nf, 4, part).transpose(0, 2, 1).reshape(width, 4)
        w_heads = jnp.concatenate([mine, gather(vectors), biases, jnp.zeros((width, 52), BF)], axis=1)
        w_out_full = gather(w_out)
        ups = gather(w_up).reshape(width, nf, 4, part).transpose(2, 0, 1, 3).reshape(4, width, width)
        downs = gather(w_down).reshape(nf, 4, part, width).transpose(1, 0, 2, 3).reshape(4, width, width)
        one = lambda a, k: lax.dynamic_index_in_dim(a, at ^ k, 0, keepdims=False)
        chunks = [(one(ups, k), one(downs, k)) for k in range(4)]

    xs = (own, beside, across, seq_swap(after(across, w_heads), 1))

    over_seq = lambda a: lax.all_to_all(a, "seq", split_axis=0, concat_axis=0, tiled=True)
    q, k, v, c, lse, vt = forward(info, ranges, xs, segments, w_heads)
    kept = (q, k, v, lse)
    contexts = over_seq(c)
    if fast:
        gathered = after(gathered, vt)
        y_rows, n2, w_out_full = middle(info, contexts, own, vt, gathered)
        weights_a = weights_b = [gathered]
    else:
        y_rows, n2 = middle(info, contexts, own, vt, w_out_full)
        weights_a, weights_b = [*chunks[0], *chunks[1]], [*chunks[2], *chunks[3]]

    dz = cotangent.reshape(micros * tokens, width)
    za, dna, g0, g1, bias_a = mlp(fast, info, 0, n2, dz, vt, weights_a, None)
    if fast:
        near_c = seq_swap(g1, 1)
        near_s = add(g0[:, 1], near_c[:, 1])
        near_y = y_swap(near_s)
        za, dna = after((za, dna), near_s)
    zb, dnb, g2, g3, bias_b = mlp(fast, info, 2, n2, dz, vt, weights_b, (za, dna))
    if fast:
        far_c = seq_swap(g3, 1)

    results, dy_a, da_a, d_a, sums_a = turn(info, 0, 1, micros, y_rows, zb, dnb, dz, w_out_full, vt, None)
    d_a = over_seq(d_a)
    if fast:
        far_c = after(far_c, da_a)
        far_s = [add(g2[n, 1], far_c[n, 1]) for n in range(2)]
        far_y = [y_swap(a) for a in far_s]
        zb, dnb = after((zb, dnb), *far_s)
    results, dy_b, da_b, d_b, sums_b = turn(
        info, 1, micros - 1, micros, y_rows, zb, dnb, dz, w_out_full, vt, results
    )
    d_b = over_seq(d_b)
    d_first = (d_a, near_y) if fast else (d_a,)
    out_grads = outproj_grad(fast, info, after(contexts, *d_first), (da_a, da_b), nz, rows)
    carried = None
    grad_rows = None
    gate = ()
    if fast:
        groups_z = [list(range(n, nf, 2)) for n in range(2)]
        over_z = lambda a: lax.all_to_all(
            a, "fsdp", split_axis=0, concat_axis=0, tiled=True, axis_index_groups=groups_z
        )
        far_sum = lambda n: add(g2[n, 0], far_c[n, 0], far_y[n])
        own_sum = lambda n: add(g0[n, 0], near_c[n, 0], near_y[n], far_x[n])
        keep, keep_other, to_core = out_grads
        out_c = seq_swap(to_core, 1)
        far_h = far_sum(0)
        far_x = [seq_swap(far_h, 2)]
        gate = (keep, far_h)
    for m in range(micros):
        if fast and m == 1:
            far_y[1], out_c, far_x[0] = after((far_y[1], out_c, far_x[0]), dn0)
            far_h = far_sum(1)
            far_x.append(seq_swap(far_h, 2))
            out_s = add(keep_other, out_c[1])
            out_y = y_swap(out_s)
            up_h = own_sum(0)
            up_z = over_z(up_h)
            gate = (far_h, out_s, up_h)
        if fast and m == 2:
            far_x[1], out_y = after((far_x[1], out_y), dn0)
            rest_h = jnp.concatenate([own_sum(1), add(keep, out_c[0], out_y)], axis=2)
            rest_z = over_z(rest_h)
            gate = (rest_h,)
        d, d_at = (d_a, 0) if m == 0 else (d_b, m - 1)
        last = m == micros - 1
        packed = shape((nf, rows, 3 * hw + 64)) if fast else shape((width, 3 * hw + 64), F32)
        ends = (sums_a, sums_b, bias_a, bias_b, packed) if last else ()
        acc, sums, dn0, dn2, dn13 = backward(
            info, ranges, m, d, d_at, c, xs, kept, segments, after(w_heads, *gate), vt, carried, ends
        )
        carried = (acc, sums)
        got = seq_swap(dn13, 1)
        theirs = seq_swap(add(dn2, got[tokens:]), 2)
        dy, dy_at = (dy_a, 0) if m == 0 else (dy_b, m - 1)
        grad_rows = finish(m, dn0, got, theirs, dy, dy_at, own, vt, grad_rows)

    if fast:
        qkv_z = lax.all_to_all(acc, "fsdp", split_axis=0, concat_axis=0, tiled=True)
        up_z, rest_z = after((up_z, rest_z), dn0)
        total = lambda a: functools.reduce(jnp.add, [a[n].astype(F32) for n in range(nz)]).astype(BF)
        near_share = jnp.concatenate([total(up_z), total(rest_z[:, :, :width])], axis=0)
        far_share = seq_swap(near_share, 2)
        g_up, g_down = assemble_mlp(
            info, [near_share, seq_swap(near_share, 1), far_share, seq_swap(far_share, 1)], rows
        )
        qkv_z = after(qkv_z, grad_rows, g_up)
        out_z = rest_z[:, :, width:]
        heads_share = share(qkv_z, out_z)
        g_qkv, g_out, g_vec, g_bias = assemble_heads(lax.all_gather(heads_share, "seq", axis=0, tiled=False), hw)
        g_vec, g_bias = g_vec.T, g_bias.reshape(4 * part)
    else:
        total = lambda a: lax.psum(
            lax.psum_scatter(a.astype(F32), "fsdp", scatter_dimension=0, tiled=True), "seq"
        )
        head_place = lambda a: lax.dynamic_update_slice_in_dim(
            jnp.zeros((width, 3, 4, hw), F32), a.reshape(width, 3, 1, hw), at, 2
        ).reshape(width, 12 * hw)
        g_qkv = total(head_place(acc[:, : 3 * hw]))
        g_out = total(out_grads[0])
        extra = total(acc[:, 3 * hw :])
        g_vec, g_bias = extra[:, :8], extra[:, 8:12].T.reshape(4 * part)
        pairs = jnp.stack([g0, g1, g2, g3])
        order = lambda n: jnp.stack(
            [lax.dynamic_index_in_dim(pairs[:, n], at ^ s, 0, keepdims=False) for s in range(4)]
        )
        ups = order(0).reshape(4, width, nf, part).transpose(1, 2, 0, 3).reshape(width, 4 * width)
        downs = order(1).reshape(4, nf, part, width).transpose(1, 0, 2, 3).reshape(4 * width, width)
        g_up, g_down = total(ups), total(downs)
    return (
        results[:, None],
        grad_rows[:, None],
        g_qkv,
        g_out,
        g_up,
        g_down,
        g_vec,
        g_bias,
    )


def solution(mesh):
    rows = P(None, "fsdp", "seq", None)
    first = P("fsdp", None)
    in_specs = (rows, P(None, "fsdp", None), rows, first, first, first, first, first, P("fsdp"))
    out_specs = (rows, rows, first, first, first, first, first, P("fsdp"))
    return jax.shard_map(shards, mesh=mesh, in_specs=in_specs, out_specs=out_specs, check_vma=False)
```

```python
import functools
import math

import jax
import jax.numpy as jnp
from jax import lax
from jax.experimental import pallas as pl
from jax.experimental.pallas import tpu as pltpu
from jax.sharding import PartitionSpec as P

HEADS = 12
HEAD_DIM = 64
EPS = 1e-05
MASKED = -1e30
GELU_A = math.sqrt(2.0 / math.pi)
GELU_B = 0.044715
BF = jnp.bfloat16
F32 = jnp.float32
VMEM_LIMIT = 60 * 1024 * 1024


def shape(dims, dtype=BF):
    return jax.ShapeDtypeStruct(dims, dtype)


def vmem():
    return pl.BlockSpec(memory_space=pltpu.VMEM)


def smem():
    return pl.BlockSpec(memory_space=pltpu.SMEM)


def anywhere():
    return pl.BlockSpec(memory_space=pl.ANY)


def local_kernel(body, outs, name, flops=0, bytes_moved=0, exps=0, **kw):
    return pl.pallas_call(
        body,
        out_shape=outs,
        name=name,
        compiler_params=pltpu.CompilerParams(vmem_limit_bytes=VMEM_LIMIT),
        cost_estimate=pl.CostEstimate(
            flops=flops, bytes_accessed=bytes_moved, transcendentals=exps
        ),
        **kw,
    )


def mm(a, b):
    return lax.dot_general(a, b, (((1,), (0,)), ((), ())), preferred_element_type=F32)


def mm_nt(a, b):
    return lax.dot_general(a, b, (((1,), (1,)), ((), ())), preferred_element_type=F32)


def mm_tn(a, b):
    return lax.dot_general(a, b, (((0,), (0,)), ((), ())), preferred_element_type=F32)


def unit_rows(v):
    centred = v - jnp.mean(v, axis=-1, keepdims=True)
    inverse = lax.rsqrt(jnp.mean(centred * centred, axis=-1, keepdims=True) + EPS)
    return centred * inverse, inverse


def norm_back(grad, unit, inverse, gain):
    t = grad * gain
    first = jnp.mean(t, axis=-1, keepdims=True)
    second = jnp.mean(t * unit, axis=-1, keepdims=True)
    return inverse * (t - first - unit * second)


def pick(at, options):
    out = options[0]
    for s in range(1, len(options)):
        out = jnp.where(at == s, options[s], out)
    return out


def column_of(row, rows):
    return jnp.broadcast_to(row, (128, rows)).T[:, 0:1]


def prep_body(info_ref, wq_ref, wo_ref, up_ref, down_ref, vec_ref, bias_ref, qkv_ref, mlp_ref):
    rows = wq_ref.shape[0]
    width = up_ref.shape[1] // 4
    hw = wq_ref.shape[1] // 12
    part = down_ref.shape[0] // 4
    for s in range(4):

        @pl.when(info_ref[0] == s)
        def _(s=s):
            for n in range(3):
                base = n * 4 * hw + s * hw
                qkv_ref[:, n * hw : (n + 1) * hw] = wq_ref[:, base : base + hw]
            for i in range(width // part):
                col = i * 4 * part + s * part
                mlp_ref[0:rows, i * part : (i + 1) * part] = up_ref[:, col : col + part]
            mlp_ref[rows : rows + part, :] = down_ref[s * part : (s + 1) * part, :]
            third = rows // 3
            mlp_ref[rows + part :, :] = wo_ref[s % 3 * third : (s % 3 + 1) * third, :]

    lines = jnp.concatenate([vec_ref[...].astype(F32), bias_ref[...].astype(F32)], axis=0)
    lines = jnp.concatenate([lines, jnp.zeros((128 - lines.shape[0], rows), F32)], axis=0)
    qkv_ref[:, 3 * hw : 3 * hw + 64] = lines.T[:, 0:64].astype(BF)


def windows(segments, block):
    length = segments.shape[-1]
    first, last = segments[:, ::block, None], segments[:, block - 1 :: block, None]
    low = jnp.sum(segments[:, None, :] < first, axis=-1)
    high = jnp.sum(segments[:, None, :] <= last, axis=-1)
    low = low // 128 * 128
    count = (high - low + block - 1) // block
    start = jnp.minimum(low, length - count * block)
    return jnp.stack([start, count], axis=-1).astype(jnp.int32).reshape(-1)


def for_window(ranges_ref, at, block, body):
    start = pl.multiple_of(ranges_ref[2 * at], 128)
    for size in range(1, 5):

        @pl.when(ranges_ref[2 * at + 1] == size)
        def _(size=size):
            body(pl.ds(start, size * block))


def heads_apart(rows, heads):
    lane_head = lax.broadcasted_iota(jnp.int32, (1, rows.shape[1]), 1) // HEAD_DIM
    return jnp.concatenate([jnp.where(lane_head == h, rows, 0).astype(BF) for h in range(heads)], axis=0)


def own_blocks(wide, heads):
    width = wide.shape[1] // heads
    return [
        wide[h * HEAD_DIM : (h + 1) * HEAD_DIM, h * width : (h + 1) * width] for h in range(heads)
    ]


def picked(array, at):
    if array.ndim == 2:
        return pl.BlockSpec(array.shape, lambda i: (0, 0))
    return pl.BlockSpec((None,) + array.shape[1:], lambda i: (at,) + (0,) * (array.ndim - 1))


def whole(dims):
    return pl.BlockSpec(dims, lambda i: (0,) * len(dims))


def forward_body(info_ref, ranges_ref, x0, x1, x2, x3, seg_ref, w_ref, *refs):
    q_ref, k_ref, v_ref, c_ref, lse_ref, vt_ref, n1_ref, vtr_ref, seg_s = refs
    at = info_ref[0]
    micro = pl.program_id(0)
    tokens, width = x0.shape
    hw = q_ref.shape[1]
    heads = hw // HEAD_DIM
    tail = (3 * hw) // 128 * 128
    off = 3 * hw - tail
    vt_ref[...] = w_ref[:, tail : tail + 128].astype(F32).T[off : off + 16]
    g1, s1 = vt_ref[0:1, :], vt_ref[1:2, :]
    bq = pick(at, [vt_ref[2:3, s * hw : (s + 1) * hw] for s in range(4)])
    bv = pick(at, [vt_ref[3:4, s * hw : (s + 1) * hw] for s in range(4)])
    seg_s[...] = jnp.broadcast_to(seg_ref[...].astype(F32), (128, seg_ref.shape[1])).T
    for k, x_ref in enumerate((x0, x1, x2, x3)):
        unit, _ = unit_rows(x_ref[...].astype(F32))
        n1_ref[pl.ds(pl.multiple_of((at ^ k) * tokens, 128), tokens), :] = (unit * g1 + s1).astype(BF)
    project = mm(n1_ref[...], w_ref[:, : 3 * hw])
    q_ref[...] = ((project[:, :hw] + bq) * 0.125).astype(BF)
    keys = project[:, hw : 2 * hw]
    k_ref[...] = keys.astype(BF)
    values = project[:, 2 * hw : 3 * hw] + bv
    v_ref[...] = values.astype(BF)
    vtr_ref[...] = values.T.astype(BF)
    lse_ref[...] = jnp.zeros(lse_ref.shape, F32)

    def block(b, carry):
        rows = pl.ds(pl.multiple_of(b * tokens, 128), tokens)
        queries = heads_apart(q_ref[rows, :], heads)
        seg_row = seg_ref[0:1, rows].astype(F32)

        def body(span):
            bias = jnp.where(seg_s[span, 0:1] == seg_row, 0.0, MASKED)
            scores = mm_nt(k_ref[span, :], queries) + jnp.concatenate([bias] * heads, axis=1)
            top = jnp.max(scores, axis=0, keepdims=True)
            raised = jnp.exp(scores - top)
            total = jnp.sum(raised, axis=0, keepdims=True)
            context = mm(vtr_ref[:, span], raised.astype(BF)) * (1.0 / total)
            c_ref[b] = jnp.concatenate(own_blocks(context, heads), axis=0).astype(BF)
            log_sum = top + jnp.log(total)
            for h in range(heads):
                lse_ref[h : h + 1, rows] = log_sum[:, h * tokens : (h + 1) * tokens]

        for_window(ranges_ref, 4 * micro + b, tokens, body)
        return carry

    lax.fori_loop(0, 4, block, 0)


def quarters(array, at=None):
    dims = (array.shape[0], None) + array.shape[2:]
    return pl.BlockSpec(dims, (lambda i: (0, i, 0, 0)) if at is None else (lambda i: (0, at, 0, 0)))


def forward(info, ranges, xs, seg, w):
    micros, tokens, width = xs[0].shape
    hw = width // 4
    length = 4 * tokens
    outs = (
        shape((micros, length, hw)),
        shape((micros, length, hw)),
        shape((micros, length, hw)),
        shape((4, micros, hw, tokens)),
        shape((micros, 8, length), F32),
        shape((16, width), F32),
    )
    flops = micros * (2 * length * width * 3 * hw + 16 * length * length * hw)
    return local_kernel(
        forward_body, outs, "attention_forward",
        flops, micros * 4 * length * width * 2, micros * 3 * length * length,
        grid=(micros,),
        in_specs=[smem(), smem()] + [stepped(a) for a in (*xs, seg)] + [whole(w.shape)],
        out_specs=tuple(quarters(o) if n == 3 else stepped(o) for n, o in enumerate(outs)),
        scratch_shapes=[
            pltpu.VMEM((length, width), BF),
            pltpu.VMEM((hw, length), BF),
            pltpu.VMEM((length, 128), F32),
        ],
    )(info, ranges, *xs, seg, w)


def stepped(array, start=0):
    if array.ndim == 2:
        return whole(array.shape)
    return pl.BlockSpec((None,) + array.shape[1:], lambda i: (start + i,) + (0,) * (array.ndim - 1))


def middle_body(halves, info_ref, c_ref, x_ref, vt_ref, *refs):
    if halves:
        src, y_ref, n2_ref, w_ref, sem = refs

        @pl.when(pl.program_id(0) == 0)
        def _():
            pieces = w_ref.shape[0] * 4 // src.shape[0]
            part = pieces // 3
            base = src.shape[1] - part
            copies = [
                pltpu.make_async_copy(
                    src.at[4 * i + s, pl.ds(base, part), :],
                    w_ref.at[pl.ds(i * pieces + s * part, part), :],
                    sem.at[3 * i + s],
                )
                for i in range(src.shape[0] // 4)
                for s in range(3)
            ]
            for c in copies:
                c.start()
            for c in copies:
                c.wait()
    else:
        w_ref, y_ref, n2_ref = refs
    context = c_ref[...].reshape(w_ref.shape[0], c_ref.shape[2])
    y = x_ref[...].astype(F32) + vt_ref[4:5, :] + mm_tn(context, w_ref[...])
    y_ref[...] = y
    unit, _ = unit_rows(y)
    n2_ref[...] = (unit * vt_ref[5:6, :] + vt_ref[6:7, :]).astype(BF)


def middle(info, c, inputs, vt, w):
    micros, tokens, width = inputs.shape
    halves = w.ndim == 3
    outs = (shape((micros * tokens, width), F32), shape((micros * tokens, width)))
    outs += (shape((width, width)),) if halves else ()
    rows = pl.BlockSpec((tokens, width), lambda i: (i, 0))
    return local_kernel(
        functools.partial(middle_body, halves), outs, "middle",
        2 * micros * tokens * width * width, 12 * micros * tokens * width, 0,
        grid=(micros,),
        in_specs=[smem(), quarters(c), stepped(inputs), whole(vt.shape), anywhere() if halves else whole(w.shape)],
        out_specs=(rows, rows) + ((whole((width, width)),) if halves else ()),
        scratch_shapes=[pltpu.SemaphoreType.DMA((w.shape[0],))] if halves else [],
    )(info, c, inputs, vt, w)


def mlp_body(fast, first, lead, info_ref, *refs):
    refs = list(refs)
    take = lambda n: [refs.pop(0) for _ in range(n)]
    n2_ref, dz_ref, vt_ref = take(3)
    weights = take(1 if fast else 4)
    z_in, dn_in = (None, None) if first else take(2)
    z_ref, dn_ref = take(2)
    sides = 2 if fast else 1
    grads = take(2 * sides)
    (bias_ref,) = take(1)
    wu_s, wd_s, n2t_s, g_s, sem_w, sem_g = take(6)
    if not first:
        za_s, dna_s, sem_a = take(3)
        carried = [
            pltpu.make_async_copy(z_in, za_s, sem_a.at[0]),
            pltpu.make_async_copy(dn_in, dna_s, sem_a.at[1]),
        ]
    step = pl.program_id(0)
    width = n2_ref.shape[1]
    y = info_ref[1]
    results = [
        pltpu.make_async_copy(g_s.at[n // sides, n % sides], grads[n], sem_g.at[n]) for n in range(2 * sides)
    ]

    @pl.when(step == 0)
    def _():
        for ch in range(2):
            if fast:
                src = weights[0]
                count = src.shape[0] // 4
                rank = info_ref[0] ^ (lead + ch)
                rows = width // count
                for i in range(count):
                    for n, dest in enumerate((wu_s, wd_s)):
                        pltpu.make_async_copy(
                            src.at[4 * i + rank, pl.ds(n * rows, rows), :],
                            dest.at[ch, pl.ds(i * rows, rows), :],
                            sem_w.at[2 * ch + n],
                        ).start()
            else:
                for n, dest in enumerate((wu_s, wd_s)):
                    pltpu.make_async_copy(weights[2 * ch + n], dest.at[ch], sem_w.at[2 * ch + n]).start()
        if not first:
            for c in carried:
                c.start()
        n2t_s[...] = n2_ref[...].T
        bias_ref[...] = jnp.zeros(bias_ref.shape, F32)

    for n, dest in enumerate((wu_s, wd_s)):
        pltpu.make_async_copy(dest.at[step], dest.at[step], sem_w.at[2 * step + n]).wait()
    wu, wd = wu_s[step], wd_s[step]
    bias = vt_ref[pl.ds(8 + (info_ref[0] ^ (lead + step)), 1), :]
    u = mm(n2_ref[...], wu) + bias
    square = u * u
    t = jnp.tanh(GELU_A * u * (1.0 + GELU_B * square))
    f = (0.5 * u * (1.0 + t)).astype(BF)
    slope = 0.5 * (1.0 + t) + (0.5 * GELU_A) * u * (1.0 - t * t) * (1.0 + 3.0 * GELU_B * square)
    dz = dz_ref[...]
    du = (mm_nt(dz, wd) * slope).astype(BF)
    bias_ref[pl.ds(step, 1), :] = jnp.sum(du.astype(F32), axis=0, keepdims=True)
    grad_up = mm(n2t_s[...], du).astype(BF)
    grad_down = mm_tn(f, dz).astype(BF)
    if fast:
        count = 2 * g_s.shape[2]
        rows = width // count
        for yy in range(2):

            @pl.when(y == yy)
            def _(yy=yy):
                for i in range(count):
                    g_s[step, int(i % 2 != yy), i // 2, 0] = grad_up[i * rows : (i + 1) * rows]
                    g_s[step, int(i % 2 != yy), i // 2, 1] = grad_down[i * rows : (i + 1) * rows]
    else:
        g_s[step, 0, 0] = grad_up
        g_s[step, 0, 1] = grad_down
    for ch in range(2):

        @pl.when(step == ch)
        def _(ch=ch):
            for r in results[ch * sides : (ch + 1) * sides]:
                r.start()

    z, dn = mm(f, wd), mm_nt(du, wu)

    @pl.when(step == 0)
    def _():
        z_ref[...] = z
        dn_ref[...] = dn

    @pl.when(step == 1)
    def _():
        if first:
            z_ref[...] += z
            dn_ref[...] += dn
        else:
            for c in carried:
                c.wait()
            z_ref[...] += z + za_s[...]
            dn_ref[...] += dn + dna_s[...]
        for r in results:
            r.wait()


def mlp(fast, info, lead, n2, dz, vt, weights, carried):
    first = carried is None
    tokens, width = dz.shape
    acc = shape((tokens, width), F32)
    nf = weights[0].shape[0] // 4
    sides, one = (2, (nf // 2, 2, width // nf, width)) if fast else (1, (2, width, width))
    outs = (acc, acc, *(shape(one),) * (2 * sides), shape((8, width), F32))
    ins = (info, n2, dz, vt, *weights, *(() if first else carried))
    specs = [smem()] + [whole(a.shape) for a in (n2, dz, vt)] + [anywhere()] * len(weights)
    specs += [] if first else [anywhere()] * 2
    more = [] if first else [
        pltpu.VMEM((tokens, width), F32),
        pltpu.VMEM((tokens, width), F32),
        pltpu.SemaphoreType.DMA((2,)),
    ]
    return local_kernel(
        functools.partial(mlp_body, fast, first, lead), outs, "feed_forward",
        24 * tokens * width * width, 30 * tokens * width, 2 * tokens * width,
        grid=(2,),
        in_specs=specs,
        out_specs=(whole(acc.shape),) * 2 + (anywhere(),) * (2 * sides) + (whole((8, width)),),
        scratch_shapes=[
            pltpu.VMEM((2, width, width), BF),
            pltpu.VMEM((2, width, width), BF),
            pltpu.VMEM((width, tokens), BF),
            pltpu.VMEM((2, sides) + one, BF),
            pltpu.SemaphoreType.DMA((4,)),
            pltpu.SemaphoreType.DMA((2 * sides,)),
            *more,
        ],
    )(*ins)


def turn_body(chained, info_ref, y_ref, z_ref, dn_ref, dz_ref, w_ref, vt_ref, *refs):
    result_ref, dy_ref, da_ref, d_ref, sums_ref = refs[1:] if chained else refs
    y = y_ref[...]
    result_ref[...] = (y + z_ref[...] + vt_ref[7:8, :]).astype(BF)
    unit, inverse = unit_rows(y)
    dz = dz_ref[...].astype(F32)
    dn = dn_ref[...]
    dy = dz + norm_back(dn, unit, inverse, vt_ref[5:6, :])
    dy_ref[...] = dy
    da = dy.astype(BF)
    da_ref[...] = da
    d_ref[...] = mm_nt(w_ref[...], da).astype(BF).reshape(d_ref.shape)
    total = lambda a: jnp.sum(a, axis=0, keepdims=True)
    rest = jnp.zeros((4, y.shape[1]), F32)
    sums = jnp.concatenate([total(da.astype(F32)), total(dn * unit), total(dn), total(dz), rest], axis=0)

    @pl.when(pl.program_id(0) == 0)
    def _():
        sums_ref[...] = sums

    @pl.when(pl.program_id(0) > 0)
    def _():
        sums_ref[...] += sums


def turn(info, start, count, micros, y, z, dn, dz, w_out, vt, results):
    width = dz.shape[1]
    tokens = dz.shape[0] // micros
    hw = width // 4
    block = pl.BlockSpec((tokens, width), lambda i: (start + i, 0))
    rows = pl.BlockSpec((tokens, width), lambda i: (i, 0))
    outs = (
        shape((micros, tokens, width)),
        shape((count * tokens, width), F32),
        shape((count * tokens, width)),
        shape((4, count, hw, tokens)),
        shape((8, width), F32),
    )
    chained = results is not None
    return local_kernel(
        functools.partial(turn_body, chained), outs, "turn",
        2 * count * tokens * width, 2 * count * tokens, 0,
        grid=(count,),
        in_specs=[smem(), block, block, block, block, whole(w_out.shape), whole(vt.shape)]
        + ([anywhere()] if chained else []),
        out_specs=(stepped(outs[0], start), rows, rows, quarters(outs[3]), whole((8, width))),
        input_output_aliases={7: 0} if chained else {},
    )(info, y, z, dn, dz, w_out, vt, *((results,) if chained else ()))


def outproj_body(fast, info_ref, c_ref, *refs):
    outs, scratch = refs[:-1][-3 if fast else -1 :], refs[-1]
    das = refs[: -4 if fast else -2]
    at, y = info_ref[0], info_ref[1]
    da = jnp.concatenate([d[...] for d in das], axis=0)
    rows, micros = scratch.shape[0], c_ref.shape[1]
    left = jnp.concatenate([c_ref[:, m].reshape(rows, c_ref.shape[3]) for m in range(micros)], axis=1)
    scratch[...] = mm(left, da)
    if not fast:
        outs[0][...] = scratch[...]
        return
    keep, keep_other, send = outs
    nz, part, half = keep.shape
    first = lax.rem(at, 2) == 0
    for z in range(nz):
        for n in range(2):
            i = 2 * z + (y if n == 0 else 1 - y)
            block = scratch[pl.ds(pl.multiple_of(i * part, 16), part), :].astype(BF)
            left, right = block[:, :half], block[:, half:]
            (keep, keep_other)[n][z] = jnp.where(first, left, right)
            send[n, z] = jnp.where(first, right, left)


def outproj_grad(fast, info, c, das, nz, part):
    width = das[0].shape[1]
    total = sum(d.shape[0] for d in das)
    if fast:
        one = shape((nz, part, width // 2))
        outs = (one, one, shape((2, nz, part, width // 2)))
    else:
        outs = (shape((width, width), F32),)
    return local_kernel(
        functools.partial(outproj_body, fast), outs, "outproj_grad",
        2 * total * width * width, 6 * width * width, 0,
        in_specs=[smem()] + [vmem()] * (1 + len(das)),
        out_specs=(vmem(),) * len(outs),
        scratch_shapes=[pltpu.VMEM((width, width), F32)],
    )(info, c, *das)


def backward_body(first, last, micro, info_ref, ranges_ref, *refs):
    refs = list(refs)
    take = lambda n: [refs.pop(0) for _ in range(n)]
    d_ref, c_ref = take(2)
    xs = take(4)
    q_ref, k_ref, v_ref, lse_ref, seg_ref, w_ref, vt_ref = take(7)
    acc_in, sums_in = (None, None) if first else take(2)
    turned, biases = (take(2), take(2)) if last else ((), ())
    acc_ref, sums_ref, dn0_ref, dn2_ref, dn13_ref = take(5)
    dk_s, dv_s, dp_s, seg_s, dc_s, delta_s, kt_s, n1_s, unit_s = take(9)
    at = info_ref[0]
    _, hw, tokens = d_ref.shape
    heads = hw // HEAD_DIM
    seg_s[...] = jnp.broadcast_to(seg_ref[...].astype(F32), (128, seg_ref.shape[1])).T
    dk_s[...] = jnp.zeros(dk_s.shape, F32)
    dv_s[...] = jnp.zeros(dv_s.shape, F32)
    kt_s[...] = k_ref[...].astype(F32).T.astype(BF)
    for b in range(4):
        dct = d_ref[b].astype(F32)
        dc_s[b] = dct.T.astype(BF)
        product = dct * c_ref[b].astype(F32)
        for h in range(heads):
            delta_s[b, h : h + 1, :] = jnp.sum(product[h * HEAD_DIM : (h + 1) * HEAD_DIM], axis=0, keepdims=True)
    for k in range(4):
        rows = pl.ds(pl.multiple_of((at ^ k) * tokens, 128), tokens)
        unit, _ = unit_rows(xs[k][...].astype(F32))
        unit_s[rows, :] = unit
        n1_s[rows, :] = (unit * vt_ref[0:1, :] + vt_ref[1:2, :]).astype(BF)

    def block(b, carry):
        rows = pl.ds(pl.multiple_of(b * tokens, 128), tokens)
        queries = heads_apart(q_ref[rows, :], heads)
        contexts = heads_apart(dc_s[b], heads)
        seg_row = seg_ref[0:1, rows].astype(F32)
        log_sum = jnp.concatenate([lse_ref[h : h + 1, rows] for h in range(heads)], axis=1)
        delta = jnp.concatenate([delta_s[b, h : h + 1, :] for h in range(heads)], axis=1)

        def body(span):
            bias = jnp.where(seg_s[span, 0:1] == seg_row, 0.0, MASKED)
            scores = mm_nt(k_ref[span, :], queries) + jnp.concatenate([bias] * heads, axis=1)
            p = jnp.exp(scores - log_sum)
            g = (p * (mm_nt(v_ref[span, :], contexts) - delta)).astype(BF)
            dk_s[span, :] += mm(g, queries)
            dv_s[span, :] += mm(p.astype(BF), contexts)
            dq = jnp.concatenate(own_blocks(mm(kt_s[:, span], g), heads), axis=0).T.astype(BF)
            dp_s[rows, 0:hw] = (dq.astype(F32) * 0.125).astype(BF)

        for_window(ranges_ref, 4 * micro + b, tokens, body)
        return carry

    lax.fori_loop(0, 4, block, 0)
    dp_s[:, hw : 2 * hw] = dk_s[...].astype(BF)
    dp_s[:, 2 * hw : 3 * hw] = dv_s[...].astype(BF)
    total = lambda a: jnp.sum(a, axis=0, keepdims=True)
    acc = mm_tn(n1_s[...], dp_s[...])
    acc = acc if first else acc_in[...] + acc
    dg1 = ds1 = None
    outs = ((dn0_ref, 0), (dn13_ref, 0), (dn2_ref, 0), (dn13_ref, tokens))
    for k in range(4):
        rows = pl.ds(pl.multiple_of((at ^ k) * tokens, 128), tokens)
        dn1 = mm_nt(dp_s[rows, :], w_ref[:, : 3 * hw])
        a, b = total(dn1 * unit_s[rows, :]), total(dn1)
        dg1, ds1 = (a, b) if k == 0 else (dg1 + a, ds1 + b)
        ref, base = outs[k]
        ref[base : base + tokens, :] = dn1.astype(BF)
    dbq, dbv = (total(dp_s[:, n * hw : (n + 1) * hw].astype(F32)) for n in (0, 2))
    spread = lambda r: jnp.concatenate([jnp.where(at == s, r, 0.0) for s in range(4)], axis=1)
    sums = jnp.concatenate([dg1, ds1, spread(dbq), spread(dbv), jnp.zeros((4, dg1.shape[1]), F32)], axis=0)
    sums = sums if first else sums_in[...] + sums
    sums_ref[...] = sums
    if not last:
        acc_ref[...] = acc
        return
    width = acc.shape[0]
    rest = turned[0][...] + turned[1][...]
    chunk_rows = [biases[k // 2][k % 2 : k % 2 + 1, :] for k in range(4)]
    lines = [sums[0:4], rest[0:4]] + [pick(at ^ s, chunk_rows) for s in range(4)]
    lines = jnp.concatenate(lines + [jnp.zeros((116, width), F32)], axis=0)
    full = jnp.concatenate([acc, lines.T[:, 0:64]], axis=1)
    acc_ref[...] = full.astype(acc_ref.dtype).reshape(acc_ref.shape)


def backward(info, ranges, micro, d, d_at, c, xs, kept, seg, w, vt, carried, ends):
    q, k, v, lse = kept
    hw, tokens = d.shape[2:]
    length, width = k.shape[1], w.shape[0]
    first, last = carried is None, bool(ends)
    outs = (
        ends[-1] if last else shape((width, 3 * hw), F32),
        shape((8, width), F32),
        shape((tokens, width)),
        shape((tokens, width)),
        shape((2 * tokens, width)),
    )
    rest = (w, vt, *(() if first else carried), *ends[:-1])
    stacked = (*xs, q, k, v, lse, seg)
    specs = [smem(), smem(), quarters(d, d_at), quarters(c, micro)] + [picked(a, micro) for a in stacked]
    specs += [whole(a.shape) for a in rest]
    flops = 4 * length * width * 3 * hw + 40 * length * length * hw
    return local_kernel(
        functools.partial(backward_body, first, last, micro), outs, "attention_backward",
        flops, 8 * length * width * 2, 3 * length * length,
        grid=(1,),
        in_specs=specs,
        out_specs=tuple(whole(o.shape) for o in outs),
        scratch_shapes=[
            pltpu.VMEM((length, hw), F32),
            pltpu.VMEM((length, hw), F32),
            pltpu.VMEM((length, 3 * hw), BF),
            pltpu.VMEM((length, 128), F32),
            pltpu.VMEM((4, tokens, hw), BF),
            pltpu.VMEM((4, 8, tokens), F32),
            pltpu.VMEM((hw, length), BF),
            pltpu.VMEM((length, width), BF),
            pltpu.VMEM((length, width), F32),
        ],
    )(info, ranges, d, c, *stacked, *rest)


def finish_body(chained, a_ref, b_ref, r_ref, dy_ref, x_ref, vt_ref, *refs):
    gx_ref = refs[-1]
    unit, inverse = unit_rows(x_ref[...].astype(F32))
    dn1 = a_ref[...].astype(F32) + b_ref[...].astype(F32) + r_ref[...].astype(F32)
    gx_ref[...] = dy_ref[...] + norm_back(dn1, unit, inverse, vt_ref[0:1, :])


def finish(micro, a, b, r, dy, dy_at, inputs, vt, grads):
    tokens, width = a.shape
    chained = grads is not None
    out = shape(inputs.shape, F32)
    top = pl.BlockSpec((tokens, width), lambda i: (0, 0))
    return local_kernel(
        functools.partial(finish_body, chained), out, "finish", 20 * a.size, 14 * a.size, 0,
        grid=(1,),
        in_specs=[top, top, top, pl.BlockSpec((tokens, width), lambda i: (dy_at, 0)), picked(inputs, micro), whole(vt.shape)] + ([anywhere()] if chained else []),
        out_specs=picked(out, micro),
        input_output_aliases={6: 0} if chained else {},
    )(a, b, r, dy, inputs, vt, *((grads,) if chained else ()))


def split_body(count, info_ref, *refs):
    ins, outs = refs[:count], refs[count:]
    nz = len(outs)
    for d in range(nz):
        at = lax.rem(info_ref[2] + nz - d, nz)
        total = ins[0][at].astype(F32)
        for r in ins[1:]:
            total = total + r[at].astype(F32)
        outs[d][...] = total.astype(BF)


def split(info, terms):
    nz, *dims = terms[-1].shape
    dims = tuple(dims)

    def spec(t, at):
        block = tuple(None if a is not None else n for a, n in zip(at, t.shape))
        return pl.BlockSpec(block, lambda i: tuple(0 if a is None else a for a in at))

    pairs = [t if isinstance(t, tuple) else (t, (None,) * t.ndim) for t in terms]
    return local_kernel(
        functools.partial(split_body, len(terms)), (shape(dims),) * nz, "split",
        0, 2 * (len(terms) + 1) * nz * math.prod(dims), 0,
        grid=(1,),
        in_specs=[smem()] + [spec(t, at) for t, at in pairs],
        out_specs=(whole(dims),) * nz,
    )(info, *(t for t, _ in pairs))


def collect_body(count, *refs):
    up, down, out = refs[:count], refs[count : 2 * count], refs[-1]
    total = lambda rs: functools.reduce(jnp.add, [r[...].astype(F32) for r in rs]).astype(BF)
    rows = up[0].shape[0]
    out[:rows] = total(up)
    out[rows:] = total(down)


def collect(ups, downs):
    rows, width = ups[0].shape
    return local_kernel(
        functools.partial(collect_body, len(ups)), shape((2 * rows, width)), "collect",
        0, 20 * rows * width, 0,
        in_specs=[vmem()] * (2 * len(ups)),
        out_specs=vmem(),
    )(*ups, *downs)


def assemble_mlp_body(info_ref, *refs):
    ms, (gu_ref, gd_ref, all_s) = refs[:-3], refs[-3:]
    at = info_ref[0]
    for k, r in enumerate(ms):
        all_s[at ^ k] = r[...]
    rows, part = gu_ref.shape[0], gd_ref.shape[0] // 4
    for s in range(4):
        up = all_s[s, 0:rows, :].astype(F32)
        for i in range(up.shape[1] // part):
            col = i * 4 * part + s * part
            gu_ref[:, col : col + part] = up[:, i * part : (i + 1) * part]
        gd_ref[s * part : (s + 1) * part, :] = all_s[s, rows : rows + part, :].astype(F32)


def assemble_mlp(info, ms, rows):
    width = ms[0].shape[1]
    part = ms[0].shape[0] - rows
    outs = (shape((rows, 4 * width), F32), shape((4 * part, width), F32))
    return local_kernel(
        assemble_mlp_body, outs, "assemble_mlp", 0, 12 * rows * width * 4, 0,
        in_specs=[smem()] + [vmem()] * 4,
        out_specs=(vmem(),) * 2,
        scratch_shapes=[pltpu.VMEM((4,) + ms[0].shape, BF)],
    )(info, *ms)


def share_body(q_ref, o_ref, out_ref):
    total = lambda r: functools.reduce(jnp.add, [r[n].astype(F32) for n in range(r.shape[0])])
    out_ref[...] = jnp.concatenate([total(q_ref), total(o_ref)], axis=1).astype(BF)


def share(q, o):
    return local_kernel(
        share_body, shape((q.shape[1], q.shape[2] + o.shape[2])), "share", 0, 2 * (q.size + o.size), 0,
        in_specs=[vmem()] * 2,
        out_specs=vmem(),
    )(q, o)


def assemble_heads_body(q_ref, gq_ref, go_ref, gv_ref, gb_ref):
    hw = gq_ref.shape[1] // 12
    half = go_ref.shape[1] // 2
    for s in range(4):
        for n in range(3):
            base = n * 4 * hw + s * hw
            gq_ref[:, base : base + hw] = q_ref[s, :, n * hw : (n + 1) * hw].astype(F32)
    for h in range(2):
        a, b = (q_ref[h + 2 * n, :, 3 * hw + 64 :].astype(F32) for n in range(2))
        go_ref[:, h * half : (h + 1) * half] = a + b
    tail = (3 * hw) // 128 * 128
    off = 3 * hw - tail
    extra = functools.reduce(jnp.add, [q_ref[s, :, tail : tail + 128].astype(F32) for s in range(4)]).T
    gv_ref[...] = extra[off : off + 8]
    gb_ref[...] = extra[off + 8 : off + 12]


def assemble_heads(q, hw):
    rows = q.shape[1]
    outs = (
        shape((rows, 12 * hw), F32),
        shape((rows, 4 * hw), F32),
        shape((8, rows), F32),
        shape((4, rows), F32),
    )
    return local_kernel(
        assemble_heads_body, outs, "assemble_heads", 0, 12 * rows * hw * 16, 0,
        in_specs=[vmem()],
        out_specs=(vmem(),) * 4,
    )(q)


def send(x, axis, to):
    n = lax.axis_size(axis)
    return lax.ppermute(x, axis, [(s, to(s)) for s in range(n)])


def seq_swap(x, k):
    return send(x, "seq", lambda s: s ^ k)


def add(*terms):
    out = terms[0].astype(F32)
    for t in terms[1:]:
        out = out + t.astype(F32)
    return out.astype(BF)


def after(values, *others):
    out = lax.optimization_barrier((values, others))
    return out[0]


def shards(inputs, segments, cotangent, w_qkv, w_out, w_up, w_down, vectors, bias_up):
    micros, _, tokens, width = inputs.shape
    nf = lax.axis_size("fsdp")
    assert lax.axis_size("seq") == 4 and inputs.shape[1] == 1
    rows = w_qkv.shape[0]
    part = w_down.shape[0] // 4
    hw = width // 4
    nz = nf // 2
    fast = nf == 8 and rows % 32 == 0 and part == rows
    at = lax.axis_index("seq")
    me = lax.axis_index("fsdp")
    z, y = me // 2, me % 2
    info = jnp.stack([at, y, z]).astype(jnp.int32)
    y_swap = lambda x: send(x, "fsdp", lambda s: s ^ 1)
    z_pull = lambda x, d: send(x, "fsdp", lambda s: (s - 2 * d) % nf)
    pulled = lambda x: [x] + [z_pull(x, d) for d in range(1, nz)]

    ranges = windows(segments[:, 0], tokens)

    own = inputs[:, 0]
    across = seq_swap(own, 2)
    beside = seq_swap(own, 1)

    if fast:
        qkv_piece, mlp_piece = local_kernel(
            prep_body,
            (shape((rows, 3 * hw + 64)), shape((rows + part + rows // 3, width))),
            "prep", 0, 6 * rows * 4 * width, 0,
            in_specs=[smem()] + [vmem()] * 6,
            out_specs=(vmem(),) * 2,
        )(info, w_qkv, w_out, w_up, w_down, vectors.T, bias_up.reshape(4, part))
        w_heads = lax.all_gather(qkv_piece, "fsdp", axis=0, tiled=True)
        gathered = lax.all_gather(mlp_piece, ("fsdp", "seq"), axis=0, tiled=False)
    else:
        gather = lambda a: lax.all_gather(a, "fsdp", axis=0, tiled=True)
        by_head = gather(w_qkv).reshape(width, 3, 4, hw)
        mine = lax.dynamic_index_in_dim(by_head, at, 2, keepdims=False).reshape(width, 3 * hw)
        biases = gather(bias_up).reshape(nf, 4, part).transpose(0, 2, 1).reshape(width, 4)
        w_heads = jnp.concatenate([mine, gather(vectors), biases, jnp.zeros((width, 52), BF)], axis=1)
        w_out_full = gather(w_out)
        ups = gather(w_up).reshape(width, nf, 4, part).transpose(2, 0, 1, 3).reshape(4, width, width)
        downs = gather(w_down).reshape(nf, 4, part, width).transpose(1, 0, 2, 3).reshape(4, width, width)
        one = lambda a, k: lax.dynamic_index_in_dim(a, at ^ k, 0, keepdims=False)
        chunks = [(one(ups, k), one(downs, k)) for k in range(4)]

    xs = (own, beside, across, seq_swap(after(across, w_heads), 1))

    over_seq = lambda a: lax.all_to_all(a, "seq", split_axis=0, concat_axis=0, tiled=True)
    q, k, v, c, lse, vt = forward(info, ranges, xs, segments, w_heads)
    kept = (q, k, v, lse)
    contexts = over_seq(c)
    if fast:
        gathered = after(gathered, vt)
        y_rows, n2, w_out_full = middle(info, contexts, own, vt, gathered)
        weights_a = weights_b = [gathered]
    else:
        y_rows, n2 = middle(info, contexts, own, vt, w_out_full)
        weights_a, weights_b = [*chunks[0], *chunks[1]], [*chunks[2], *chunks[3]]

    dz = cotangent.reshape(micros * tokens, width)
    za, dna, *near_g, bias_a = mlp(fast, info, 0, n2, dz, vt, weights_a, None)
    if fast:
        near_own, near_oth = (seq_swap(a, 1) for a in near_g[2:])
        near_s = add(near_g[1], near_oth)
        near_y = y_swap(near_s)
        za, dna = after((za, dna), near_s)
    zb, dnb, *far_g, bias_b = mlp(fast, info, 2, n2, dz, vt, weights_b, (za, dna))

    results, dy_a, da_a, d_a, sums_a = turn(info, 0, 1, micros, y_rows, zb, dnb, dz, w_out_full, vt, None)
    d_a = over_seq(d_a)
    if fast:
        zb, dnb = after((zb, dnb), near_y)
    results, dy_b, da_b, d_b, sums_b = turn(
        info, 1, micros - 1, micros, y_rows, zb, dnb, dz, w_out_full, vt, results
    )
    d_b = over_seq(d_b)
    if fast:
        far_own, far_oth = (seq_swap(after(a, da_b), 1) for a in far_g[2:])
        over_near = lambda parts: [parts[0]] + [z_pull(parts[d], d) for d in range(1, nz)]
        half = lambda a, n: (a, (None, n, None, None))
        near_z = over_near(split(info, [near_g[0], near_own, near_y]))
        contexts = after(contexts, near_z[0])
    out_grads = outproj_grad(fast, info, contexts, (da_a, da_b), nz, rows)
    carried = None
    pending, settled = [], []

    def settle(m, own_part, across_part, got, later):
        if later is not None:
            got = after(got, later)
        total = add(across_part, got[tokens:])
        settled.append((m, own_part, got, seq_swap(total, 2)))
        return total

    gate = ()
    if fast:
        groups_z = [list(range(n, nf, 2)) for n in range(2)]
        over_z = lambda a: lax.all_to_all(
            a, "fsdp", split_axis=0, concat_axis=0, tiled=True, axis_index_groups=groups_z
        )
        keep, keep_other, to_core = out_grads
        out_c = seq_swap(to_core, 1)
        far_own, far_oth = after((far_own, far_oth), keep)
        far_s = [add(far_g[1][:, n], far_oth[:, n]) for n in range(2)]
        far_y = [y_swap(a) for a in far_s]
        gate = (keep, *far_s)
    for m in range(micros):
        if fast and m == 1:
            far_y[0], out_c, near_z = after((far_y[0], out_c, near_z), dn0)
            out_s = add(keep_other, out_c[1])
            out_y = y_swap(out_s)
            far_z = [over_near(split(info, [half(far_g[0], 0), half(far_own, 0), far_y[0]]))]
            gate = (far_z[0][0], out_s)
        if fast and m == 2:
            out_y, far_y[1], far_z[0], near_z = after((out_y, far_y[1], far_z[0], near_z), dn0)
            far_z.append(over_near(split(info, [half(far_g[0], 1), half(far_own, 1), far_y[1]])))
            out_h = add(keep, out_c[0], out_y)
            out_z = over_z(out_h)
            near_sum = add(*near_z).reshape(rows + part, width)
            near_x = seq_swap(near_sum, 2)
            gate = (far_z[1][0], out_h, near_sum)
        d, d_at = (d_a, 0) if m == 0 else (d_b, m - 1)
        last = m == micros - 1
        packed = shape((nf, rows, 3 * hw + 64)) if fast else shape((width, 3 * hw + 64), F32)
        ends = (sums_a, sums_b, bias_a, bias_b, packed) if last else ()
        acc, sums, dn0, dn2, dn13 = backward(
            info, ranges, m, d, d_at, c, xs, kept, segments, after(w_heads, *gate), vt, carried, ends
        )
        carried = (acc, sums)
        pending.append((m, dn0, dn2, seq_swap(dn13, 1)))
        if m > 0:
            settle(*pending.pop(0), dn0)
    if fast:
        acc = after(acc, *far_z[1][1:], settled[0][3], out_z, near_x)
    last_total = settle(*pending.pop(0), None)
    grad_rows = None
    for m, own_part, got, theirs in settled:
        dy, dy_at = (dy_a, 0) if m == 0 else (dy_b, m - 1)
        grad_rows = finish(m, own_part, got, theirs, dy, dy_at, own, vt, grad_rows)

    if fast:
        qkv_z = lax.all_to_all(acc, "fsdp", split_axis=0, concat_axis=0, tiled=True)
        far_sum = collect(*far_z)
        mine = add(near_sum, after(seq_swap(far_sum, 2), last_total))
        theirs = add(near_x, far_sum)
        g_up, g_down = assemble_mlp(info, [mine, seq_swap(mine, 1), theirs, seq_swap(theirs, 1)], rows)
        qkv_z = after(qkv_z, grad_rows)
        heads_share = share(qkv_z, out_z)
        g_qkv, g_out, g_vec, g_bias = assemble_heads(lax.all_gather(heads_share, "seq", axis=0, tiled=False), hw)
        g_vec, g_bias = g_vec.T, g_bias.reshape(4 * part)
    else:
        total = lambda a: lax.psum(
            lax.psum_scatter(a.astype(F32), "fsdp", scatter_dimension=0, tiled=True), "seq"
        )
        head_place = lambda a: lax.dynamic_update_slice_in_dim(
            jnp.zeros((width, 3, 4, hw), F32), a.reshape(width, 3, 1, hw), at, 2
        ).reshape(width, 12 * hw)
        g_qkv = total(head_place(acc[:, : 3 * hw]))
        g_out = total(out_grads[0])
        extra = total(acc[:, 3 * hw :])
        g_vec, g_bias = extra[:, :8], extra[:, 8:12].T.reshape(4 * part)
        pairs = jnp.stack([*near_g, *far_g])
        order = lambda n: jnp.stack(
            [lax.dynamic_index_in_dim(pairs[:, n], at ^ s, 0, keepdims=False) for s in range(4)]
        )
        ups = order(0).reshape(4, width, nf, part).transpose(1, 2, 0, 3).reshape(width, 4 * width)
        downs = order(1).reshape(4, nf, part, width).transpose(1, 0, 2, 3).reshape(4 * width, width)
        g_up, g_down = total(ups), total(downs)
    return (
        results[:, None],
        grad_rows[:, None],
        g_qkv,
        g_out,
        g_up,
        g_down,
        g_vec,
        g_bias,
    )


def solution(mesh):
    rows = P(None, "fsdp", "seq", None)
    first = P("fsdp", None)
    in_specs = (rows, P(None, "fsdp", None), rows, first, first, first, first, first, P("fsdp"))
    out_specs = (rows, rows, first, first, first, first, first, P("fsdp"))
    return jax.shard_map(shards, mesh=mesh, in_specs=in_specs, out_specs=out_specs, check_vma=False)
```

```python
import functools
import math

import jax
import jax.numpy as jnp
from jax import lax
from jax.experimental import pallas as pl
from jax.experimental.pallas import tpu as pltpu
from jax.sharding import PartitionSpec as P

HEADS = 12
HEAD_DIM = 64
EPS = 1e-05
MASKED = -1e30
GELU_A = math.sqrt(2.0 / math.pi)
GELU_B = 0.044715
BF = jnp.bfloat16
F32 = jnp.float32
VMEM_LIMIT = 60 * 1024 * 1024


def shape(dims, dtype=BF):
    return jax.ShapeDtypeStruct(dims, dtype)


def vmem():
    return pl.BlockSpec(memory_space=pltpu.VMEM)


def smem():
    return pl.BlockSpec(memory_space=pltpu.SMEM)


def anywhere():
    return pl.BlockSpec(memory_space=pl.ANY)


def local_kernel(body, outs, name, flops=0, bytes_moved=0, exps=0, **kw):
    return pl.pallas_call(
        body,
        out_shape=outs,
        name=name,
        compiler_params=pltpu.CompilerParams(vmem_limit_bytes=VMEM_LIMIT),
        cost_estimate=pl.CostEstimate(
            flops=flops, bytes_accessed=bytes_moved, transcendentals=exps
        ),
        **kw,
    )


def mm(a, b):
    return lax.dot_general(a, b, (((1,), (0,)), ((), ())), preferred_element_type=F32)


def mm_nt(a, b):
    return lax.dot_general(a, b, (((1,), (1,)), ((), ())), preferred_element_type=F32)


def mm_tn(a, b):
    return lax.dot_general(a, b, (((0,), (0,)), ((), ())), preferred_element_type=F32)


def unit_rows(v):
    centred = v - jnp.mean(v, axis=-1, keepdims=True)
    inverse = lax.rsqrt(jnp.mean(centred * centred, axis=-1, keepdims=True) + EPS)
    return centred * inverse, inverse


def norm_back(grad, unit, inverse, gain):
    t = grad * gain
    first = jnp.mean(t, axis=-1, keepdims=True)
    second = jnp.mean(t * unit, axis=-1, keepdims=True)
    return inverse * (t - first - unit * second)


def pick(at, options):
    out = options[0]
    for s in range(1, len(options)):
        out = jnp.where(at == s, options[s], out)
    return out


def column_of(row, rows):
    return jnp.broadcast_to(row, (128, rows)).T[:, 0:1]


def prep_body(info_ref, wq_ref, wo_ref, up_ref, down_ref, vec_ref, bias_ref, qkv_ref, mlp_ref, out_ref):
    rows = wq_ref.shape[0]
    width = up_ref.shape[1] // 4
    hw = wq_ref.shape[1] // 12
    part = down_ref.shape[0] // 4
    for s in range(4):

        @pl.when(info_ref[0] == s)
        def _(s=s):
            for n in range(3):
                base = n * 4 * hw + s * hw
                qkv_ref[:, n * hw : (n + 1) * hw] = wq_ref[:, base : base + hw]
            for i in range(width // part):
                col = i * 4 * part + s * part
                mlp_ref[0:rows, i * part : (i + 1) * part] = up_ref[:, col : col + part]
            mlp_ref[rows : rows + part, :] = down_ref[s * part : (s + 1) * part, :]
            for n in range(out_ref.shape[0]):
                out_ref[n] = wo_ref[s % 2 * (rows // 2) : (s % 2 + 1) * (rows // 2), :]

    lines = jnp.concatenate([vec_ref[...].astype(F32), bias_ref[...].astype(F32)], axis=0)
    lines = jnp.concatenate([lines, jnp.zeros((128 - lines.shape[0], rows), F32)], axis=0)
    qkv_ref[:, 3 * hw : 3 * hw + 64] = lines.T[:, 0:64].astype(BF)


def windows(segments, block):
    length = segments.shape[-1]
    first, last = segments[:, ::block, None], segments[:, block - 1 :: block, None]
    low = jnp.sum(segments[:, None, :] < first, axis=-1)
    high = jnp.sum(segments[:, None, :] <= last, axis=-1)
    low = low // 128 * 128
    count = (high - low + block - 1) // block
    start = jnp.minimum(low, length - count * block)
    return jnp.stack([start, count], axis=-1).astype(jnp.int32).reshape(-1)


def for_window(ranges_ref, at, block, body):
    start = pl.multiple_of(ranges_ref[2 * at], 128)
    for size in range(1, 5):

        @pl.when(ranges_ref[2 * at + 1] == size)
        def _(size=size):
            body(pl.ds(start, size * block))


def heads_apart(rows, heads):
    lane_head = lax.broadcasted_iota(jnp.int32, (1, rows.shape[1]), 1) // HEAD_DIM
    return jnp.concatenate([jnp.where(lane_head == h, rows, 0).astype(BF) for h in range(heads)], axis=0)


def own_blocks(wide, heads):
    width = wide.shape[1] // heads
    return [
        wide[h * HEAD_DIM : (h + 1) * HEAD_DIM, h * width : (h + 1) * width] for h in range(heads)
    ]


def picked(array, at):
    if array.ndim == 2:
        return pl.BlockSpec(array.shape, lambda i: (0, 0))
    return pl.BlockSpec((None,) + array.shape[1:], lambda i: (at,) + (0,) * (array.ndim - 1))


def whole(dims):
    return pl.BlockSpec(dims, lambda i: (0,) * len(dims))


def forward_body(info_ref, ranges_ref, x0, x1, x2, x3, seg_ref, w_ref, *refs):
    q_ref, k_ref, v_ref, c_ref, lse_ref, vt_ref, n1_ref, vtr_ref, seg_s = refs
    at = info_ref[0]
    micro = pl.program_id(0)
    tokens, width = x0.shape
    hw = q_ref.shape[1]
    heads = hw // HEAD_DIM
    tail = (3 * hw) // 128 * 128
    off = 3 * hw - tail
    vt_ref[...] = w_ref[:, tail : tail + 128].astype(F32).T[off : off + 16]
    g1, s1 = vt_ref[0:1, :], vt_ref[1:2, :]
    bq = pick(at, [vt_ref[2:3, s * hw : (s + 1) * hw] for s in range(4)])
    bv = pick(at, [vt_ref[3:4, s * hw : (s + 1) * hw] for s in range(4)])
    seg_s[...] = jnp.broadcast_to(seg_ref[...].astype(F32), (128, seg_ref.shape[1])).T
    for k, x_ref in enumerate((x0, x1, x2, x3)):
        unit, _ = unit_rows(x_ref[...].astype(F32))
        n1_ref[pl.ds(pl.multiple_of((at ^ k) * tokens, 128), tokens), :] = (unit * g1 + s1).astype(BF)
    project = mm(n1_ref[...], w_ref[:, : 3 * hw])
    q_ref[...] = ((project[:, :hw] + bq) * 0.125).astype(BF)
    keys = project[:, hw : 2 * hw]
    k_ref[...] = keys.astype(BF)
    values = project[:, 2 * hw : 3 * hw] + bv
    v_ref[...] = values.astype(BF)
    vtr_ref[...] = values.T.astype(BF)
    lse_ref[...] = jnp.zeros(lse_ref.shape, F32)

    def block(b, carry):
        rows = pl.ds(pl.multiple_of(b * tokens, 128), tokens)
        queries = heads_apart(q_ref[rows, :], heads)
        seg_row = seg_ref[0:1, rows].astype(F32)

        def body(span):
            bias = jnp.where(seg_s[span, 0:1] == seg_row, 0.0, MASKED)
            scores = mm_nt(k_ref[span, :], queries) + jnp.concatenate([bias] * heads, axis=1)
            top = jnp.max(scores, axis=0, keepdims=True)
            raised = jnp.exp(scores - top)
            total = jnp.sum(raised, axis=0, keepdims=True)
            context = mm(vtr_ref[:, span], raised.astype(BF)) * (1.0 / total)
            c_ref[b] = jnp.concatenate(own_blocks(context, heads), axis=0).astype(BF)
            log_sum = top + jnp.log(total)
            for h in range(heads):
                lse_ref[h : h + 1, rows] = log_sum[:, h * tokens : (h + 1) * tokens]

        for_window(ranges_ref, 4 * micro + b, tokens, body)
        return carry

    lax.fori_loop(0, 4, block, 0)


def quarters(array, at=None):
    dims = (array.shape[0], None) + array.shape[2:]
    return pl.BlockSpec(dims, (lambda i: (0, i, 0, 0)) if at is None else (lambda i: (0, at, 0, 0)))


def forward(info, ranges, xs, seg, w):
    micros, tokens, width = xs[0].shape
    hw = width // 4
    length = 4 * tokens
    outs = (
        shape((micros, length, hw)),
        shape((micros, length, hw)),
        shape((micros, length, hw)),
        shape((4, micros, hw, tokens)),
        shape((micros, 8, length), F32),
        shape((16, width), F32),
    )
    flops = micros * (2 * length * width * 3 * hw + 16 * length * length * hw)
    return local_kernel(
        forward_body, outs, "attention_forward",
        flops, micros * 4 * length * width * 2, micros * 3 * length * length,
        grid=(micros,),
        in_specs=[smem(), smem()] + [stepped(a) for a in (*xs, seg)] + [whole(w.shape)],
        out_specs=tuple(quarters(o) if n == 3 else stepped(o) for n, o in enumerate(outs)),
        scratch_shapes=[
            pltpu.VMEM((length, width), BF),
            pltpu.VMEM((hw, length), BF),
            pltpu.VMEM((length, 128), F32),
        ],
    )(info, ranges, *xs, seg, w)


def stepped(array, start=0):
    if array.ndim == 2:
        return whole(array.shape)
    return pl.BlockSpec((None,) + array.shape[1:], lambda i: (start + i,) + (0,) * (array.ndim - 1))


def middle_body(halves, info_ref, c_ref, x_ref, vt_ref, *refs):
    if halves:
        mine, theirs, y_ref, n2_ref, w_ref, sem = refs

        @pl.when(pl.program_id(0) == 0)
        def _():
            count, part = mine.shape[:2]
            core = lax.rem(info_ref[0], 2)
            copies = []
            for n, src in enumerate((mine, theirs)):
                for i in range(count):
                    dest = pl.multiple_of(i * 2 * part + (core if n == 0 else 1 - core) * part, 16)
                    copies.append(
                        pltpu.make_async_copy(src.at[i], w_ref.at[pl.ds(dest, part), :], sem.at[n * count + i])
                    )
            for c in copies:
                c.start()
            for c in copies:
                c.wait()
    else:
        w_ref, y_ref, n2_ref = refs
    context = c_ref[...].reshape(w_ref.shape[0], c_ref.shape[2])
    y = x_ref[...].astype(F32) + vt_ref[4:5, :] + mm_tn(context, w_ref[...])
    y_ref[...] = y
    unit, _ = unit_rows(y)
    n2_ref[...] = (unit * vt_ref[5:6, :] + vt_ref[6:7, :]).astype(BF)


def middle(info, c, inputs, vt, ws):
    micros, tokens, width = inputs.shape
    halves = len(ws) == 2
    outs = (shape((micros * tokens, width), F32), shape((micros * tokens, width)))
    outs += (shape((width, width)),) if halves else ()
    rows = pl.BlockSpec((tokens, width), lambda i: (i, 0))
    return local_kernel(
        functools.partial(middle_body, halves), outs, "middle",
        2 * micros * tokens * width * width, 12 * micros * tokens * width, 0,
        grid=(micros,),
        in_specs=[smem(), quarters(c), stepped(inputs), whole(vt.shape)]
        + ([anywhere()] * 2 if halves else [whole(ws[0].shape)]),
        out_specs=(rows, rows) + ((whole((width, width)),) if halves else ()),
        scratch_shapes=[pltpu.SemaphoreType.DMA((2 * ws[0].shape[0],))] if halves else [],
    )(info, c, inputs, vt, *ws)


def mlp_body(fast, first, lead, info_ref, *refs):
    refs = list(refs)
    take = lambda n: [refs.pop(0) for _ in range(n)]
    n2_ref, dz_ref, vt_ref = take(3)
    weights = take(1 if fast else 4)
    z_in, dn_in = (None, None) if first else take(2)
    z_ref, dn_ref = take(2)
    sides = 2 if fast else 1
    grads = take(2 * sides)
    (bias_ref,) = take(1)
    wu_s, wd_s, n2t_s, g_s, sem_w, sem_g = take(6)
    if not first:
        za_s, dna_s, sem_a = take(3)
        carried = [
            pltpu.make_async_copy(z_in, za_s, sem_a.at[0]),
            pltpu.make_async_copy(dn_in, dna_s, sem_a.at[1]),
        ]
    step = pl.program_id(0)
    width = n2_ref.shape[1]
    y = info_ref[1]
    results = [
        pltpu.make_async_copy(g_s.at[n // sides, n % sides], grads[n], sem_g.at[n]) for n in range(2 * sides)
    ]

    @pl.when(step == 0)
    def _():
        for ch in range(2):
            if fast:
                src = weights[0]
                count = src.shape[0] // 4
                rank = info_ref[0] ^ (lead + ch)
                rows = width // count
                for i in range(count):
                    for n, dest in enumerate((wu_s, wd_s)):
                        pltpu.make_async_copy(
                            src.at[4 * i + rank, pl.ds(n * rows, rows), :],
                            dest.at[ch, pl.ds(i * rows, rows), :],
                            sem_w.at[2 * ch + n],
                        ).start()
            else:
                for n, dest in enumerate((wu_s, wd_s)):
                    pltpu.make_async_copy(weights[2 * ch + n], dest.at[ch], sem_w.at[2 * ch + n]).start()
        if not first:
            for c in carried:
                c.start()
        n2t_s[...] = n2_ref[...].T
        bias_ref[...] = jnp.zeros(bias_ref.shape, F32)

    for n, dest in enumerate((wu_s, wd_s)):
        pltpu.make_async_copy(dest.at[step], dest.at[step], sem_w.at[2 * step + n]).wait()
    wu, wd = wu_s[step], wd_s[step]
    bias = vt_ref[pl.ds(8 + (info_ref[0] ^ (lead + step)), 1), :]
    u = mm(n2_ref[...], wu) + bias
    square = u * u
    t = jnp.tanh(GELU_A * u * (1.0 + GELU_B * square))
    f = (0.5 * u * (1.0 + t)).astype(BF)
    slope = 0.5 * (1.0 + t) + (0.5 * GELU_A) * u * (1.0 - t * t) * (1.0 + 3.0 * GELU_B * square)
    dz = dz_ref[...]
    du = (mm_nt(dz, wd) * slope).astype(BF)
    bias_ref[pl.ds(step, 1), :] = jnp.sum(du.astype(F32), axis=0, keepdims=True)
    grad_up = mm(n2t_s[...], du).astype(BF)
    grad_down = mm_tn(f, dz).astype(BF)
    if fast:
        count = 2 * g_s.shape[2]
        rows = width // count
        for yy in range(2):

            @pl.when(y == yy)
            def _(yy=yy):
                for i in range(count):
                    g_s[step, int(i % 2 != yy), i // 2, 0] = grad_up[i * rows : (i + 1) * rows]
                    g_s[step, int(i % 2 != yy), i // 2, 1] = grad_down[i * rows : (i + 1) * rows]
    else:
        g_s[step, 0, 0] = grad_up
        g_s[step, 0, 1] = grad_down
    for ch in range(2):

        @pl.when(step == ch)
        def _(ch=ch):
            for r in results[ch * sides : (ch + 1) * sides]:
                r.start()

    z, dn = mm(f, wd), mm_nt(du, wu)

    @pl.when(step == 0)
    def _():
        z_ref[...] = z
        dn_ref[...] = dn

    @pl.when(step == 1)
    def _():
        if first:
            z_ref[...] += z
            dn_ref[...] += dn
        else:
            for c in carried:
                c.wait()
            z_ref[...] += z + za_s[...]
            dn_ref[...] += dn + dna_s[...]
        for r in results:
            r.wait()


def mlp(fast, info, lead, n2, dz, vt, weights, carried):
    first = carried is None
    tokens, width = dz.shape
    acc = shape((tokens, width), F32)
    nf = weights[0].shape[0] // 4
    sides, one = (2, (nf // 2, 2, width // nf, width)) if fast else (1, (2, width, width))
    outs = (acc, acc, *(shape(one),) * (2 * sides), shape((8, width), F32))
    ins = (info, n2, dz, vt, *weights, *(() if first else carried))
    specs = [smem()] + [whole(a.shape) for a in (n2, dz, vt)] + [anywhere()] * len(weights)
    specs += [] if first else [anywhere()] * 2
    more = [] if first else [
        pltpu.VMEM((tokens, width), F32),
        pltpu.VMEM((tokens, width), F32),
        pltpu.SemaphoreType.DMA((2,)),
    ]
    return local_kernel(
        functools.partial(mlp_body, fast, first, lead), outs, "feed_forward",
        24 * tokens * width * width, 30 * tokens * width, 2 * tokens * width,
        grid=(2,),
        in_specs=specs,
        out_specs=(whole(acc.shape),) * 2 + (anywhere(),) * (2 * sides) + (whole((8, width)),),
        scratch_shapes=[
            pltpu.VMEM((2, width, width), BF),
            pltpu.VMEM((2, width, width), BF),
            pltpu.VMEM((width, tokens), BF),
            pltpu.VMEM((2, sides) + one, BF),
            pltpu.SemaphoreType.DMA((4,)),
            pltpu.SemaphoreType.DMA((2 * sides,)),
            *more,
        ],
    )(*ins)


def turn_body(chained, info_ref, y_ref, z_ref, dn_ref, dz_ref, w_ref, vt_ref, *refs):
    result_ref, dy_ref, da_ref, d_ref, sums_ref = refs[1:] if chained else refs
    y = y_ref[...]
    result_ref[...] = (y + z_ref[...] + vt_ref[7:8, :]).astype(BF)
    unit, inverse = unit_rows(y)
    dz = dz_ref[...].astype(F32)
    dn = dn_ref[...]
    dy = dz + norm_back(dn, unit, inverse, vt_ref[5:6, :])
    dy_ref[...] = dy
    da = dy.astype(BF)
    da_ref[...] = da
    d_ref[...] = mm_nt(w_ref[...], da).astype(BF).reshape(d_ref.shape)
    total = lambda a: jnp.sum(a, axis=0, keepdims=True)
    rest = jnp.zeros((4, y.shape[1]), F32)
    sums = jnp.concatenate([total(da.astype(F32)), total(dn * unit), total(dn), total(dz), rest], axis=0)

    @pl.when(pl.program_id(0) == 0)
    def _():
        sums_ref[...] = sums

    @pl.when(pl.program_id(0) > 0)
    def _():
        sums_ref[...] += sums


def turn(info, start, count, micros, y, z, dn, dz, w_out, vt, results):
    width = dz.shape[1]
    tokens = dz.shape[0] // micros
    hw = width // 4
    block = pl.BlockSpec((tokens, width), lambda i: (start + i, 0))
    rows = pl.BlockSpec((tokens, width), lambda i: (i, 0))
    outs = (
        shape((micros, tokens, width)),
        shape((count * tokens, width), F32),
        shape((count * tokens, width)),
        shape((4, count, hw, tokens)),
        shape((8, width), F32),
    )
    chained = results is not None
    return local_kernel(
        functools.partial(turn_body, chained), outs, "turn",
        2 * count * tokens * width, 2 * count * tokens, 0,
        grid=(count,),
        in_specs=[smem(), block, block, block, block, whole(w_out.shape), whole(vt.shape)]
        + ([anywhere()] if chained else []),
        out_specs=(stepped(outs[0], start), rows, rows, quarters(outs[3]), whole((8, width))),
        input_output_aliases={7: 0} if chained else {},
    )(info, y, z, dn, dz, w_out, vt, *((results,) if chained else ()))


def outproj_body(fast, info_ref, c_ref, *refs):
    outs, scratch = refs[:-1][-3 if fast else -1 :], refs[-1]
    das = refs[: -4 if fast else -2]
    at, y = info_ref[0], info_ref[1]
    da = jnp.concatenate([d[...] for d in das], axis=0)
    rows, micros = scratch.shape[0], c_ref.shape[1]
    left = jnp.concatenate([c_ref[:, m].reshape(rows, c_ref.shape[3]) for m in range(micros)], axis=1)
    scratch[...] = mm(left, da)
    if not fast:
        outs[0][...] = scratch[...]
        return
    keep, keep_other, send = outs
    nz, part, half = keep.shape
    first = lax.rem(at, 2) == 0
    for z in range(nz):
        for n in range(2):
            i = 2 * z + (y if n == 0 else 1 - y)
            block = scratch[pl.ds(pl.multiple_of(i * part, 16), part), :].astype(BF)
            left, right = block[:, :half], block[:, half:]
            (keep, keep_other)[n][z] = jnp.where(first, left, right)
            send[n, z] = jnp.where(first, right, left)


def outproj_grad(fast, info, c, das, nz, part):
    width = das[0].shape[1]
    total = sum(d.shape[0] for d in das)
    if fast:
        one = shape((nz, part, width // 2))
        outs = (one, one, shape((2, nz, part, width // 2)))
    else:
        outs = (shape((width, width), F32),)
    return local_kernel(
        functools.partial(outproj_body, fast), outs, "outproj_grad",
        2 * total * width * width, 6 * width * width, 0,
        in_specs=[smem()] + [vmem()] * (1 + len(das)),
        out_specs=(vmem(),) * len(outs),
        scratch_shapes=[pltpu.VMEM((width, width), F32)],
    )(info, c, *das)


def backward_body(first, last, micro, info_ref, ranges_ref, *refs):
    refs = list(refs)
    take = lambda n: [refs.pop(0) for _ in range(n)]
    d_ref, c_ref = take(2)
    xs = take(4)
    q_ref, k_ref, v_ref, lse_ref, seg_ref, w_ref, vt_ref = take(7)
    acc_in, sums_in = (None, None) if first else take(2)
    turned, biases = (take(2), take(2)) if last else ((), ())
    acc_ref, sums_ref, dn0_ref, dn2_ref, dn13_ref = take(5)
    dk_s, dv_s, dp_s, seg_s, dc_s, delta_s, kt_s, n1_s, unit_s = take(9)
    at = info_ref[0]
    _, hw, tokens = d_ref.shape
    heads = hw // HEAD_DIM
    seg_s[...] = jnp.broadcast_to(seg_ref[...].astype(F32), (128, seg_ref.shape[1])).T
    dk_s[...] = jnp.zeros(dk_s.shape, F32)
    dv_s[...] = jnp.zeros(dv_s.shape, F32)
    kt_s[...] = k_ref[...].astype(F32).T.astype(BF)
    for b in range(4):
        dct = d_ref[b].astype(F32)
        dc_s[b] = dct.T.astype(BF)
        product = dct * c_ref[b].astype(F32)
        for h in range(heads):
            delta_s[b, h : h + 1, :] = jnp.sum(product[h * HEAD_DIM : (h + 1) * HEAD_DIM], axis=0, keepdims=True)
    for k in range(4):
        rows = pl.ds(pl.multiple_of((at ^ k) * tokens, 128), tokens)
        unit, _ = unit_rows(xs[k][...].astype(F32))
        unit_s[rows, :] = unit
        n1_s[rows, :] = (unit * vt_ref[0:1, :] + vt_ref[1:2, :]).astype(BF)

    def block(b, carry):
        rows = pl.ds(pl.multiple_of(b * tokens, 128), tokens)
        queries = heads_apart(q_ref[rows, :], heads)
        contexts = heads_apart(dc_s[b], heads)
        seg_row = seg_ref[0:1, rows].astype(F32)
        log_sum = jnp.concatenate([lse_ref[h : h + 1, rows] for h in range(heads)], axis=1)
        delta = jnp.concatenate([delta_s[b, h : h + 1, :] for h in range(heads)], axis=1)

        def body(span):
            bias = jnp.where(seg_s[span, 0:1] == seg_row, 0.0, MASKED)
            scores = mm_nt(k_ref[span, :], queries) + jnp.concatenate([bias] * heads, axis=1)
            p = jnp.exp(scores - log_sum)
            g = (p * (mm_nt(v_ref[span, :], contexts) - delta)).astype(BF)
            dk_s[span, :] += mm(g, queries)
            dv_s[span, :] += mm(p.astype(BF), contexts)
            dq = jnp.concatenate(own_blocks(mm(kt_s[:, span], g), heads), axis=0).T.astype(BF)
            dp_s[rows, 0:hw] = (dq.astype(F32) * 0.125).astype(BF)

        for_window(ranges_ref, 4 * micro + b, tokens, body)
        return carry

    lax.fori_loop(0, 4, block, 0)
    dp_s[:, hw : 2 * hw] = dk_s[...].astype(BF)
    dp_s[:, 2 * hw : 3 * hw] = dv_s[...].astype(BF)
    total = lambda a: jnp.sum(a, axis=0, keepdims=True)
    acc = mm_tn(n1_s[...], dp_s[...])
    acc = acc if first else acc_in[...] + acc
    dg1 = ds1 = None
    outs = ((dn0_ref, 0), (dn13_ref, 0), (dn2_ref, 0), (dn13_ref, tokens))
    for k in range(4):
        rows = pl.ds(pl.multiple_of((at ^ k) * tokens, 128), tokens)
        dn1 = mm_nt(dp_s[rows, :], w_ref[:, : 3 * hw])
        a, b = total(dn1 * unit_s[rows, :]), total(dn1)
        dg1, ds1 = (a, b) if k == 0 else (dg1 + a, ds1 + b)
        ref, base = outs[k]
        ref[base : base + tokens, :] = dn1.astype(BF)
    dbq, dbv = (total(dp_s[:, n * hw : (n + 1) * hw].astype(F32)) for n in (0, 2))
    spread = lambda r: jnp.concatenate([jnp.where(at == s, r, 0.0) for s in range(4)], axis=1)
    sums = jnp.concatenate([dg1, ds1, spread(dbq), spread(dbv), jnp.zeros((4, dg1.shape[1]), F32)], axis=0)
    sums = sums if first else sums_in[...] + sums
    sums_ref[...] = sums
    if not last:
        acc_ref[...] = acc
        return
    width = acc.shape[0]
    rest = turned[0][...] + turned[1][...]
    chunk_rows = [biases[k // 2][k % 2 : k % 2 + 1, :] for k in range(4)]
    lines = [sums[0:4], rest[0:4]] + [pick(at ^ s, chunk_rows) for s in range(4)]
    lines = jnp.concatenate(lines + [jnp.zeros((116, width), F32)], axis=0)
    full = jnp.concatenate([acc, lines.T[:, 0:64]], axis=1)
    acc_ref[...] = full.astype(acc_ref.dtype).reshape(acc_ref.shape)


def backward(info, ranges, micro, d, d_at, c, xs, kept, seg, w, vt, carried, ends):
    q, k, v, lse = kept
    hw, tokens = d.shape[2:]
    length, width = k.shape[1], w.shape[0]
    first, last = carried is None, bool(ends)
    outs = (
        ends[-1] if last else shape((width, 3 * hw), F32),
        shape((8, width), F32),
        shape((tokens, width)),
        shape((tokens, width)),
        shape((2 * tokens, width)),
    )
    rest = (w, vt, *(() if first else carried), *ends[:-1])
    stacked = (*xs, q, k, v, lse, seg)
    specs = [smem(), smem(), quarters(d, d_at), quarters(c, micro)] + [picked(a, micro) for a in stacked]
    specs += [whole(a.shape) for a in rest]
    flops = 4 * length * width * 3 * hw + 40 * length * length * hw
    return local_kernel(
        functools.partial(backward_body, first, last, micro), outs, "attention_backward",
        flops, 8 * length * width * 2, 3 * length * length,
        grid=(1,),
        in_specs=specs,
        out_specs=tuple(whole(o.shape) for o in outs),
        scratch_shapes=[
            pltpu.VMEM((length, hw), F32),
            pltpu.VMEM((length, hw), F32),
            pltpu.VMEM((length, 3 * hw), BF),
            pltpu.VMEM((length, 128), F32),
            pltpu.VMEM((4, tokens, hw), BF),
            pltpu.VMEM((4, 8, tokens), F32),
            pltpu.VMEM((hw, length), BF),
            pltpu.VMEM((length, width), BF),
            pltpu.VMEM((length, width), F32),
        ],
    )(info, ranges, d, c, *stacked, *rest)


def finish_body(chained, a_ref, b_ref, r_ref, dy_ref, x_ref, vt_ref, *refs):
    gx_ref = refs[-1]
    unit, inverse = unit_rows(x_ref[...].astype(F32))
    dn1 = a_ref[...].astype(F32) + b_ref[...].astype(F32) + r_ref[...].astype(F32)
    gx_ref[...] = dy_ref[...] + norm_back(dn1, unit, inverse, vt_ref[0:1, :])


def finish(micro, a, b, r, dy, dy_at, inputs, vt, grads):
    tokens, width = a.shape
    chained = grads is not None
    out = shape(inputs.shape, F32)
    top = pl.BlockSpec((tokens, width), lambda i: (0, 0))
    return local_kernel(
        functools.partial(finish_body, chained), out, "finish", a.shape[0], a.shape[0], 0,
        grid=(1,),
        in_specs=[top, top, top, pl.BlockSpec((tokens, width), lambda i: (dy_at, 0)), picked(inputs, micro), whole(vt.shape)] + ([anywhere()] if chained else []),
        out_specs=picked(out, micro),
        input_output_aliases={6: 0} if chained else {},
    )(a, b, r, dy, inputs, vt, *((grads,) if chained else ()))


def split_body(count, info_ref, *refs):
    ins, outs = refs[:count], refs[count:]
    nz = len(outs)
    for d in range(nz):
        at = lax.rem(info_ref[2] + nz - d, nz)
        total = ins[0][at].astype(F32)
        for r in ins[1:]:
            total = total + r[at].astype(F32)
        outs[d][...] = total.astype(BF)


def split(info, terms):
    nz, *dims = terms[-1].shape
    dims = tuple(dims)
    return local_kernel(
        functools.partial(split_body, len(terms)), (shape(dims),) * nz, "split",
        0, 2 * (len(terms) + 1) * nz * math.prod(dims), 0,
        grid=(1,),
        in_specs=[smem()] + [whole(t.shape) for t in terms],
        out_specs=(whole(dims),) * nz,
    )(info, *terms)


def block_sum(ref):
    return functools.reduce(jnp.add, [ref[n].astype(F32) for n in range(ref.shape[0])])


def collect_body(up_ref, down_ref, out_ref):
    rows = up_ref.shape[1]
    out_ref[:rows] = block_sum(up_ref).astype(BF)
    out_ref[rows:] = block_sum(down_ref).astype(BF)


def collect(up, rest):
    nz, rows, width = up.shape
    first = pl.BlockSpec(up.shape, lambda i: (0, 0, 0))
    return local_kernel(
        collect_body, shape((2 * rows, width)), "collect", 0, 20 * rows * width, 0,
        grid=(1,),
        in_specs=[first, first],
        out_specs=whole((2 * rows, width)),
    )(up, rest)


def assemble_mlp_body(info_ref, *refs):
    ms, (gu_ref, gd_ref, all_s) = refs[:-3], refs[-3:]
    at = info_ref[0]
    for k, r in enumerate(ms):
        all_s[at ^ k] = r[...]
    rows, part = gu_ref.shape[0], gd_ref.shape[0] // 4
    for s in range(4):
        up = all_s[s, 0:rows, :].astype(F32)
        for i in range(up.shape[1] // part):
            col = i * 4 * part + s * part
            gu_ref[:, col : col + part] = up[:, i * part : (i + 1) * part]
        gd_ref[s * part : (s + 1) * part, :] = all_s[s, rows : rows + part, :].astype(F32)


def assemble_mlp(info, ms, rows):
    width = ms[0].shape[1]
    part = ms[0].shape[0] - rows
    outs = (shape((rows, 4 * width), F32), shape((4 * part, width), F32))
    return local_kernel(
        assemble_mlp_body, outs, "assemble_mlp", 0, 12 * rows * width * 4, 0,
        in_specs=[smem()] + [vmem()] * 4,
        out_specs=(vmem(),) * 2,
        scratch_shapes=[pltpu.VMEM((4,) + ms[0].shape, BF)],
    )(info, *ms)


def share_body(q_ref, o_ref, out_ref):
    out_ref[...] = jnp.concatenate([block_sum(q_ref), block_sum(o_ref)], axis=1).astype(BF)


def share(q, rest, cols):
    nz, rows = rest.shape[:2]
    last = rest.shape[2] // cols - 1
    return local_kernel(
        share_body, shape((rows, q.shape[2] + cols)), "share", 0, 2 * (q.size + rest.size), 0,
        grid=(1,),
        in_specs=[whole(q.shape), pl.BlockSpec((nz, rows, cols), lambda i: (0, 0, last))],
        out_specs=whole((rows, q.shape[2] + cols)),
    )(q, rest)


def assemble_heads_body(q_ref, gq_ref, go_ref, gv_ref, gb_ref):
    hw = gq_ref.shape[1] // 12
    half = go_ref.shape[1] // 2
    for s in range(4):
        for n in range(3):
            base = n * 4 * hw + s * hw
            gq_ref[:, base : base + hw] = q_ref[s, :, n * hw : (n + 1) * hw].astype(F32)
    for h in range(2):
        a, b = (q_ref[h + 2 * n, :, 3 * hw + 64 :].astype(F32) for n in range(2))
        go_ref[:, h * half : (h + 1) * half] = a + b
    tail = (3 * hw) // 128 * 128
    off = 3 * hw - tail
    extra = functools.reduce(jnp.add, [q_ref[s, :, tail : tail + 128].astype(F32) for s in range(4)]).T
    gv_ref[...] = extra[off : off + 8]
    gb_ref[...] = extra[off + 8 : off + 12]


def assemble_heads(q, hw):
    rows = q.shape[1]
    outs = (
        shape((rows, 12 * hw), F32),
        shape((rows, 4 * hw), F32),
        shape((8, rows), F32),
        shape((4, rows), F32),
    )
    return local_kernel(
        assemble_heads_body, outs, "assemble_heads", 0, 12 * rows * hw * 16, 0,
        in_specs=[vmem()],
        out_specs=(vmem(),) * 4,
    )(q)


def send(x, axis, to):
    n = lax.axis_size(axis)
    return lax.ppermute(x, axis, [(s, to(s)) for s in range(n)])


def seq_swap(x, k):
    return send(x, "seq", lambda s: s ^ k)


def add(*terms):
    out = terms[0].astype(F32)
    for t in terms[1:]:
        out = out + t.astype(F32)
    return out.astype(BF)


def after(values, *others):
    out = lax.optimization_barrier((values, others))
    return out[0]


def shards(inputs, segments, cotangent, w_qkv, w_out, w_up, w_down, vectors, bias_up):
    micros, _, tokens, width = inputs.shape
    nf = lax.axis_size("fsdp")
    assert lax.axis_size("seq") == 4 and inputs.shape[1] == 1
    rows = w_qkv.shape[0]
    part = w_down.shape[0] // 4
    hw = width // 4
    nz = nf // 2
    fast = nf == 8 and rows % 32 == 0 and part == rows
    at = lax.axis_index("seq")
    me = lax.axis_index("fsdp")
    z, y = me // 2, me % 2
    info = jnp.stack([at, y, z]).astype(jnp.int32)
    y_swap = lambda x: send(x, "fsdp", lambda s: s ^ 1)
    z_pull = lambda x, d: send(x, "fsdp", lambda s: (s - 2 * d) % nf)
    pulled = lambda x: [x] + [z_pull(x, d) for d in range(1, nz)]

    ranges = windows(segments[:, 0], tokens)

    own = inputs[:, 0]
    across = seq_swap(own, 2)
    beside = seq_swap(own, 1)

    if fast:
        qkv_piece, mlp_piece, out_copies = local_kernel(
            prep_body,
            (shape((rows, 3 * hw + 64)), shape((rows + part, width)), shape((nf, rows // 2, width))),
            "prep", 0, 6 * rows * 4 * width, 0,
            in_specs=[smem()] + [vmem()] * 6,
            out_specs=(vmem(),) * 3,
        )(info, w_qkv, w_out, w_up, w_down, vectors.T, bias_up.reshape(4, part))
        w_heads = lax.all_gather(qkv_piece, "fsdp", axis=0, tiled=True)
        out_half = lax.all_to_all(
            after(out_copies, w_heads), "fsdp", split_axis=0, concat_axis=0, tiled=True
        )
        gathered = lax.all_gather(mlp_piece, ("fsdp", "seq"), axis=0, tiled=False)
    else:
        gather = lambda a: lax.all_gather(a, "fsdp", axis=0, tiled=True)
        by_head = gather(w_qkv).reshape(width, 3, 4, hw)
        mine = lax.dynamic_index_in_dim(by_head, at, 2, keepdims=False).reshape(width, 3 * hw)
        biases = gather(bias_up).reshape(nf, 4, part).transpose(0, 2, 1).reshape(width, 4)
        w_heads = jnp.concatenate([mine, gather(vectors), biases, jnp.zeros((width, 52), BF)], axis=1)
        w_out_full = gather(w_out)
        ups = gather(w_up).reshape(width, nf, 4, part).transpose(2, 0, 1, 3).reshape(4, width, width)
        downs = gather(w_down).reshape(nf, 4, part, width).transpose(1, 0, 2, 3).reshape(4, width, width)
        one = lambda a, k: lax.dynamic_index_in_dim(a, at ^ k, 0, keepdims=False)
        chunks = [(one(ups, k), one(downs, k)) for k in range(4)]

    xs = (own, beside, across, seq_swap(after(across, w_heads), 1))

    over_seq = lambda a: lax.all_to_all(a, "seq", split_axis=0, concat_axis=0, tiled=True)
    q, k, v, c, lse, vt = forward(info, ranges, xs, segments, w_heads)
    kept = (q, k, v, lse)
    contexts = over_seq(c)
    if fast:
        out_half = after(out_half, vt)
        y_rows, n2, w_out_full = middle(info, contexts, own, vt, (out_half, seq_swap(out_half, 1)))
        gathered = after(gathered, n2)
        weights_a = weights_b = [gathered]
    else:
        y_rows, n2 = middle(info, contexts, own, vt, (w_out_full,))
        weights_a, weights_b = [*chunks[0], *chunks[1]], [*chunks[2], *chunks[3]]

    dz = cotangent.reshape(micros * tokens, width)
    za, dna, *near_g, bias_a = mlp(fast, info, 0, n2, dz, vt, weights_a, None)
    if fast:
        near_own, near_oth = (seq_swap(a, 1) for a in near_g[2:])
        near_s = add(near_g[1], near_oth)
        near_y = y_swap(near_s)
        za, dna = after((za, dna), near_s)
    zb, dnb, *far_g, bias_b = mlp(fast, info, 2, n2, dz, vt, weights_b, (za, dna))

    results, dy_a, da_a, d_a, sums_a = turn(info, 0, 1, micros, y_rows, zb, dnb, dz, w_out_full, vt, None)
    d_a = over_seq(d_a)
    if fast:
        zb, dnb = after((zb, dnb), near_y)
    results, dy_b, da_b, d_b, sums_b = turn(
        info, 1, micros - 1, micros, y_rows, zb, dnb, dz, w_out_full, vt, results
    )
    d_b = over_seq(d_b)
    if fast:
        far_own, far_oth = (seq_swap(after(a, da_b), 1) for a in far_g[2:])
        over_near = lambda parts: [parts[0]] + [z_pull(parts[d], d) for d in range(1, nz)]
        far_part = lambda n: add(far_g[0][:, n], far_own[:, n], far_y[n])
        near_z = over_near(split(info, [near_g[0], near_own, near_y]))
        contexts = after(contexts, near_z[0])
    out_grads = outproj_grad(fast, info, contexts, (da_a, da_b), nz, rows)
    carried = None
    pending, settled, totals = [], [], []

    def settle(m, own_part, across_part, got, later):
        if later is not None:
            got = after(got, later)
        total = add(across_part, got[tokens:])
        settled.append((m, own_part, got, seq_swap(total, 2)))
        return total

    gate = ()
    if fast:
        groups_z = [list(range(n, nf, 2)) for n in range(2)]
        over_z = lambda a: lax.all_to_all(
            a, "fsdp", split_axis=0, concat_axis=0, tiled=True, axis_index_groups=groups_z
        )
        keep, keep_other, to_core = out_grads
        out_c = seq_swap(to_core, 1)
        far_own, far_oth = after((far_own, far_oth), keep)
        far_s = [add(far_g[1][:, n], far_oth[:, n]) for n in range(2)]
        far_y = [y_swap(a) for a in far_s]
        gate = (keep, *far_s)
    for m in range(micros):
        if fast and m == 1:
            far_y[0], out_c, near_z = after((far_y[0], out_c, near_z), dn0)
            out_s = add(keep_other, out_c[1])
            out_y = y_swap(out_s)
            far_up = far_part(0)
            far_up_z = over_z(far_up)
            gate = (far_up, out_s)
        if fast and m == 2:
            out_y, far_y[1], far_up_z, near_z = after((out_y, far_y[1], far_up_z, near_z), dn0)
            rest = jnp.concatenate([far_part(1), add(keep, out_c[0], out_y)], axis=2)
            rest_z = over_z(rest)
            near_sum = add(*near_z).reshape(rows + part, width)
            near_x = seq_swap(near_sum, 2)
            gate = (rest, near_sum)
        d, d_at = (d_a, 0) if m == 0 else (d_b, m - 1)
        last = m == micros - 1
        packed = shape((nf, rows, 3 * hw + 64)) if fast else shape((width, 3 * hw + 64), F32)
        ends = (sums_a, sums_b, bias_a, bias_b, packed) if last else ()
        acc, sums, dn0, dn2, dn13 = backward(
            info, ranges, m, d, d_at, c, xs, kept, segments, after(w_heads, *gate), vt, carried, ends
        )
        carried = (acc, sums)
        pending.append((m, dn0, dn2, seq_swap(dn13, 1)))
        if m > 0:
            totals.append(settle(*pending.pop(0), dn0))
    if fast:
        acc = after(acc, rest_z, settled[0][3], near_x)
    last_total = settle(*pending.pop(0), None)
    if fast:
        far_sum = collect(far_up_z, rest_z)
        m, own_part, got, theirs = settled[0]
        settled[0] = (m, after(own_part, far_sum, last_total, *totals), got, theirs)
    grad_rows, rows_done = None, []
    for m, own_part, got, theirs in settled:
        dy, dy_at = (dy_a, 0) if m == 0 else (dy_b, m - 1)
        grad_rows = finish(m, own_part, got, theirs, dy, dy_at, own, vt, grad_rows)
        rows_done.append(grad_rows)

    if fast:
        qkv_z = lax.all_to_all(acc, "fsdp", split_axis=0, concat_axis=0, tiled=True)
        mine = add(near_sum, after(seq_swap(far_sum, 2), rows_done[0]))
        theirs = add(near_x, far_sum)
        g_up, g_down = assemble_mlp(info, [mine, seq_swap(mine, 1), theirs, seq_swap(theirs, 1)], rows)
        qkv_z = after(qkv_z, grad_rows)
        heads_share = share(qkv_z, rest_z, width // 2)
        g_qkv, g_out, g_vec, g_bias = assemble_heads(lax.all_gather(heads_share, "seq", axis=0, tiled=False), hw)
        g_vec, g_bias = g_vec.T, g_bias.reshape(4 * part)
    else:
        total = lambda a: lax.psum(
            lax.psum_scatter(a.astype(F32), "fsdp", scatter_dimension=0, tiled=True), "seq"
        )
        head_place = lambda a: lax.dynamic_update_slice_in_dim(
            jnp.zeros((width, 3, 4, hw), F32), a.reshape(width, 3, 1, hw), at, 2
        ).reshape(width, 12 * hw)
        g_qkv = total(head_place(acc[:, : 3 * hw]))
        g_out = total(out_grads[0])
        extra = total(acc[:, 3 * hw :])
        g_vec, g_bias = extra[:, :8], extra[:, 8:12].T.reshape(4 * part)
        pairs = jnp.stack([*near_g, *far_g])
        order = lambda n: jnp.stack(
            [lax.dynamic_index_in_dim(pairs[:, n], at ^ s, 0, keepdims=False) for s in range(4)]
        )
        ups = order(0).reshape(4, width, nf, part).transpose(1, 2, 0, 3).reshape(width, 4 * width)
        downs = order(1).reshape(4, nf, part, width).transpose(1, 0, 2, 3).reshape(4 * width, width)
        g_up, g_down = total(ups), total(downs)
    return (
        results[:, None],
        grad_rows[:, None],
        g_qkv,
        g_out,
        g_up,
        g_down,
        g_vec,
        g_bias,
    )


def solution(mesh):
    rows = P(None, "fsdp", "seq", None)
    first = P("fsdp", None)
    in_specs = (rows, P(None, "fsdp", None), rows, first, first, first, first, first, P("fsdp"))
    out_specs = (rows, rows, first, first, first, first, first, P("fsdp"))
    return jax.shard_map(shards, mesh=mesh, in_specs=in_specs, out_specs=out_specs, check_vma=False)
```

```python
import functools
import math

import jax
import jax.numpy as jnp
from jax import lax
from jax.experimental import pallas as pl
from jax.experimental.pallas import tpu as pltpu
from jax.sharding import PartitionSpec as P

HEADS = 12
HEAD_DIM = 64
EPS = 1e-05
MASKED = -1e30
GELU_A = math.sqrt(2.0 / math.pi)
GELU_B = 0.044715
BF = jnp.bfloat16
F32 = jnp.float32
VMEM_LIMIT = 60 * 1024 * 1024


def shape(dims, dtype=BF):
    return jax.ShapeDtypeStruct(dims, dtype)


def vmem():
    return pl.BlockSpec(memory_space=pltpu.VMEM)


def smem():
    return pl.BlockSpec(memory_space=pltpu.SMEM)


def anywhere():
    return pl.BlockSpec(memory_space=pl.ANY)


def local_kernel(body, outs, name, flops=0, bytes_moved=0, exps=0, **kw):
    return pl.pallas_call(
        body,
        out_shape=outs,
        name=name,
        compiler_params=pltpu.CompilerParams(vmem_limit_bytes=VMEM_LIMIT),
        cost_estimate=pl.CostEstimate(
            flops=flops, bytes_accessed=bytes_moved, transcendentals=exps
        ),
        **kw,
    )


def mm(a, b):
    return lax.dot_general(a, b, (((1,), (0,)), ((), ())), preferred_element_type=F32)


def mm_nt(a, b):
    return lax.dot_general(a, b, (((1,), (1,)), ((), ())), preferred_element_type=F32)


def mm_tn(a, b):
    return lax.dot_general(a, b, (((0,), (0,)), ((), ())), preferred_element_type=F32)


def unit_rows(v):
    centred = v - jnp.mean(v, axis=-1, keepdims=True)
    inverse = lax.rsqrt(jnp.mean(centred * centred, axis=-1, keepdims=True) + EPS)
    return centred * inverse, inverse


def norm_back(grad, unit, inverse, gain):
    t = grad * gain
    first = jnp.mean(t, axis=-1, keepdims=True)
    second = jnp.mean(t * unit, axis=-1, keepdims=True)
    return inverse * (t - first - unit * second)


def pick(at, options):
    out = options[0]
    for s in range(1, len(options)):
        out = jnp.where(at == s, options[s], out)
    return out


def column_of(row, rows):
    return jnp.broadcast_to(row, (128, rows)).T[:, 0:1]


def prep_body(info_ref, wq_ref, wo_ref, up_ref, down_ref, vec_ref, bias_ref, qkv_ref, mlp_ref, out_ref):
    rows = wq_ref.shape[0]
    width = up_ref.shape[1] // 4
    hw = wq_ref.shape[1] // 12
    part = down_ref.shape[0] // 4
    for s in range(4):

        @pl.when(info_ref[0] == s)
        def _(s=s):
            for n in range(3):
                base = n * 4 * hw + s * hw
                qkv_ref[:, n * hw : (n + 1) * hw] = wq_ref[:, base : base + hw]
            for i in range(width // part):
                col = i * 4 * part + s * part
                mlp_ref[0:rows, i * part : (i + 1) * part] = up_ref[:, col : col + part]
            mlp_ref[rows : rows + part, :] = down_ref[s * part : (s + 1) * part, :]
            for n in range(out_ref.shape[0]):
                out_ref[n] = wo_ref[s % 2 * (rows // 2) : (s % 2 + 1) * (rows // 2), :]

    lines = jnp.concatenate([vec_ref[...].astype(F32), bias_ref[...].astype(F32)], axis=0)
    lines = jnp.concatenate([lines, jnp.zeros((128 - lines.shape[0], rows), F32)], axis=0)
    qkv_ref[:, 3 * hw : 3 * hw + 64] = lines.T[:, 0:64].astype(BF)


def windows(segments, block):
    length = segments.shape[-1]
    first, last = segments[:, ::block, None], segments[:, block - 1 :: block, None]
    low = jnp.sum(segments[:, None, :] < first, axis=-1)
    high = jnp.sum(segments[:, None, :] <= last, axis=-1)
    low = low // 128 * 128
    count = (high - low + block - 1) // block
    start = jnp.minimum(low, length - count * block)
    return jnp.stack([start, count], axis=-1).astype(jnp.int32).reshape(-1)


def for_window(ranges_ref, at, block, body):
    start = pl.multiple_of(ranges_ref[2 * at], 128)
    for size in range(1, 5):

        @pl.when(ranges_ref[2 * at + 1] == size)
        def _(size=size):
            body(pl.ds(start, size * block))


def heads_apart(rows, heads):
    lane_head = lax.broadcasted_iota(jnp.int32, (1, rows.shape[1]), 1) // HEAD_DIM
    return jnp.concatenate([jnp.where(lane_head == h, rows, 0).astype(BF) for h in range(heads)], axis=0)


def own_blocks(wide, heads):
    width = wide.shape[1] // heads
    return [
        wide[h * HEAD_DIM : (h + 1) * HEAD_DIM, h * width : (h + 1) * width] for h in range(heads)
    ]


def picked(array, at):
    if array.ndim == 2:
        return pl.BlockSpec(array.shape, lambda i: (0, 0))
    return pl.BlockSpec((None,) + array.shape[1:], lambda i: (at,) + (0,) * (array.ndim - 1))


def whole(dims):
    return pl.BlockSpec(dims, lambda i: (0,) * len(dims))


def forward_body(info_ref, ranges_ref, x0, x1, x2, x3, seg_ref, w_ref, *refs):
    q_ref, k_ref, v_ref, c_ref, lse_ref, vt_ref, n1_ref, vtr_ref, seg_s = refs
    at = info_ref[0]
    micro = pl.program_id(0)
    tokens, width = x0.shape
    hw = q_ref.shape[1]
    heads = hw // HEAD_DIM
    tail = (3 * hw) // 128 * 128
    off = 3 * hw - tail
    vt_ref[...] = w_ref[:, tail : tail + 128].astype(F32).T[off : off + 16]
    g1, s1 = vt_ref[0:1, :], vt_ref[1:2, :]
    bq = pick(at, [vt_ref[2:3, s * hw : (s + 1) * hw] for s in range(4)])
    bv = pick(at, [vt_ref[3:4, s * hw : (s + 1) * hw] for s in range(4)])
    seg_s[...] = jnp.broadcast_to(seg_ref[...].astype(F32), (128, seg_ref.shape[1])).T
    for k, x_ref in enumerate((x0, x1, x2, x3)):
        unit, _ = unit_rows(x_ref[...].astype(F32))
        n1_ref[pl.ds(pl.multiple_of((at ^ k) * tokens, 128), tokens), :] = (unit * g1 + s1).astype(BF)
    project = mm(n1_ref[...], w_ref[:, : 3 * hw])
    q_ref[...] = ((project[:, :hw] + bq) * 0.125).astype(BF)
    keys = project[:, hw : 2 * hw]
    k_ref[...] = keys.astype(BF)
    values = project[:, 2 * hw : 3 * hw] + bv
    v_ref[...] = values.astype(BF)
    vtr_ref[...] = values.T.astype(BF)
    lse_ref[...] = jnp.zeros(lse_ref.shape, F32)

    def block(b, carry):
        rows = pl.ds(pl.multiple_of(b * tokens, 128), tokens)
        queries = heads_apart(q_ref[rows, :], heads)
        seg_row = seg_ref[0:1, rows].astype(F32)

        def body(span):
            bias = jnp.where(seg_s[span, 0:1] == seg_row, 0.0, MASKED)
            scores = mm_nt(k_ref[span, :], queries) + jnp.concatenate([bias] * heads, axis=1)
            top = jnp.max(scores, axis=0, keepdims=True)
            raised = jnp.exp(scores - top)
            total = jnp.sum(raised, axis=0, keepdims=True)
            context = mm(vtr_ref[:, span], raised.astype(BF)) * (1.0 / total)
            c_ref[b] = jnp.concatenate(own_blocks(context, heads), axis=0).astype(BF)
            log_sum = top + jnp.log(total)
            for h in range(heads):
                lse_ref[h : h + 1, rows] = log_sum[:, h * tokens : (h + 1) * tokens]

        for_window(ranges_ref, 4 * micro + b, tokens, body)
        return carry

    lax.fori_loop(0, 4, block, 0)


def quarters(array, at=None):
    dims = (array.shape[0], None) + array.shape[2:]
    return pl.BlockSpec(dims, (lambda i: (0, i, 0, 0)) if at is None else (lambda i: (0, at, 0, 0)))


def forward(info, ranges, xs, seg, w):
    micros, tokens, width = xs[0].shape
    hw = width // 4
    length = 4 * tokens
    outs = (
        shape((micros, length, hw)),
        shape((micros, length, hw)),
        shape((micros, length, hw)),
        shape((4, micros, hw, tokens)),
        shape((micros, 8, length), F32),
        shape((16, width), F32),
    )
    flops = micros * (2 * length * width * 3 * hw + 16 * length * length * hw)
    return local_kernel(
        forward_body, outs, "attention_forward",
        flops, micros * 4 * length * width * 2, micros * 3 * length * length,
        grid=(micros,),
        in_specs=[smem(), smem()] + [stepped(a) for a in (*xs, seg)] + [whole(w.shape)],
        out_specs=tuple(quarters(o) if n == 3 else stepped(o) for n, o in enumerate(outs)),
        scratch_shapes=[
            pltpu.VMEM((length, width), BF),
            pltpu.VMEM((hw, length), BF),
            pltpu.VMEM((length, 128), F32),
        ],
    )(info, ranges, *xs, seg, w)


def stepped(array, start=0):
    if array.ndim == 2:
        return whole(array.shape)
    return pl.BlockSpec((None,) + array.shape[1:], lambda i: (start + i,) + (0,) * (array.ndim - 1))


def middle_body(halves, info_ref, c_ref, x_ref, vt_ref, *refs):
    if halves:
        mine, theirs, y_ref, n2_ref, w_ref, sem = refs

        @pl.when(pl.program_id(0) == 0)
        def _():
            count, part = mine.shape[:2]
            core = lax.rem(info_ref[0], 2)
            copies = []
            for n, src in enumerate((mine, theirs)):
                for i in range(count):
                    dest = pl.multiple_of(i * 2 * part + (core if n == 0 else 1 - core) * part, 16)
                    copies.append(
                        pltpu.make_async_copy(src.at[i], w_ref.at[pl.ds(dest, part), :], sem.at[n * count + i])
                    )
            for c in copies:
                c.start()
            for c in copies:
                c.wait()
    else:
        w_ref, y_ref, n2_ref = refs
    context = c_ref[...].reshape(w_ref.shape[0], c_ref.shape[2])
    y = x_ref[...].astype(F32) + vt_ref[4:5, :] + mm_tn(context, w_ref[...])
    y_ref[...] = y
    unit, _ = unit_rows(y)
    n2_ref[...] = (unit * vt_ref[5:6, :] + vt_ref[6:7, :]).astype(BF)


def middle(info, c, inputs, vt, ws):
    micros, tokens, width = inputs.shape
    halves = len(ws) == 2
    outs = (shape((micros * tokens, width), F32), shape((micros * tokens, width)))
    outs += (shape((width, width)),) if halves else ()
    rows = pl.BlockSpec((tokens, width), lambda i: (i, 0))
    return local_kernel(
        functools.partial(middle_body, halves), outs, "middle",
        2 * micros * tokens * width * width, 12 * micros * tokens * width, 0,
        grid=(micros,),
        in_specs=[smem(), quarters(c), stepped(inputs), whole(vt.shape)]
        + ([anywhere()] * 2 if halves else [whole(ws[0].shape)]),
        out_specs=(rows, rows) + ((whole((width, width)),) if halves else ()),
        scratch_shapes=[pltpu.SemaphoreType.DMA((2 * ws[0].shape[0],))] if halves else [],
    )(info, c, inputs, vt, *ws)


def mlp_body(fast, first, lead, info_ref, *refs):
    refs = list(refs)
    take = lambda n: [refs.pop(0) for _ in range(n)]
    n2_ref, dz_ref, vt_ref = take(3)
    weights = take(1 if fast else 4)
    z_in, dn_in = (None, None) if first else take(2)
    z_ref, dn_ref = take(2)
    sides = 2 if fast else 1
    grads = take(2 * sides)
    (bias_ref,) = take(1)
    wu_s, wd_s, n2t_s, g_s, sem_w, sem_g = take(6)
    if not first:
        za_s, dna_s, sem_a = take(3)
        carried = [
            pltpu.make_async_copy(z_in, za_s, sem_a.at[0]),
            pltpu.make_async_copy(dn_in, dna_s, sem_a.at[1]),
        ]
    step = pl.program_id(0)
    width = n2_ref.shape[1]
    y = info_ref[1]
    results = [
        pltpu.make_async_copy(g_s.at[n // sides, n % sides], grads[n], sem_g.at[n]) for n in range(2 * sides)
    ]

    @pl.when(step == 0)
    def _():
        for ch in range(2):
            if fast:
                src = weights[0]
                count = src.shape[0] // 4
                rank = info_ref[0] ^ (lead + ch)
                rows = width // count
                for i in range(count):
                    for n, dest in enumerate((wu_s, wd_s)):
                        pltpu.make_async_copy(
                            src.at[4 * i + rank, pl.ds(n * rows, rows), :],
                            dest.at[ch, pl.ds(i * rows, rows), :],
                            sem_w.at[2 * ch + n],
                        ).start()
            else:
                for n, dest in enumerate((wu_s, wd_s)):
                    pltpu.make_async_copy(weights[2 * ch + n], dest.at[ch], sem_w.at[2 * ch + n]).start()
        if not first:
            for c in carried:
                c.start()
        n2t_s[...] = n2_ref[...].T
        bias_ref[...] = jnp.zeros(bias_ref.shape, F32)

    for n, dest in enumerate((wu_s, wd_s)):
        pltpu.make_async_copy(dest.at[step], dest.at[step], sem_w.at[2 * step + n]).wait()
    wu, wd = wu_s[step], wd_s[step]
    bias = vt_ref[pl.ds(8 + (info_ref[0] ^ (lead + step)), 1), :]
    u = mm(n2_ref[...], wu) + bias
    square = u * u
    t = jnp.tanh(GELU_A * u * (1.0 + GELU_B * square))
    f = (0.5 * u * (1.0 + t)).astype(BF)
    slope = 0.5 * (1.0 + t) + (0.5 * GELU_A) * u * (1.0 - t * t) * (1.0 + 3.0 * GELU_B * square)
    dz = dz_ref[...]
    du = (mm_nt(dz, wd) * slope).astype(BF)
    bias_ref[pl.ds(step, 1), :] = jnp.sum(du.astype(F32), axis=0, keepdims=True)
    grad_up = mm(n2t_s[...], du).astype(BF)
    grad_down = mm_tn(f, dz).astype(BF)
    if fast:
        count = 2 * g_s.shape[2]
        rows = width // count
        for yy in range(2):

            @pl.when(y == yy)
            def _(yy=yy):
                for i in range(count):
                    g_s[step, int(i % 2 != yy), i // 2, 0] = grad_up[i * rows : (i + 1) * rows]
                    g_s[step, int(i % 2 != yy), i // 2, 1] = grad_down[i * rows : (i + 1) * rows]
    else:
        g_s[step, 0, 0] = grad_up
        g_s[step, 0, 1] = grad_down
    for ch in range(2):

        @pl.when(step == ch)
        def _(ch=ch):
            for r in results[ch * sides : (ch + 1) * sides]:
                r.start()

    z, dn = mm(f, wd), mm_nt(du, wu)

    @pl.when(step == 0)
    def _():
        z_ref[...] = z
        dn_ref[...] = dn

    @pl.when(step == 1)
    def _():
        if first:
            z_ref[...] += z
            dn_ref[...] += dn
        else:
            for c in carried:
                c.wait()
            z_ref[...] += z + za_s[...]
            dn_ref[...] += dn + dna_s[...]
        for r in results:
            r.wait()


def mlp(fast, info, lead, n2, dz, vt, weights, carried):
    first = carried is None
    tokens, width = dz.shape
    acc = shape((tokens, width), F32)
    nf = weights[0].shape[0] // 4
    sides, one = (2, (nf // 2, 2, width // nf, width)) if fast else (1, (2, width, width))
    outs = (acc, acc, *(shape(one),) * (2 * sides), shape((8, width), F32))
    ins = (info, n2, dz, vt, *weights, *(() if first else carried))
    specs = [smem()] + [whole(a.shape) for a in (n2, dz, vt)] + [anywhere()] * len(weights)
    specs += [] if first else [anywhere()] * 2
    more = [] if first else [
        pltpu.VMEM((tokens, width), F32),
        pltpu.VMEM((tokens, width), F32),
        pltpu.SemaphoreType.DMA((2,)),
    ]
    return local_kernel(
        functools.partial(mlp_body, fast, first, lead), outs, "feed_forward",
        24 * tokens * width * width, 30 * tokens * width, 2 * tokens * width,
        grid=(2,),
        in_specs=specs,
        out_specs=(whole(acc.shape),) * 2 + (anywhere(),) * (2 * sides) + (whole((8, width)),),
        scratch_shapes=[
            pltpu.VMEM((2, width, width), BF),
            pltpu.VMEM((2, width, width), BF),
            pltpu.VMEM((width, tokens), BF),
            pltpu.VMEM((2, sides) + one, BF),
            pltpu.SemaphoreType.DMA((4,)),
            pltpu.SemaphoreType.DMA((2 * sides,)),
            *more,
        ],
    )(*ins)


def turn_body(chained, info_ref, y_ref, z_ref, dn_ref, dz_ref, w_ref, vt_ref, *refs):
    result_ref, dy_ref, da_ref, d_ref, sums_ref = refs[1:] if chained else refs
    y = y_ref[...]
    result_ref[...] = (y + z_ref[...] + vt_ref[7:8, :]).astype(BF)
    unit, inverse = unit_rows(y)
    dz = dz_ref[...].astype(F32)
    dn = dn_ref[...]
    dy = dz + norm_back(dn, unit, inverse, vt_ref[5:6, :])
    dy_ref[...] = dy
    da = dy.astype(BF)
    da_ref[...] = da
    d_ref[...] = mm_nt(w_ref[...], da).astype(BF).reshape(d_ref.shape)
    total = lambda a: jnp.sum(a, axis=0, keepdims=True)
    rest = jnp.zeros((4, y.shape[1]), F32)
    sums = jnp.concatenate([total(da.astype(F32)), total(dn * unit), total(dn), total(dz), rest], axis=0)

    @pl.when(pl.program_id(0) == 0)
    def _():
        sums_ref[...] = sums

    @pl.when(pl.program_id(0) > 0)
    def _():
        sums_ref[...] += sums


def turn(info, start, count, micros, y, z, dn, dz, w_out, vt, results):
    width = dz.shape[1]
    tokens = dz.shape[0] // micros
    hw = width // 4
    block = pl.BlockSpec((tokens, width), lambda i: (start + i, 0))
    rows = pl.BlockSpec((tokens, width), lambda i: (i, 0))
    outs = (
        shape((micros, tokens, width)),
        shape((count * tokens, width), F32),
        shape((count * tokens, width)),
        shape((4, count, hw, tokens)),
        shape((8, width), F32),
    )
    chained = results is not None
    return local_kernel(
        functools.partial(turn_body, chained), outs, "turn",
        2 * count * tokens * width, 2 * count * tokens, 0,
        grid=(count,),
        in_specs=[smem(), block, block, block, block, whole(w_out.shape), whole(vt.shape)]
        + ([anywhere()] if chained else []),
        out_specs=(stepped(outs[0], start), rows, rows, quarters(outs[3]), whole((8, width))),
        input_output_aliases={7: 0} if chained else {},
    )(info, y, z, dn, dz, w_out, vt, *((results,) if chained else ()))


def outproj_body(fast, info_ref, c_ref, *refs):
    outs, scratch = refs[:-1][-3 if fast else -1 :], refs[-1]
    das = refs[: -4 if fast else -2]
    at, y = info_ref[0], info_ref[1]
    da = jnp.concatenate([d[...] for d in das], axis=0)
    rows, micros = scratch.shape[0], c_ref.shape[1]
    left = jnp.concatenate([c_ref[:, m].reshape(rows, c_ref.shape[3]) for m in range(micros)], axis=1)
    scratch[...] = mm(left, da)
    if not fast:
        outs[0][...] = scratch[...]
        return
    keep, keep_other, send = outs
    nz, part, half = keep.shape
    first = lax.rem(at, 2) == 0
    for z in range(nz):
        for n in range(2):
            i = 2 * z + (y if n == 0 else 1 - y)
            block = scratch[pl.ds(pl.multiple_of(i * part, 16), part), :].astype(BF)
            left, right = block[:, :half], block[:, half:]
            (keep, keep_other)[n][z] = jnp.where(first, left, right)
            send[n, z] = jnp.where(first, right, left)


def outproj_grad(fast, info, c, das, nz, part):
    width = das[0].shape[1]
    total = sum(d.shape[0] for d in das)
    if fast:
        one = shape((nz, part, width // 2))
        outs = (one, one, shape((2, nz, part, width // 2)))
    else:
        outs = (shape((width, width), F32),)
    return local_kernel(
        functools.partial(outproj_body, fast), outs, "outproj_grad",
        2 * total * width * width, 6 * width * width, 0,
        in_specs=[smem()] + [vmem()] * (1 + len(das)),
        out_specs=(vmem(),) * len(outs),
        scratch_shapes=[pltpu.VMEM((width, width), F32)],
    )(info, c, *das)


def backward_body(first, last, micro, info_ref, ranges_ref, *refs):
    refs = list(refs)
    take = lambda n: [refs.pop(0) for _ in range(n)]
    d_ref, c_ref = take(2)
    xs = take(4)
    q_ref, k_ref, v_ref, lse_ref, seg_ref, w_ref, vt_ref = take(7)
    acc_in, sums_in = (None, None) if first else take(2)
    turned, biases = (take(2), take(2)) if last else ((), ())
    acc_ref, sums_ref, dn0_ref, dn2_ref, dn13_ref = take(5)
    dk_s, dv_s, dp_s, seg_s, dc_s, delta_s, kt_s, n1_s = take(8)
    x_s, w_s, acc_s, dn_s, sem_in, sem_out = take(6)
    loads = [pltpu.make_async_copy(x.at[micro], x_s.at[k], sem_in.at[k]) for k, x in enumerate(xs)]
    loads.append(pltpu.make_async_copy(w_ref, w_s, sem_in.at[4]))
    if not first:
        loads.append(pltpu.make_async_copy(acc_in, acc_s, sem_in.at[5]))
    for load in loads:
        load.start()
    at = info_ref[0]
    _, hw, tokens = d_ref.shape
    heads = hw // HEAD_DIM
    seg_s[...] = jnp.broadcast_to(seg_ref[...].astype(F32), (128, seg_ref.shape[1])).T
    dk_s[...] = jnp.zeros(dk_s.shape, F32)
    dv_s[...] = jnp.zeros(dv_s.shape, F32)
    kt_s[...] = k_ref[...].astype(F32).T.astype(BF)
    for b in range(4):
        dct = d_ref[b].astype(F32)
        dc_s[b] = dct.T.astype(BF)
        product = dct * c_ref[b].astype(F32)
        for h in range(heads):
            delta_s[b, h : h + 1, :] = jnp.sum(product[h * HEAD_DIM : (h + 1) * HEAD_DIM], axis=0, keepdims=True)

    def block(b, carry):
        rows = pl.ds(pl.multiple_of(b * tokens, 128), tokens)
        queries = heads_apart(q_ref[rows, :], heads)
        contexts = heads_apart(dc_s[b], heads)
        seg_row = seg_ref[0:1, rows].astype(F32)
        log_sum = jnp.concatenate([lse_ref[h : h + 1, rows] for h in range(heads)], axis=1)
        delta = jnp.concatenate([delta_s[b, h : h + 1, :] for h in range(heads)], axis=1)

        def body(span):
            bias = jnp.where(seg_s[span, 0:1] == seg_row, 0.0, MASKED)
            scores = mm_nt(k_ref[span, :], queries) + jnp.concatenate([bias] * heads, axis=1)
            p = jnp.exp(scores - log_sum)
            g = (p * (mm_nt(v_ref[span, :], contexts) - delta)).astype(BF)
            dk_s[span, :] += mm(g, queries)
            dv_s[span, :] += mm(p.astype(BF), contexts)
            dq = jnp.concatenate(own_blocks(mm(kt_s[:, span], g), heads), axis=0).T.astype(BF)
            dp_s[rows, 0:hw] = (dq.astype(F32) * 0.125).astype(BF)

        for_window(ranges_ref, 4 * micro + b, tokens, body)
        return carry

    lax.fori_loop(0, 4, block, 0)
    dp_s[:, hw : 2 * hw] = dk_s[...].astype(BF)
    dp_s[:, 2 * hw : 3 * hw] = dv_s[...].astype(BF)
    total = lambda a: jnp.sum(a, axis=0, keepdims=True)
    for load in loads:
        load.wait()
    dg1 = ds1 = None
    outs = (dn0_ref, dn13_ref.at[pl.ds(0, tokens)], dn2_ref, dn13_ref.at[pl.ds(tokens, tokens)])
    stores = [pltpu.make_async_copy(dn_s.at[k], out, sem_out.at[k]) for k, out in enumerate(outs)]
    for k in range(4):
        rows = pl.ds(pl.multiple_of((at ^ k) * tokens, 128), tokens)
        unit, _ = unit_rows(x_s[k].astype(F32))
        n1_s[rows, :] = (unit * vt_ref[0:1, :] + vt_ref[1:2, :]).astype(BF)
        dn1 = mm_nt(dp_s[rows, :], w_s[:, : 3 * hw])
        a, b = total(dn1 * unit), total(dn1)
        dg1, ds1 = (a, b) if k == 0 else (dg1 + a, ds1 + b)
        dn_s[k] = dn1.astype(BF)
        stores[k].start()
    acc = mm_tn(n1_s[...], dp_s[...])
    acc = acc if first else acc_s[...] + acc
    dbq, dbv = (total(dp_s[:, n * hw : (n + 1) * hw].astype(F32)) for n in (0, 2))
    spread = lambda r: jnp.concatenate([jnp.where(at == s, r, 0.0) for s in range(4)], axis=1)
    sums = jnp.concatenate([dg1, ds1, spread(dbq), spread(dbv), jnp.zeros((4, dg1.shape[1]), F32)], axis=0)
    sums = sums if first else sums_in[...] + sums
    sums_ref[...] = sums
    if not last:
        acc_ref[...] = acc
        for store in stores:
            store.wait()
        return
    width = acc.shape[0]
    rest = turned[0][...] + turned[1][...]
    chunk_rows = [biases[k // 2][k % 2 : k % 2 + 1, :] for k in range(4)]
    lines = [sums[0:4], rest[0:4]] + [pick(at ^ s, chunk_rows) for s in range(4)]
    lines = jnp.concatenate(lines + [jnp.zeros((116, width), F32)], axis=0)
    full = jnp.concatenate([acc, lines.T[:, 0:64]], axis=1)
    acc_ref[...] = full.astype(acc_ref.dtype).reshape(acc_ref.shape)
    for store in stores:
        store.wait()


def backward(info, ranges, micro, d, d_at, c, xs, kept, seg, w, vt, carried, ends):
    q, k, v, lse = kept
    hw, tokens = d.shape[2:]
    length, width = k.shape[1], w.shape[0]
    first, last = carried is None, bool(ends)
    outs = (
        ends[-1] if last else shape((width, 3 * hw), F32),
        shape((8, width), F32),
        shape((tokens, width)),
        shape((tokens, width)),
        shape((2 * tokens, width)),
    )
    rest = (w, vt, *(() if first else carried), *ends[:-1])
    stacked = (*xs, q, k, v, lse, seg)
    specs = [smem(), smem(), quarters(d, d_at), quarters(c, micro)] + [anywhere()] * 4
    specs += [picked(a, micro) for a in stacked[4:]] + [anywhere(), whole(vt.shape)]
    specs += [] if first else [anywhere(), whole(carried[1].shape)]
    specs += [whole(a.shape) for a in ends[:-1]]
    flops = 4 * length * width * 3 * hw + 40 * length * length * hw
    return local_kernel(
        functools.partial(backward_body, first, last, micro), outs, "attention_backward",
        flops, 8 * length * width * 2, 3 * length * length,
        grid=(1,),
        in_specs=specs,
        out_specs=tuple(whole(o.shape) for o in outs[:2]) + (anywhere(),) * 3,
        scratch_shapes=[
            pltpu.VMEM((length, hw), F32),
            pltpu.VMEM((length, hw), F32),
            pltpu.VMEM((length, 3 * hw), BF),
            pltpu.VMEM((length, 128), F32),
            pltpu.VMEM((4, tokens, hw), BF),
            pltpu.VMEM((4, 8, tokens), F32),
            pltpu.VMEM((hw, length), BF),
            pltpu.VMEM((length, width), BF),
            pltpu.VMEM((4, tokens, width), BF),
            pltpu.VMEM(w.shape, BF),
            pltpu.VMEM((8, 128) if first else (width, 3 * hw), F32),
            pltpu.VMEM((4, tokens, width), BF),
            pltpu.SemaphoreType.DMA((6,)),
            pltpu.SemaphoreType.DMA((4,)),
        ],
    )(info, ranges, d, c, *stacked, *rest)


def finish_body(chained, a_ref, b_ref, r_ref, dy_ref, x_ref, vt_ref, *refs):
    gx_ref = refs[-1]
    unit, inverse = unit_rows(x_ref[...].astype(F32))
    dn1 = a_ref[...].astype(F32) + b_ref[...].astype(F32) + r_ref[...].astype(F32)
    gx_ref[...] = dy_ref[...] + norm_back(dn1, unit, inverse, vt_ref[0:1, :])


def finish(micro, a, b, r, dy, dy_at, inputs, vt, grads):
    tokens, width = a.shape
    chained = grads is not None
    out = shape(inputs.shape, F32)
    top = pl.BlockSpec((tokens, width), lambda i: (0, 0))
    return local_kernel(
        functools.partial(finish_body, chained), out, "finish", a.shape[0], a.shape[0], 0,
        grid=(1,),
        in_specs=[top, top, top, pl.BlockSpec((tokens, width), lambda i: (dy_at, 0)), picked(inputs, micro), whole(vt.shape)] + ([anywhere()] if chained else []),
        out_specs=picked(out, micro),
        input_output_aliases={6: 0} if chained else {},
    )(a, b, r, dy, inputs, vt, *((grads,) if chained else ()))


def split_body(count, info_ref, *refs):
    ins, outs = refs[:count], refs[count:]
    nz = len(outs)
    for d in range(nz):
        at = lax.rem(info_ref[2] + nz - d, nz)
        total = ins[0][at].astype(F32)
        for r in ins[1:]:
            total = total + r[at].astype(F32)
        outs[d][...] = total.astype(BF)


def split(info, terms):
    nz, *dims = terms[-1].shape
    dims = tuple(dims)
    return local_kernel(
        functools.partial(split_body, len(terms)), (shape(dims),) * nz, "split",
        0, 2 * (len(terms) + 1) * nz * math.prod(dims), 0,
        grid=(1,),
        in_specs=[smem()] + [whole(t.shape) for t in terms],
        out_specs=(whole(dims),) * nz,
    )(info, *terms)


def block_sum(ref):
    return functools.reduce(jnp.add, [ref[n].astype(F32) for n in range(ref.shape[0])])


def collect_body(up_ref, down_ref, out_ref):
    rows = up_ref.shape[1]
    out_ref[:rows] = block_sum(up_ref).astype(BF)
    out_ref[rows:] = block_sum(down_ref).astype(BF)


def collect(up, rest):
    nz, rows, width = up.shape
    first = pl.BlockSpec(up.shape, lambda i: (0, 0, 0))
    return local_kernel(
        collect_body, shape((2 * rows, width)), "collect", 0, 20 * rows * width, 0,
        grid=(1,),
        in_specs=[first, first],
        out_specs=whole((2 * rows, width)),
    )(up, rest)


def assemble_mlp_body(info_ref, *refs):
    ms, (gu_ref, gd_ref, all_s) = refs[:-3], refs[-3:]
    at = info_ref[0]
    for k, r in enumerate(ms):
        all_s[at ^ k] = r[...]
    rows, part = gu_ref.shape[0], gd_ref.shape[0] // 4
    for s in range(4):
        up = all_s[s, 0:rows, :].astype(F32)
        for i in range(up.shape[1] // part):
            col = i * 4 * part + s * part
            gu_ref[:, col : col + part] = up[:, i * part : (i + 1) * part]
        gd_ref[s * part : (s + 1) * part, :] = all_s[s, rows : rows + part, :].astype(F32)


def assemble_mlp(info, ms, rows):
    width = ms[0].shape[1]
    part = ms[0].shape[0] - rows
    outs = (shape((rows, 4 * width), F32), shape((4 * part, width), F32))
    return local_kernel(
        assemble_mlp_body, outs, "assemble_mlp", 0, 12 * rows * width * 4, 0,
        in_specs=[smem()] + [vmem()] * 4,
        out_specs=(vmem(),) * 2,
        scratch_shapes=[pltpu.VMEM((4,) + ms[0].shape, BF)],
    )(info, *ms)


def share_body(q_ref, o_ref, out_ref):
    out_ref[...] = jnp.concatenate([block_sum(q_ref), block_sum(o_ref)], axis=1).astype(BF)


def share(q, rest, cols):
    nz, rows = rest.shape[:2]
    last = rest.shape[2] // cols - 1
    return local_kernel(
        share_body, shape((rows, q.shape[2] + cols)), "share", 0, 2 * (q.size + rest.size), 0,
        grid=(1,),
        in_specs=[whole(q.shape), pl.BlockSpec((nz, rows, cols), lambda i: (0, 0, last))],
        out_specs=whole((rows, q.shape[2] + cols)),
    )(q, rest)


def assemble_heads_body(q_ref, gq_ref, go_ref, gv_ref, gb_ref):
    hw = gq_ref.shape[1] // 12
    half = go_ref.shape[1] // 2
    for s in range(4):
        for n in range(3):
            base = n * 4 * hw + s * hw
            gq_ref[:, base : base + hw] = q_ref[s, :, n * hw : (n + 1) * hw].astype(F32)
    for h in range(2):
        a, b = (q_ref[h + 2 * n, :, 3 * hw + 64 :].astype(F32) for n in range(2))
        go_ref[:, h * half : (h + 1) * half] = a + b
    tail = (3 * hw) // 128 * 128
    off = 3 * hw - tail
    extra = functools.reduce(jnp.add, [q_ref[s, :, tail : tail + 128].astype(F32) for s in range(4)]).T
    gv_ref[...] = extra[off : off + 8]
    gb_ref[...] = extra[off + 8 : off + 12]


def assemble_heads(q, hw):
    rows = q.shape[1]
    outs = (
        shape((rows, 12 * hw), F32),
        shape((rows, 4 * hw), F32),
        shape((8, rows), F32),
        shape((4, rows), F32),
    )
    return local_kernel(
        assemble_heads_body, outs, "assemble_heads", 0, 12 * rows * hw * 16, 0,
        in_specs=[vmem()],
        out_specs=(vmem(),) * 4,
    )(q)


def send(x, axis, to):
    n = lax.axis_size(axis)
    return lax.ppermute(x, axis, [(s, to(s)) for s in range(n)])


def seq_swap(x, k):
    return send(x, "seq", lambda s: s ^ k)


def add(*terms):
    out = terms[0].astype(F32)
    for t in terms[1:]:
        out = out + t.astype(F32)
    return out.astype(BF)


def after(values, *others):
    out = lax.optimization_barrier((values, others))
    return out[0]


def shards(inputs, segments, cotangent, w_qkv, w_out, w_up, w_down, vectors, bias_up):
    micros, _, tokens, width = inputs.shape
    nf = lax.axis_size("fsdp")
    assert lax.axis_size("seq") == 4 and inputs.shape[1] == 1
    rows = w_qkv.shape[0]
    part = w_down.shape[0] // 4
    hw = width // 4
    nz = nf // 2
    fast = nf == 8 and rows % 32 == 0 and part == rows
    at = lax.axis_index("seq")
    me = lax.axis_index("fsdp")
    z, y = me // 2, me % 2
    info = jnp.stack([at, y, z]).astype(jnp.int32)
    y_swap = lambda x: send(x, "fsdp", lambda s: s ^ 1)
    z_pull = lambda x, d: send(x, "fsdp", lambda s: (s - 2 * d) % nf)
    pulled = lambda x: [x] + [z_pull(x, d) for d in range(1, nz)]

    ranges = windows(segments[:, 0], tokens)

    own = inputs[:, 0]
    across = seq_swap(own, 2)
    beside = seq_swap(own, 1)

    if fast:
        qkv_piece, mlp_piece, out_copies = local_kernel(
            prep_body,
            (shape((rows, 3 * hw + 64)), shape((rows + part, width)), shape((nf, rows // 2, width))),
            "prep", 0, 6 * rows * 4 * width, 0,
            in_specs=[smem()] + [vmem()] * 6,
            out_specs=(vmem(),) * 3,
        )(info, w_qkv, w_out, w_up, w_down, vectors.T, bias_up.reshape(4, part))
        w_heads = lax.all_gather(qkv_piece, "fsdp", axis=0, tiled=True)
        out_half = lax.all_to_all(
            after(out_copies, w_heads), "fsdp", split_axis=0, concat_axis=0, tiled=True
        )
        gathered = lax.all_gather(mlp_piece, ("fsdp", "seq"), axis=0, tiled=False)
    else:
        gather = lambda a: lax.all_gather(a, "fsdp", axis=0, tiled=True)
        by_head = gather(w_qkv).reshape(width, 3, 4, hw)
        mine = lax.dynamic_index_in_dim(by_head, at, 2, keepdims=False).reshape(width, 3 * hw)
        biases = gather(bias_up).reshape(nf, 4, part).transpose(0, 2, 1).reshape(width, 4)
        w_heads = jnp.concatenate([mine, gather(vectors), biases, jnp.zeros((width, 52), BF)], axis=1)
        w_out_full = gather(w_out)
        ups = gather(w_up).reshape(width, nf, 4, part).transpose(2, 0, 1, 3).reshape(4, width, width)
        downs = gather(w_down).reshape(nf, 4, part, width).transpose(1, 0, 2, 3).reshape(4, width, width)
        one = lambda a, k: lax.dynamic_index_in_dim(a, at ^ k, 0, keepdims=False)
        chunks = [(one(ups, k), one(downs, k)) for k in range(4)]

    xs = (own, beside, across, seq_swap(after(across, w_heads), 1))

    over_seq = lambda a: lax.all_to_all(a, "seq", split_axis=0, concat_axis=0, tiled=True)
    q, k, v, c, lse, vt = forward(info, ranges, xs, segments, w_heads)
    kept = (q, k, v, lse)
    contexts = over_seq(c)
    if fast:
        out_half = after(out_half, vt)
        y_rows, n2, w_out_full = middle(info, contexts, own, vt, (out_half, seq_swap(out_half, 1)))
        gathered = after(gathered, n2)
        weights_a = weights_b = [gathered]
    else:
        y_rows, n2 = middle(info, contexts, own, vt, (w_out_full,))
        weights_a, weights_b = [*chunks[0], *chunks[1]], [*chunks[2], *chunks[3]]

    dz = cotangent.reshape(micros * tokens, width)
    za, dna, *near_g, bias_a = mlp(fast, info, 0, n2, dz, vt, weights_a, None)
    if fast:
        near_own, near_oth = (seq_swap(a, 1) for a in near_g[2:])
        near_s = add(near_g[1], near_oth)
        near_y = y_swap(near_s)
        za, dna = after((za, dna), near_s)
    zb, dnb, *far_g, bias_b = mlp(fast, info, 2, n2, dz, vt, weights_b, (za, dna))

    results, dy_a, da_a, d_a, sums_a = turn(info, 0, 1, micros, y_rows, zb, dnb, dz, w_out_full, vt, None)
    d_a = over_seq(d_a)
    if fast:
        zb, dnb = after((zb, dnb), near_y)
    results, dy_b, da_b, d_b, sums_b = turn(
        info, 1, micros - 1, micros, y_rows, zb, dnb, dz, w_out_full, vt, results
    )
    d_b = over_seq(d_b)
    if fast:
        far_own, far_oth = (seq_swap(after(a, da_b), 1) for a in far_g[2:])
        over_near = lambda parts: [parts[0]] + [z_pull(parts[d], d) for d in range(1, nz)]
        far_part = lambda n: add(far_g[0][:, n], far_own[:, n], far_y[n])
        near_z = over_near(split(info, [near_g[0], near_own, near_y]))
        contexts = after(contexts, near_z[0])
    out_grads = outproj_grad(fast, info, contexts, (da_a, da_b), nz, rows)
    carried = None
    pending, settled, totals = [], [], []

    def settle(m, own_part, across_part, got, later):
        if later is not None:
            got = after(got, later)
        total = add(across_part, got[tokens:])
        settled.append((m, own_part, got, seq_swap(total, 2)))
        return total

    gate = ()
    if fast:
        groups_z = [list(range(n, nf, 2)) for n in range(2)]
        over_z = lambda a: lax.all_to_all(
            a, "fsdp", split_axis=0, concat_axis=0, tiled=True, axis_index_groups=groups_z
        )
        keep, keep_other, to_core = out_grads
        out_c = seq_swap(to_core, 1)
        far_own, far_oth = after((far_own, far_oth), keep)
        far_s = [add(far_g[1][:, n], far_oth[:, n]) for n in range(2)]
        far_y = [y_swap(a) for a in far_s]
        gate = (keep, *far_s)
    for m in range(micros):
        if fast and m == 1:
            far_y[0], out_c, near_z = after((far_y[0], out_c, near_z), dn0)
            out_s = add(keep_other, out_c[1])
            out_y = y_swap(out_s)
            far_up = far_part(0)
            far_up_z = over_z(far_up)
            gate = (far_up, out_s)
        if fast and m == 2:
            out_y, far_y[1], far_up_z, near_z = after((out_y, far_y[1], far_up_z, near_z), dn0)
            rest = jnp.concatenate([far_part(1), add(keep, out_c[0], out_y)], axis=2)
            rest_z = over_z(rest)
            near_sum = add(*near_z).reshape(rows + part, width)
            near_x = seq_swap(near_sum, 2)
            gate = (rest, near_sum)
        d, d_at = (d_a, 0) if m == 0 else (d_b, m - 1)
        last = m == micros - 1
        packed = shape((nf, rows, 3 * hw + 64)) if fast else shape((width, 3 * hw + 64), F32)
        ends = (sums_a, sums_b, bias_a, bias_b, packed) if last else ()
        acc, sums, dn0, dn2, dn13 = backward(
            info, ranges, m, d, d_at, c, xs, kept, segments, after(w_heads, *gate), vt, carried, ends
        )
        carried = (acc, sums)
        pending.append((m, dn0, dn2, seq_swap(dn13, 1)))
        if m > 0:
            totals.append(settle(*pending.pop(0), dn0))
    if fast:
        acc = after(acc, rest_z, settled[0][3], near_x)
    last_total = settle(*pending.pop(0), None)
    if fast:
        far_sum = collect(far_up_z, rest_z)
        m, own_part, got, theirs = settled[0]
        settled[0] = (m, after(own_part, far_sum, last_total, *totals), got, theirs)
    grad_rows, rows_done = None, []
    for m, own_part, got, theirs in settled:
        dy, dy_at = (dy_a, 0) if m == 0 else (dy_b, m - 1)
        grad_rows = finish(m, own_part, got, theirs, dy, dy_at, own, vt, grad_rows)
        rows_done.append(grad_rows)

    if fast:
        qkv_z = lax.all_to_all(acc, "fsdp", split_axis=0, concat_axis=0, tiled=True)
        mine = add(near_sum, after(seq_swap(far_sum, 2), rows_done[0]))
        theirs = add(near_x, far_sum)
        g_up, g_down = assemble_mlp(info, [mine, seq_swap(mine, 1), theirs, seq_swap(theirs, 1)], rows)
        qkv_z = after(qkv_z, grad_rows)
        heads_share = share(qkv_z, rest_z, width // 2)
        g_qkv, g_out, g_vec, g_bias = assemble_heads(lax.all_gather(heads_share, "seq", axis=0, tiled=False), hw)
        g_vec, g_bias = g_vec.T, g_bias.reshape(4 * part)
    else:
        total = lambda a: lax.psum(
            lax.psum_scatter(a.astype(F32), "fsdp", scatter_dimension=0, tiled=True), "seq"
        )
        head_place = lambda a: lax.dynamic_update_slice_in_dim(
            jnp.zeros((width, 3, 4, hw), F32), a.reshape(width, 3, 1, hw), at, 2
        ).reshape(width, 12 * hw)
        g_qkv = total(head_place(acc[:, : 3 * hw]))
        g_out = total(out_grads[0])
        extra = total(acc[:, 3 * hw :])
        g_vec, g_bias = extra[:, :8], extra[:, 8:12].T.reshape(4 * part)
        pairs = jnp.stack([*near_g, *far_g])
        order = lambda n: jnp.stack(
            [lax.dynamic_index_in_dim(pairs[:, n], at ^ s, 0, keepdims=False) for s in range(4)]
        )
        ups = order(0).reshape(4, width, nf, part).transpose(1, 2, 0, 3).reshape(width, 4 * width)
        downs = order(1).reshape(4, nf, part, width).transpose(1, 0, 2, 3).reshape(4 * width, width)
        g_up, g_down = total(ups), total(downs)
    return (
        results[:, None],
        grad_rows[:, None],
        g_qkv,
        g_out,
        g_up,
        g_down,
        g_vec,
        g_bias,
    )


def solution(mesh):
    rows = P(None, "fsdp", "seq", None)
    first = P("fsdp", None)
    in_specs = (rows, P(None, "fsdp", None), rows, first, first, first, first, first, P("fsdp"))
    out_specs = (rows, rows, first, first, first, first, first, P("fsdp"))
    return jax.shard_map(shards, mesh=mesh, in_specs=in_specs, out_specs=out_specs, check_vma=False)
```

```python
import functools
import math

import jax
import jax.numpy as jnp
from jax import lax
from jax.experimental import pallas as pl
from jax.experimental.pallas import tpu as pltpu
from jax.sharding import PartitionSpec as P

HEADS = 12
HEAD_DIM = 64
EPS = 1e-05
MASKED = -1e30
GELU_A = math.sqrt(2.0 / math.pi)
GELU_B = 0.044715
BF = jnp.bfloat16
F32 = jnp.float32
VMEM_LIMIT = 60 * 1024 * 1024


def shape(dims, dtype=BF):
    return jax.ShapeDtypeStruct(dims, dtype)


def vmem():
    return pl.BlockSpec(memory_space=pltpu.VMEM)


def smem():
    return pl.BlockSpec(memory_space=pltpu.SMEM)


def anywhere():
    return pl.BlockSpec(memory_space=pl.ANY)


def local_kernel(body, outs, name, flops=0, bytes_moved=0, exps=0, **kw):
    return pl.pallas_call(
        body,
        out_shape=outs,
        name=name,
        compiler_params=pltpu.CompilerParams(vmem_limit_bytes=VMEM_LIMIT),
        cost_estimate=pl.CostEstimate(
            flops=flops, bytes_accessed=bytes_moved, transcendentals=exps
        ),
        **kw,
    )


def mm(a, b):
    return lax.dot_general(a, b, (((1,), (0,)), ((), ())), preferred_element_type=F32)


def mm_nt(a, b):
    return lax.dot_general(a, b, (((1,), (1,)), ((), ())), preferred_element_type=F32)


def mm_tn(a, b):
    return lax.dot_general(a, b, (((0,), (0,)), ((), ())), preferred_element_type=F32)


def unit_rows(v):
    centred = v - jnp.mean(v, axis=-1, keepdims=True)
    inverse = lax.rsqrt(jnp.mean(centred * centred, axis=-1, keepdims=True) + EPS)
    return centred * inverse, inverse


def norm_back(grad, unit, inverse, gain):
    t = grad * gain
    first = jnp.mean(t, axis=-1, keepdims=True)
    second = jnp.mean(t * unit, axis=-1, keepdims=True)
    return inverse * (t - first - unit * second)


def pick(at, options):
    out = options[0]
    for s in range(1, len(options)):
        out = jnp.where(at == s, options[s], out)
    return out


def column_of(row, rows):
    return jnp.broadcast_to(row, (128, rows)).T[:, 0:1]


def prep_body(info_ref, wq_ref, wo_ref, up_ref, down_ref, vec_ref, bias_ref, qkv_ref, mlp_ref, out_ref):
    rows = wq_ref.shape[0]
    width = up_ref.shape[1] // 4
    hw = wq_ref.shape[1] // 12
    part = down_ref.shape[0] // 4
    for s in range(4):

        @pl.when(info_ref[0] == s)
        def _(s=s):
            for n in range(3):
                base = n * 4 * hw + s * hw
                qkv_ref[:, n * hw : (n + 1) * hw] = wq_ref[:, base : base + hw]
            for i in range(width // part):
                col = i * 4 * part + s * part
                mlp_ref[0:rows, i * part : (i + 1) * part] = up_ref[:, col : col + part]
            mlp_ref[rows : rows + part, :] = down_ref[s * part : (s + 1) * part, :]
            for n in range(out_ref.shape[0]):
                out_ref[n] = wo_ref[s % 2 * (rows // 2) : (s % 2 + 1) * (rows // 2), :]

    lines = jnp.concatenate([vec_ref[...].astype(F32), bias_ref[...].astype(F32)], axis=0)
    lines = jnp.concatenate([lines, jnp.zeros((128 - lines.shape[0], rows), F32)], axis=0)
    qkv_ref[:, 3 * hw : 3 * hw + 64] = lines.T[:, 0:64].astype(BF)


def windows(segments, block):
    length = segments.shape[-1]
    first, last = segments[:, ::block, None], segments[:, block - 1 :: block, None]
    low = jnp.sum(segments[:, None, :] < first, axis=-1)
    high = jnp.sum(segments[:, None, :] <= last, axis=-1)
    low = low // 128 * 128
    count = (high - low + block - 1) // block
    start = jnp.minimum(low, length - count * block)
    return jnp.stack([start, count], axis=-1).astype(jnp.int32).reshape(-1)


def for_window(ranges_ref, at, block, body):
    start = pl.multiple_of(ranges_ref[2 * at], 128)
    for size in range(1, 5):

        @pl.when(ranges_ref[2 * at + 1] == size)
        def _(size=size):
            body(pl.ds(start, size * block))


def heads_apart(rows, heads):
    lane_head = lax.broadcasted_iota(jnp.int32, (1, rows.shape[1]), 1) // HEAD_DIM
    return jnp.concatenate([jnp.where(lane_head == h, rows, 0).astype(BF) for h in range(heads)], axis=0)


def own_blocks(wide, heads):
    width = wide.shape[1] // heads
    return [
        wide[h * HEAD_DIM : (h + 1) * HEAD_DIM, h * width : (h + 1) * width] for h in range(heads)
    ]


def picked(array, at):
    if array.ndim == 2:
        return pl.BlockSpec(array.shape, lambda i: (0, 0))
    return pl.BlockSpec((None,) + array.shape[1:], lambda i: (at,) + (0,) * (array.ndim - 1))


def whole(dims):
    return pl.BlockSpec(dims, lambda i: (0,) * len(dims))


def forward_body(info_ref, ranges_ref, x0, x1, x2, x3, seg_ref, w_ref, *refs):
    q_ref, k_ref, v_ref, c_ref, lse_ref, vt_ref, n1_ref, vtr_ref, seg_s = refs
    at = info_ref[0]
    micro = pl.program_id(0)
    tokens, width = x0.shape
    hw = q_ref.shape[1]
    heads = hw // HEAD_DIM
    tail = (3 * hw) // 128 * 128
    off = 3 * hw - tail
    vt_ref[...] = w_ref[:, tail : tail + 128].astype(F32).T[off : off + 16]
    g1, s1 = vt_ref[0:1, :], vt_ref[1:2, :]
    bq = pick(at, [vt_ref[2:3, s * hw : (s + 1) * hw] for s in range(4)])
    bv = pick(at, [vt_ref[3:4, s * hw : (s + 1) * hw] for s in range(4)])
    seg_s[...] = jnp.broadcast_to(seg_ref[...].astype(F32), (128, seg_ref.shape[1])).T
    for k, x_ref in enumerate((x0, x1, x2, x3)):
        unit, _ = unit_rows(x_ref[...].astype(F32))
        n1_ref[pl.ds(pl.multiple_of((at ^ k) * tokens, 128), tokens), :] = (unit * g1 + s1).astype(BF)
    project = mm(n1_ref[...], w_ref[:, : 3 * hw])
    q_ref[...] = ((project[:, :hw] + bq) * 0.125).astype(BF)
    keys = project[:, hw : 2 * hw]
    k_ref[...] = keys.astype(BF)
    values = project[:, 2 * hw : 3 * hw] + bv
    v_ref[...] = values.astype(BF)
    vtr_ref[...] = values.T.astype(BF)
    lse_ref[...] = jnp.zeros(lse_ref.shape, F32)

    def block(b, carry):
        rows = pl.ds(pl.multiple_of(b * tokens, 128), tokens)
        queries = heads_apart(q_ref[rows, :], heads)
        seg_row = seg_ref[0:1, rows].astype(F32)

        def body(span):
            bias = jnp.where(seg_s[span, 0:1] == seg_row, 0.0, MASKED)
            scores = mm_nt(k_ref[span, :], queries) + jnp.concatenate([bias] * heads, axis=1)
            top = jnp.max(scores, axis=0, keepdims=True)
            raised = jnp.exp(scores - top)
            total = jnp.sum(raised, axis=0, keepdims=True)
            context = mm(vtr_ref[:, span], raised.astype(BF)) * (1.0 / total)
            c_ref[b] = jnp.concatenate(own_blocks(context, heads), axis=0).astype(BF)
            log_sum = top + jnp.log(total)
            for h in range(heads):
                lse_ref[h : h + 1, rows] = log_sum[:, h * tokens : (h + 1) * tokens]

        for_window(ranges_ref, 4 * micro + b, tokens, body)
        return carry

    lax.fori_loop(0, 4, block, 0)


def quarters(array, at=None):
    dims = (array.shape[0], None) + array.shape[2:]
    return pl.BlockSpec(dims, (lambda i: (0, i, 0, 0)) if at is None else (lambda i: (0, at, 0, 0)))


def forward(info, ranges, xs, seg, w):
    micros, tokens, width = xs[0].shape
    hw = width // 4
    length = 4 * tokens
    outs = (
        shape((micros, length, hw)),
        shape((micros, length, hw)),
        shape((micros, length, hw)),
        shape((4, micros, hw, tokens)),
        shape((micros, 8, length), F32),
        shape((16, width), F32),
    )
    flops = micros * (2 * length * width * 3 * hw + 16 * length * length * hw)
    return local_kernel(
        forward_body, outs, "attention_forward",
        flops, micros * 4 * length * width * 2, micros * 3 * length * length,
        grid=(micros,),
        in_specs=[smem(), smem()] + [stepped(a) for a in (*xs, seg)] + [whole(w.shape)],
        out_specs=tuple(quarters(o) if n == 3 else stepped(o) for n, o in enumerate(outs)),
        scratch_shapes=[
            pltpu.VMEM((length, width), BF),
            pltpu.VMEM((hw, length), BF),
            pltpu.VMEM((length, 128), F32),
        ],
    )(info, ranges, *xs, seg, w)


def stepped(array, start=0):
    if array.ndim == 2:
        return whole(array.shape)
    return pl.BlockSpec((None,) + array.shape[1:], lambda i: (start + i,) + (0,) * (array.ndim - 1))


def middle_body(halves, info_ref, c_ref, x_ref, vt_ref, *refs):
    if halves:
        mine, theirs, y_ref, n2_ref, w_ref, sem = refs

        @pl.when(pl.program_id(0) == 0)
        def _():
            count, part = mine.shape[:2]
            core = lax.rem(info_ref[0], 2)
            copies = []
            for n, src in enumerate((mine, theirs)):
                for i in range(count):
                    dest = pl.multiple_of(i * 2 * part + (core if n == 0 else 1 - core) * part, 16)
                    copies.append(
                        pltpu.make_async_copy(src.at[i], w_ref.at[pl.ds(dest, part), :], sem.at[n * count + i])
                    )
            for c in copies:
                c.start()
            for c in copies:
                c.wait()
    else:
        w_ref, y_ref, n2_ref = refs
    context = c_ref[...].reshape(w_ref.shape[0], c_ref.shape[2])
    y = x_ref[...].astype(F32) + vt_ref[4:5, :] + mm_tn(context, w_ref[...])
    y_ref[...] = y
    unit, _ = unit_rows(y)
    n2_ref[...] = (unit * vt_ref[5:6, :] + vt_ref[6:7, :]).astype(BF)


def middle(info, c, inputs, vt, ws):
    micros, tokens, width = inputs.shape
    halves = len(ws) == 2
    outs = (shape((micros * tokens, width), F32), shape((micros * tokens, width)))
    outs += (shape((width, width)),) if halves else ()
    rows = pl.BlockSpec((tokens, width), lambda i: (i, 0))
    return local_kernel(
        functools.partial(middle_body, halves), outs, "middle",
        2 * micros * tokens * width * width, 12 * micros * tokens * width, 0,
        grid=(micros,),
        in_specs=[smem(), quarters(c), stepped(inputs), whole(vt.shape)]
        + ([anywhere()] * 2 if halves else [whole(ws[0].shape)]),
        out_specs=(rows, rows) + ((whole((width, width)),) if halves else ()),
        scratch_shapes=[pltpu.SemaphoreType.DMA((2 * ws[0].shape[0],))] if halves else [],
    )(info, c, inputs, vt, *ws)


def mlp_body(fast, first, lead, info_ref, *refs):
    refs = list(refs)
    take = lambda n: [refs.pop(0) for _ in range(n)]
    n2_ref, dz_ref, vt_ref = take(3)
    weights = take(1 if fast else 4)
    z_in, dn_in = (None, None) if first else take(2)
    z_ref, dn_ref = take(2)
    sides = 2 if fast else 1
    grads = take(2 * sides)
    (bias_ref,) = take(1)
    wu_s, wd_s, n2t_s, g_s, sem_w, sem_g = take(6)
    if not first:
        za_s, dna_s, sem_a = take(3)
        carried = [
            pltpu.make_async_copy(z_in, za_s, sem_a.at[0]),
            pltpu.make_async_copy(dn_in, dna_s, sem_a.at[1]),
        ]
    step = pl.program_id(0)
    width = n2_ref.shape[1]
    y = info_ref[1]
    results = [
        pltpu.make_async_copy(g_s.at[n // sides, n % sides], grads[n], sem_g.at[n]) for n in range(2 * sides)
    ]

    @pl.when(step == 0)
    def _():
        for ch in range(2):
            if fast:
                src = weights[0]
                count = src.shape[0] // 4
                rank = info_ref[0] ^ (lead + ch)
                rows = width // count
                for i in range(count):
                    for n, dest in enumerate((wu_s, wd_s)):
                        pltpu.make_async_copy(
                            src.at[4 * i + rank, pl.ds(n * rows, rows), :],
                            dest.at[ch, pl.ds(i * rows, rows), :],
                            sem_w.at[2 * ch + n],
                        ).start()
            else:
                for n, dest in enumerate((wu_s, wd_s)):
                    pltpu.make_async_copy(weights[2 * ch + n], dest.at[ch], sem_w.at[2 * ch + n]).start()
        if not first:
            for c in carried:
                c.start()
        n2t_s[...] = n2_ref[...].T
        bias_ref[...] = jnp.zeros(bias_ref.shape, F32)

    for n, dest in enumerate((wu_s, wd_s)):
        pltpu.make_async_copy(dest.at[step], dest.at[step], sem_w.at[2 * step + n]).wait()
    wu, wd = wu_s[step], wd_s[step]
    bias = vt_ref[pl.ds(8 + (info_ref[0] ^ (lead + step)), 1), :]
    u = mm(n2_ref[...], wu) + bias
    square = u * u
    t = jnp.tanh(GELU_A * u * (1.0 + GELU_B * square))
    f = (0.5 * u * (1.0 + t)).astype(BF)
    slope = 0.5 * (1.0 + t) + (0.5 * GELU_A) * u * (1.0 - t * t) * (1.0 + 3.0 * GELU_B * square)
    dz = dz_ref[...]
    du = (mm_nt(dz, wd) * slope).astype(BF)
    bias_ref[pl.ds(step, 1), :] = jnp.sum(du.astype(F32), axis=0, keepdims=True)
    grad_up = mm(n2t_s[...], du).astype(BF)
    grad_down = mm_tn(f, dz).astype(BF)
    if fast:
        count = 2 * g_s.shape[2]
        rows = width // count
        for yy in range(2):

            @pl.when(y == yy)
            def _(yy=yy):
                for i in range(count):
                    g_s[step, int(i % 2 != yy), i // 2, 0] = grad_up[i * rows : (i + 1) * rows]
                    g_s[step, int(i % 2 != yy), i // 2, 1] = grad_down[i * rows : (i + 1) * rows]
    else:
        g_s[step, 0, 0] = grad_up
        g_s[step, 0, 1] = grad_down
    for ch in range(2):

        @pl.when(step == ch)
        def _(ch=ch):
            for r in results[ch * sides : (ch + 1) * sides]:
                r.start()

    z, dn = mm(f, wd), mm_nt(du, wu)

    @pl.when(step == 0)
    def _():
        z_ref[...] = z
        dn_ref[...] = dn

    @pl.when(step == 1)
    def _():
        if first:
            z_ref[...] += z
            dn_ref[...] += dn
        else:
            for c in carried:
                c.wait()
            z_ref[...] += z + za_s[...]
            dn_ref[...] += dn + dna_s[...]
        for r in results:
            r.wait()


def mlp(fast, info, lead, n2, dz, vt, weights, carried):
    first = carried is None
    tokens, width = dz.shape
    acc = shape((tokens, width), F32)
    nf = weights[0].shape[0] // 4
    sides, one = (2, (nf // 2, 2, width // nf, width)) if fast else (1, (2, width, width))
    outs = (acc, acc, *(shape(one),) * (2 * sides), shape((8, width), F32))
    ins = (info, n2, dz, vt, *weights, *(() if first else carried))
    specs = [smem()] + [whole(a.shape) for a in (n2, dz, vt)] + [anywhere()] * len(weights)
    specs += [] if first else [anywhere()] * 2
    more = [] if first else [
        pltpu.VMEM((tokens, width), F32),
        pltpu.VMEM((tokens, width), F32),
        pltpu.SemaphoreType.DMA((2,)),
    ]
    return local_kernel(
        functools.partial(mlp_body, fast, first, lead), outs, "feed_forward",
        24 * tokens * width * width, 30 * tokens * width, 2 * tokens * width,
        grid=(2,),
        in_specs=specs,
        out_specs=(whole(acc.shape),) * 2 + (anywhere(),) * (2 * sides) + (whole((8, width)),),
        scratch_shapes=[
            pltpu.VMEM((2, width, width), BF),
            pltpu.VMEM((2, width, width), BF),
            pltpu.VMEM((width, tokens), BF),
            pltpu.VMEM((2, sides) + one, BF),
            pltpu.SemaphoreType.DMA((4,)),
            pltpu.SemaphoreType.DMA((2 * sides,)),
            *more,
        ],
    )(*ins)


def turn_body(chained, info_ref, y_ref, z_ref, dn_ref, dz_ref, w_ref, vt_ref, *refs):
    result_ref, dy_ref, da_ref, d_ref, sums_ref = refs[1:] if chained else refs
    y = y_ref[...]
    result_ref[...] = (y + z_ref[...] + vt_ref[7:8, :]).astype(BF)
    unit, inverse = unit_rows(y)
    dz = dz_ref[...].astype(F32)
    dn = dn_ref[...]
    dy = dz + norm_back(dn, unit, inverse, vt_ref[5:6, :])
    dy_ref[...] = dy
    da = dy.astype(BF)
    da_ref[...] = da
    d_ref[...] = mm_nt(w_ref[...], da).astype(BF).reshape(d_ref.shape)
    total = lambda a: jnp.sum(a, axis=0, keepdims=True)
    rest = jnp.zeros((4, y.shape[1]), F32)
    sums = jnp.concatenate([total(da.astype(F32)), total(dn * unit), total(dn), total(dz), rest], axis=0)

    @pl.when(pl.program_id(0) == 0)
    def _():
        sums_ref[...] = sums

    @pl.when(pl.program_id(0) > 0)
    def _():
        sums_ref[...] += sums


def turn(info, start, count, micros, y, z, dn, dz, w_out, vt, results):
    width = dz.shape[1]
    tokens = dz.shape[0] // micros
    hw = width // 4
    block = pl.BlockSpec((tokens, width), lambda i: (start + i, 0))
    rows = pl.BlockSpec((tokens, width), lambda i: (i, 0))
    outs = (
        shape((micros, tokens, width)),
        shape((count * tokens, width), F32),
        shape((count * tokens, width)),
        shape((4, count, hw, tokens)),
        shape((8, width), F32),
    )
    chained = results is not None
    return local_kernel(
        functools.partial(turn_body, chained), outs, "turn",
        2 * count * tokens * width, 2 * count * tokens, 0,
        grid=(count,),
        in_specs=[smem(), block, block, block, block, whole(w_out.shape), whole(vt.shape)]
        + ([anywhere()] if chained else []),
        out_specs=(stepped(outs[0], start), rows, rows, quarters(outs[3]), whole((8, width))),
        input_output_aliases={7: 0} if chained else {},
    )(info, y, z, dn, dz, w_out, vt, *((results,) if chained else ()))


def outproj_body(fast, info_ref, c_ref, *refs):
    outs, scratch = refs[:-1][-3 if fast else -1 :], refs[-1]
    das = refs[: -4 if fast else -2]
    at, y = info_ref[0], info_ref[1]
    da = jnp.concatenate([d[...] for d in das], axis=0)
    rows, micros = scratch.shape[0], c_ref.shape[1]
    left = jnp.concatenate([c_ref[:, m].reshape(rows, c_ref.shape[3]) for m in range(micros)], axis=1)
    scratch[...] = mm(left, da)
    if not fast:
        outs[0][...] = scratch[...]
        return
    keep, keep_other, send = outs
    nz, part, half = keep.shape
    first = lax.rem(at, 2) == 0
    for z in range(nz):
        for n in range(2):
            i = 2 * z + (y if n == 0 else 1 - y)
            block = scratch[pl.ds(pl.multiple_of(i * part, 16), part), :].astype(BF)
            left, right = block[:, :half], block[:, half:]
            (keep, keep_other)[n][z] = jnp.where(first, left, right)
            send[n, z] = jnp.where(first, right, left)


def outproj_grad(fast, info, c, das, nz, part):
    width = das[0].shape[1]
    total = sum(d.shape[0] for d in das)
    if fast:
        one = shape((nz, part, width // 2))
        outs = (one, one, shape((2, nz, part, width // 2)))
    else:
        outs = (shape((width, width), F32),)
    return local_kernel(
        functools.partial(outproj_body, fast), outs, "outproj_grad",
        2 * total * width * width, 6 * width * width, 0,
        in_specs=[smem()] + [vmem()] * (1 + len(das)),
        out_specs=(vmem(),) * len(outs),
        scratch_shapes=[pltpu.VMEM((width, width), F32)],
    )(info, c, *das)


def backward_body(first, last, micro, info_ref, ranges_ref, *refs):
    refs = list(refs)
    take = lambda n: [refs.pop(0) for _ in range(n)]
    d_ref, c_ref = take(2)
    xs = take(4)
    q_ref, k_ref, v_ref, lse_ref, seg_ref, w_ref, vt_ref = take(7)
    acc_in, sums_in = (None, None) if first else take(2)
    turned, biases = (take(2), take(2)) if last else ((), ())
    acc_ref, sums_ref, dn0_ref, dn2_ref, dn13_ref = take(5)
    dk_s, dv_s, dp_s, seg_s, dc_s, delta_s, kt_s, n1_s = take(8)
    x_s, w_s, acc_s, dn_s, sem_in, sem_out = take(6)
    loads = [pltpu.make_async_copy(x.at[micro], x_s.at[k], sem_in.at[k]) for k, x in enumerate(xs)]
    loads.append(pltpu.make_async_copy(w_ref, w_s, sem_in.at[4]))
    if not first:
        loads.append(pltpu.make_async_copy(acc_in, acc_s, sem_in.at[5]))
    for load in loads:
        load.start()
    at = info_ref[0]
    _, hw, tokens = d_ref.shape
    heads = hw // HEAD_DIM
    seg_s[...] = jnp.broadcast_to(seg_ref[...].astype(F32), (128, seg_ref.shape[1])).T
    dk_s[...] = jnp.zeros(dk_s.shape, F32)
    dv_s[...] = jnp.zeros(dv_s.shape, F32)
    kt_s[...] = k_ref[...].astype(F32).T.astype(BF)
    for b in range(4):
        dct = d_ref[b].astype(F32)
        dc_s[b] = dct.T.astype(BF)
        product = dct * c_ref[b].astype(F32)
        for h in range(heads):
            delta_s[b, h : h + 1, :] = jnp.sum(product[h * HEAD_DIM : (h + 1) * HEAD_DIM], axis=0, keepdims=True)

    def block(b, carry):
        rows = pl.ds(pl.multiple_of(b * tokens, 128), tokens)
        queries = heads_apart(q_ref[rows, :], heads)
        contexts = heads_apart(dc_s[b], heads)
        seg_row = seg_ref[0:1, rows].astype(F32)
        log_sum = jnp.concatenate([lse_ref[h : h + 1, rows] for h in range(heads)], axis=1)
        delta = jnp.concatenate([delta_s[b, h : h + 1, :] for h in range(heads)], axis=1)

        def body(span):
            bias = jnp.where(seg_s[span, 0:1] == seg_row, 0.0, MASKED)
            scores = mm_nt(k_ref[span, :], queries) + jnp.concatenate([bias] * heads, axis=1)
            p = jnp.exp(scores - log_sum)
            g = (p * (mm_nt(v_ref[span, :], contexts) - delta)).astype(BF)
            dk_s[span, :] += mm(g, queries)
            dv_s[span, :] += mm(p.astype(BF), contexts)
            dq = jnp.concatenate(own_blocks(mm(kt_s[:, span], g), heads), axis=0).T.astype(BF)
            dp_s[rows, 0:hw] = (dq.astype(F32) * 0.125).astype(BF)

        for_window(ranges_ref, 4 * micro + b, tokens, body)
        return carry

    lax.fori_loop(0, 4, block, 0)
    dp_s[:, hw : 2 * hw] = dk_s[...].astype(BF)
    dp_s[:, 2 * hw : 3 * hw] = dv_s[...].astype(BF)
    total = lambda a: jnp.sum(a, axis=0, keepdims=True)
    for load in loads:
        load.wait()
    dg1 = ds1 = None
    outs = (dn0_ref, dn13_ref.at[pl.ds(0, tokens)], dn2_ref, dn13_ref.at[pl.ds(tokens, tokens)])
    stores = [pltpu.make_async_copy(dn_s.at[k], out, sem_out.at[k]) for k, out in enumerate(outs)]
    for k in range(4):
        rows = pl.ds(pl.multiple_of((at ^ k) * tokens, 128), tokens)
        unit, _ = unit_rows(x_s[k].astype(F32))
        n1_s[rows, :] = (unit * vt_ref[0:1, :] + vt_ref[1:2, :]).astype(BF)
        dn1 = mm_nt(dp_s[rows, :], w_s[:, : 3 * hw])
        a, b = total(dn1 * unit), total(dn1)
        dg1, ds1 = (a, b) if k == 0 else (dg1 + a, ds1 + b)
        dn_s[k] = dn1.astype(BF)
        stores[k].start()
    acc = mm_tn(n1_s[...], dp_s[...])
    acc = acc if first else acc_s[...] + acc
    dbq, dbv = (total(dp_s[:, n * hw : (n + 1) * hw].astype(F32)) for n in (0, 2))
    spread = lambda r: jnp.concatenate([jnp.where(at == s, r, 0.0) for s in range(4)], axis=1)
    sums = jnp.concatenate([dg1, ds1, spread(dbq), spread(dbv), jnp.zeros((4, dg1.shape[1]), F32)], axis=0)
    sums = sums if first else sums_in[...] + sums
    sums_ref[...] = sums
    if not last:
        acc_ref[...] = acc
        for store in stores:
            store.wait()
        return
    width = acc.shape[0]
    rest = turned[0][...] + turned[1][...]
    chunk_rows = [biases[k // 2][k % 2 : k % 2 + 1, :] for k in range(4)]
    lines = [sums[0:4], rest[0:4]] + [pick(at ^ s, chunk_rows) for s in range(4)]
    lines = jnp.concatenate(lines + [jnp.zeros((116, width), F32)], axis=0)
    full = jnp.concatenate([acc, lines.T[:, 0:64]], axis=1)
    acc_ref[...] = full.astype(acc_ref.dtype).reshape(acc_ref.shape)
    for store in stores:
        store.wait()


def backward(info, ranges, micro, d, d_at, c, xs, kept, seg, w, vt, carried, ends):
    q, k, v, lse = kept
    hw, tokens = d.shape[2:]
    length, width = k.shape[1], w.shape[0]
    first, last = carried is None, bool(ends)
    outs = (
        ends[-1] if last else shape((width, 3 * hw), F32),
        shape((8, width), F32),
        shape((tokens, width)),
        shape((tokens, width)),
        shape((2 * tokens, width)),
    )
    rest = (w, vt, *(() if first else carried), *ends[:-1])
    stacked = (*xs, q, k, v, lse, seg)
    specs = [smem(), smem(), quarters(d, d_at), quarters(c, micro)] + [anywhere()] * 4
    specs += [picked(a, micro) for a in stacked[4:]] + [anywhere(), whole(vt.shape)]
    specs += [] if first else [anywhere(), whole(carried[1].shape)]
    specs += [whole(a.shape) for a in ends[:-1]]
    flops = 4 * length * width * 3 * hw + 40 * length * length * hw
    return local_kernel(
        functools.partial(backward_body, first, last, micro), outs, "attention_backward",
        flops, 8 * length * width * 2, 3 * length * length,
        grid=(1,),
        in_specs=specs,
        out_specs=tuple(whole(o.shape) for o in outs[:2]) + (anywhere(),) * 3,
        scratch_shapes=[
            pltpu.VMEM((length, hw), F32),
            pltpu.VMEM((length, hw), F32),
            pltpu.VMEM((length, 3 * hw), BF),
            pltpu.VMEM((length, 128), F32),
            pltpu.VMEM((4, tokens, hw), BF),
            pltpu.VMEM((4, 8, tokens), F32),
            pltpu.VMEM((hw, length), BF),
            pltpu.VMEM((length, width), BF),
            pltpu.VMEM((4, tokens, width), BF),
            pltpu.VMEM(w.shape, BF),
            pltpu.VMEM((8, 128) if first else (width, 3 * hw), F32),
            pltpu.VMEM((4, tokens, width), BF),
            pltpu.SemaphoreType.DMA((6,)),
            pltpu.SemaphoreType.DMA((4,)),
        ],
    )(info, ranges, d, c, *stacked, *rest)


def finish_body(chained, a_ref, b_ref, r_ref, dy_ref, x_ref, vt_ref, *refs):
    gx_ref = refs[-1]
    unit, inverse = unit_rows(x_ref[...].astype(F32))
    dn1 = a_ref[...].astype(F32) + b_ref[...].astype(F32) + r_ref[...].astype(F32)
    gx_ref[...] = dy_ref[...] + norm_back(dn1, unit, inverse, vt_ref[0:1, :])


def finish(micro, a, b, r, dy, dy_at, inputs, vt, grads):
    tokens, width = a.shape
    chained = grads is not None
    out = shape(inputs.shape, F32)
    top = pl.BlockSpec((tokens, width), lambda i: (0, 0))
    return local_kernel(
        functools.partial(finish_body, chained), out, "finish", a.shape[0], a.shape[0], 0,
        grid=(1,),
        in_specs=[top, top, top, pl.BlockSpec((tokens, width), lambda i: (dy_at, 0)), picked(inputs, micro), whole(vt.shape)] + ([anywhere()] if chained else []),
        out_specs=picked(out, micro),
        input_output_aliases={6: 0} if chained else {},
    )(a, b, r, dy, inputs, vt, *((grads,) if chained else ()))


def split_body(count, info_ref, *refs):
    ins, outs = refs[:count], refs[count:]
    nz = len(outs)
    for d in range(nz):
        at = lax.rem(info_ref[2] + nz - d, nz)
        total = ins[0][at].astype(F32)
        for r in ins[1:]:
            total = total + r[at].astype(F32)
        outs[d][...] = total.astype(BF)


def split(info, terms):
    nz, *dims = terms[-1].shape
    dims = tuple(dims)
    return local_kernel(
        functools.partial(split_body, len(terms)), (shape(dims),) * nz, "split",
        0, 2 * (len(terms) + 1) * nz * math.prod(dims), 0,
        grid=(1,),
        in_specs=[smem()] + [whole(t.shape) for t in terms],
        out_specs=(whole(dims),) * nz,
    )(info, *terms)


def block_sum(ref):
    return functools.reduce(jnp.add, [ref[n].astype(F32) for n in range(ref.shape[0])])


def collect_body(up_ref, down_ref, out_ref):
    rows = up_ref.shape[1]
    out_ref[:rows] = block_sum(up_ref).astype(BF)
    out_ref[rows:] = block_sum(down_ref).astype(BF)


def collect(up, rest):
    nz, rows, width = up.shape
    first = pl.BlockSpec(up.shape, lambda i: (0, 0, 0))
    return local_kernel(
        collect_body, shape((2 * rows, width)), "collect", 0, 20 * rows * width, 0,
        grid=(1,),
        in_specs=[first, first],
        out_specs=whole((2 * rows, width)),
    )(up, rest)


def assemble_mlp_body(info_ref, *refs):
    ms, (gu_ref, gd_ref, all_s) = refs[:-3], refs[-3:]
    at = info_ref[0]
    for k, r in enumerate(ms):
        all_s[at ^ k] = r[...]
    rows, part = gu_ref.shape[0], gd_ref.shape[0] // 4
    for s in range(4):
        up = all_s[s, 0:rows, :].astype(F32)
        for i in range(up.shape[1] // part):
            col = i * 4 * part + s * part
            gu_ref[:, col : col + part] = up[:, i * part : (i + 1) * part]
        gd_ref[s * part : (s + 1) * part, :] = all_s[s, rows : rows + part, :].astype(F32)


def assemble_mlp(info, ms, rows):
    width = ms[0].shape[1]
    part = ms[0].shape[0] - rows
    outs = (shape((rows, 4 * width), F32), shape((4 * part, width), F32))
    return local_kernel(
        assemble_mlp_body, outs, "assemble_mlp", 0, 12 * rows * width * 4, 0,
        in_specs=[smem()] + [vmem()] * 4,
        out_specs=(vmem(),) * 2,
        scratch_shapes=[pltpu.VMEM((4,) + ms[0].shape, BF)],
    )(info, *ms)


def share_body(q_ref, o_ref, out_ref):
    out_ref[...] = jnp.concatenate([block_sum(q_ref), block_sum(o_ref)], axis=1).astype(BF)


def share(q, rest, cols):
    nz, rows = rest.shape[:2]
    last = rest.shape[2] // cols - 1
    return local_kernel(
        share_body, shape((rows, q.shape[2] + cols)), "share", 0, 2 * (q.size + rest.size), 0,
        grid=(1,),
        in_specs=[whole(q.shape), pl.BlockSpec((nz, rows, cols), lambda i: (0, 0, last))],
        out_specs=whole((rows, q.shape[2] + cols)),
    )(q, rest)


def assemble_heads_body(q_ref, gq_ref, go_ref, gv_ref, gb_ref):
    hw = gq_ref.shape[1] // 12
    half = go_ref.shape[1] // 2
    for s in range(4):
        for n in range(3):
            base = n * 4 * hw + s * hw
            gq_ref[:, base : base + hw] = q_ref[s, :, n * hw : (n + 1) * hw].astype(F32)
    for h in range(2):
        a, b = (q_ref[h + 2 * n, :, 3 * hw + 64 :].astype(F32) for n in range(2))
        go_ref[:, h * half : (h + 1) * half] = a + b
    tail = (3 * hw) // 128 * 128
    off = 3 * hw - tail
    extra = functools.reduce(jnp.add, [q_ref[s, :, tail : tail + 128].astype(F32) for s in range(4)]).T
    gv_ref[...] = extra[off : off + 8]
    gb_ref[...] = extra[off + 8 : off + 12]


def assemble_heads(q, hw):
    rows = q.shape[1]
    outs = (
        shape((rows, 12 * hw), F32),
        shape((rows, 4 * hw), F32),
        shape((8, rows), F32),
        shape((4, rows), F32),
    )
    return local_kernel(
        assemble_heads_body, outs, "assemble_heads", 0, 12 * rows * hw * 16, 0,
        in_specs=[vmem()],
        out_specs=(vmem(),) * 4,
    )(q)


def send(x, axis, to):
    n = lax.axis_size(axis)
    return lax.ppermute(x, axis, [(s, to(s)) for s in range(n)])


def seq_swap(x, k):
    return send(x, "seq", lambda s: s ^ k)


def add(*terms):
    out = terms[0].astype(F32)
    for t in terms[1:]:
        out = out + t.astype(F32)
    return out.astype(BF)


def after(values, *others):
    out = lax.optimization_barrier((values, others))
    return out[0]


def shards(inputs, segments, cotangent, w_qkv, w_out, w_up, w_down, vectors, bias_up):
    micros, _, tokens, width = inputs.shape
    nf = lax.axis_size("fsdp")
    assert lax.axis_size("seq") == 4 and inputs.shape[1] == 1
    rows = w_qkv.shape[0]
    part = w_down.shape[0] // 4
    hw = width // 4
    nz = nf // 2
    fast = nf == 8 and rows % 32 == 0 and part == rows
    at = lax.axis_index("seq")
    me = lax.axis_index("fsdp")
    z, y = me // 2, me % 2
    info = jnp.stack([at, y, z]).astype(jnp.int32)
    y_swap = lambda x: send(x, "fsdp", lambda s: s ^ 1)
    z_pull = lambda x, d: send(x, "fsdp", lambda s: (s - 2 * d) % nf)
    pulled = lambda x: [x] + [z_pull(x, d) for d in range(1, nz)]

    ranges = windows(segments[:, 0], tokens)

    own = inputs[:, 0]
    across = seq_swap(own, 2)
    beside = seq_swap(own, 1)

    if fast:
        qkv_piece, mlp_piece, out_copies = local_kernel(
            prep_body,
            (shape((rows, 3 * hw + 64)), shape((rows + part, width)), shape((nf, rows // 2, width))),
            "prep", 0, 6 * rows * 4 * width, 0,
            in_specs=[smem()] + [vmem()] * 6,
            out_specs=(vmem(),) * 3,
        )(info, w_qkv, w_out, w_up, w_down, vectors.T, bias_up.reshape(4, part))
        w_heads = lax.all_gather(qkv_piece, "fsdp", axis=0, tiled=True)
        out_half = lax.all_to_all(
            after(out_copies, w_heads), "fsdp", split_axis=0, concat_axis=0, tiled=True
        )
        gathered = lax.all_gather(mlp_piece, ("fsdp", "seq"), axis=0, tiled=False)
    else:
        gather = lambda a: lax.all_gather(a, "fsdp", axis=0, tiled=True)
        by_head = gather(w_qkv).reshape(width, 3, 4, hw)
        mine = lax.dynamic_index_in_dim(by_head, at, 2, keepdims=False).reshape(width, 3 * hw)
        biases = gather(bias_up).reshape(nf, 4, part).transpose(0, 2, 1).reshape(width, 4)
        w_heads = jnp.concatenate([mine, gather(vectors), biases, jnp.zeros((width, 52), BF)], axis=1)
        w_out_full = gather(w_out)
        ups = gather(w_up).reshape(width, nf, 4, part).transpose(2, 0, 1, 3).reshape(4, width, width)
        downs = gather(w_down).reshape(nf, 4, part, width).transpose(1, 0, 2, 3).reshape(4, width, width)
        one = lambda a, k: lax.dynamic_index_in_dim(a, at ^ k, 0, keepdims=False)
        chunks = [(one(ups, k), one(downs, k)) for k in range(4)]

    xs = (own, beside, across, seq_swap(after(across, w_heads), 1))

    over_seq = lambda a: lax.all_to_all(a, "seq", split_axis=0, concat_axis=0, tiled=True)
    q, k, v, c, lse, vt = forward(info, ranges, xs, segments, w_heads)
    kept = (q, k, v, lse)
    contexts = over_seq(c)
    if fast:
        out_half = after(out_half, vt)
        y_rows, n2, w_out_full = middle(info, contexts, own, vt, (out_half, seq_swap(out_half, 1)))
        gathered = after(gathered, n2)
        weights_a = weights_b = [gathered]
    else:
        y_rows, n2 = middle(info, contexts, own, vt, (w_out_full,))
        weights_a, weights_b = [*chunks[0], *chunks[1]], [*chunks[2], *chunks[3]]

    dz = cotangent.reshape(micros * tokens, width)
    za, dna, *near_g, bias_a = mlp(fast, info, 0, n2, dz, vt, weights_a, None)
    if fast:
        near_own, near_oth = (seq_swap(a, 1) for a in near_g[2:])
        near_s = add(near_g[1], near_oth)
        near_y = y_swap(near_s)
        za, dna = after((za, dna), near_s)
    zb, dnb, *far_g, bias_b = mlp(fast, info, 2, n2, dz, vt, weights_b, (za, dna))

    results, dy_a, da_a, d_a, sums_a = turn(info, 0, 1, micros, y_rows, zb, dnb, dz, w_out_full, vt, None)
    d_a = over_seq(d_a)
    if fast:
        zb, dnb = after((zb, dnb), near_y)
    results, dy_b, da_b, d_b, sums_b = turn(
        info, 1, micros - 1, micros, y_rows, zb, dnb, dz, w_out_full, vt, results
    )
    d_b = over_seq(d_b)
    if fast:
        far_own, far_oth = (seq_swap(after(a, da_b), 1) for a in far_g[2:])
        over_near = lambda parts: [parts[0]] + [z_pull(parts[d], d) for d in range(1, nz)]
        far_part = lambda n: add(far_g[0][:, n], far_own[:, n], far_y[n])
        near_z = over_near(split(info, [near_g[0], near_own, near_y]))
        contexts = after(contexts, near_z[0])
    out_grads = outproj_grad(fast, info, contexts, (da_a, da_b), nz, rows)
    carried = None
    pending, settled, totals = [], [], []

    def settle(m, own_part, across_part, got, later):
        if later is not None:
            got = after(got, later)
        total = add(across_part, got[tokens:])
        settled.append((m, own_part, got, seq_swap(total, 2)))
        return total

    gate = ()
    if fast:
        groups_z = [list(range(n, nf, 2)) for n in range(2)]
        over_z = lambda a: lax.all_to_all(
            a, "fsdp", split_axis=0, concat_axis=0, tiled=True, axis_index_groups=groups_z
        )
        keep, keep_other, to_core = out_grads
        out_c = seq_swap(to_core, 1)
        far_own, far_oth = after((far_own, far_oth), keep)
        far_s = [add(far_g[1][:, n], far_oth[:, n]) for n in range(2)]
        far_y = [y_swap(a) for a in far_s]
        gate = (keep, *far_s)
    for m in range(micros):
        if fast and m == 1:
            far_y[0], out_c, near_z = after((far_y[0], out_c, near_z), dn0)
            out_s = add(keep_other, out_c[1])
            out_y = y_swap(out_s)
            far_up = far_part(0)
            far_up_z = over_z(far_up)
            gate = (far_up, out_s)
        if fast and m == 2:
            out_y, far_y[1], far_up_z, near_z = after((out_y, far_y[1], far_up_z, near_z), dn0)
            rest = jnp.concatenate([far_part(1), add(keep, out_c[0], out_y)], axis=2)
            rest_z = over_z(rest)
            near_sum = add(*near_z).reshape(rows + part, width)
            near_x = seq_swap(near_sum, 2)
            gate = (rest, near_sum)
        d, d_at = (d_a, 0) if m == 0 else (d_b, m - 1)
        last = m == micros - 1
        packed = shape((nf, rows, 3 * hw + 64)) if fast else shape((width, 3 * hw + 64), F32)
        ends = (sums_a, sums_b, bias_a, bias_b, packed) if last else ()
        acc, sums, dn0, dn2, dn13 = backward(
            info, ranges, m, d, d_at, c, xs, kept, segments, after(w_heads, *gate), vt, carried, ends
        )
        carried = (acc, sums)
        pending.append((m, dn0, dn2, seq_swap(dn13, 1)))
        if m > 0:
            totals.append(settle(*pending.pop(0), dn0))
    if fast:
        acc = after(acc, rest_z, settled[0][3], near_x)
    last_total = settle(*pending.pop(0), None)
    if fast:
        far_sum = collect(far_up_z, rest_z)
        m, own_part, got, theirs = settled[0]
        settled[0] = (m, after(own_part, far_sum, last_total, *totals), got, theirs)
    grad_rows, rows_done = None, []
    for m, own_part, got, theirs in settled:
        dy, dy_at = (dy_a, 0) if m == 0 else (dy_b, m - 1)
        grad_rows = finish(m, own_part, got, theirs, dy, dy_at, own, vt, grad_rows)
        rows_done.append(grad_rows)

    if fast:
        qkv_z = lax.all_to_all(acc, "fsdp", split_axis=0, concat_axis=0, tiled=True)
        mine = add(near_sum, after(seq_swap(far_sum, 2), rows_done[0]))
        theirs = add(near_x, far_sum)
        g_up, g_down = assemble_mlp(info, [mine, seq_swap(mine, 1), theirs, seq_swap(theirs, 1)], rows)
        qkv_z = after(qkv_z, rows_done[-2])
        heads_share = share(qkv_z, rest_z, width // 2)
        g_qkv, g_out, g_vec, g_bias = assemble_heads(lax.all_gather(heads_share, "seq", axis=0, tiled=False), hw)
        g_vec, g_bias = g_vec.T, g_bias.reshape(4 * part)
    else:
        total = lambda a: lax.psum(
            lax.psum_scatter(a.astype(F32), "fsdp", scatter_dimension=0, tiled=True), "seq"
        )
        head_place = lambda a: lax.dynamic_update_slice_in_dim(
            jnp.zeros((width, 3, 4, hw), F32), a.reshape(width, 3, 1, hw), at, 2
        ).reshape(width, 12 * hw)
        g_qkv = total(head_place(acc[:, : 3 * hw]))
        g_out = total(out_grads[0])
        extra = total(acc[:, 3 * hw :])
        g_vec, g_bias = extra[:, :8], extra[:, 8:12].T.reshape(4 * part)
        pairs = jnp.stack([*near_g, *far_g])
        order = lambda n: jnp.stack(
            [lax.dynamic_index_in_dim(pairs[:, n], at ^ s, 0, keepdims=False) for s in range(4)]
        )
        ups = order(0).reshape(4, width, nf, part).transpose(1, 2, 0, 3).reshape(width, 4 * width)
        downs = order(1).reshape(4, nf, part, width).transpose(1, 0, 2, 3).reshape(4 * width, width)
        g_up, g_down = total(ups), total(downs)
    return (
        results[:, None],
        grad_rows[:, None],
        g_qkv,
        g_out,
        g_up,
        g_down,
        g_vec,
        g_bias,
    )


def solution(mesh):
    rows = P(None, "fsdp", "seq", None)
    first = P("fsdp", None)
    in_specs = (rows, P(None, "fsdp", None), rows, first, first, first, first, first, P("fsdp"))
    out_specs = (rows, rows, first, first, first, first, first, P("fsdp"))
    return jax.shard_map(shards, mesh=mesh, in_specs=in_specs, out_specs=out_specs, check_vma=False)
```
